32 devices in a mesh: dp: 8 (over z, x), blk: 4 (over y, core).
Axes of the slice: x: 2, y: 2, z: 4, core: 2. Of those that a mesh axis runs over, the one named last changes fastest.
Arguments:
- histories: bfloat16 [256, 128, 512], P(('dp', 'blk')), may hold values from -50 to 50
- lengths: int32 [256], P(('dp', 'blk')), may hold values from 1 to 128, as said below
- targets: int32 [256, 128], P(('dp', 'blk')), may hold values from 0 to 1023
- send_list: int32 [256], P(('dp', 'blk')), may hold values from 0 to 7, as said below
- w_in: bfloat16 [512, 2048], replicated, may hold values from -0.25 to 0.25
- w_out: bfloat16 [512, 512], replicated, may hold values from -0.25 to 0.25
- rel_bias: float32 [4, 128], replicated, may hold values from -4 to 4
- item_pool: bfloat16 [8192, 512], P(('dp', 'blk')), may hold values from -13 to 13
Outputs:
- row_loss: float32 [256, 128], P(('dp', 'blk'))
- pool_grad: float32 [8192, 512], P(('dp', 'blk'))
The draws below stay inside these ranges and needn't reach their ends.
Inputs may be any that keep to these rules, and one draw needn't show every extreme that they name: `lengths`: some history has exactly 128 events in every draw. `send_list`: on each device a permutation of its 8 users; entry d + k names the user sent to slot k of data group d.
All inputs are finite; a program needn't handle non-finite values.
Results may differ from the reference program's by a relative error of at most 0.0095.
Values may be sent and summed in bfloat16 or wider, within the bound.
No kernel may reach another device: no remote copies, remote signals or barrier semaphores. Data moves between devices by JAX's collectives and lax.ppermute only.
A program may use at most 64 MiB of HBM per device.

```python
import math
import jax
import jax.numpy as jnp
from jax import lax

D = 512
HEADS = 4
HDIM = 128
LMAX = 128
USER_SLOTS = 1
U_DEV = 8
USERS = 256
POOL = 1024
ITEMS = 8192
N_DP = 8
N_BLK = 4


def history_lengths(key):
    key = jax.random.fold_in(key, 11)
    first_key, second_key, third_key = jax.random.split(key, 3)
    device_count = USERS // U_DEV
    heavy = 2 ** jax.random.randint(first_key, (device_count, 1), 0, 4)
    ceiling = LMAX * heavy // 8
    raw_draw = jax.random.randint(second_key, (device_count, U_DEV), 0, LMAX)
    drawn = (raw_draw % ceiling + 1).reshape(USERS)
    longest = jax.random.randint(third_key, (), 0, USERS)
    drawn = jnp.where(jnp.arange(USERS) == longest, LMAX, drawn)
    return drawn.astype(jnp.int32)


def log_scales(key, shape):
    return jnp.exp(jax.random.uniform(key, shape, jnp.float32, 0.0, math.log(10.0)))


def draw_lengths(key, part):
    return history_lengths(key)


def draw_send_list(key, part):
    device_count = USERS // U_DEV
    group_count = U_DEV // USER_SLOTS
    blk_count = device_count // group_count
    user_len = history_lengths(key).reshape(device_count, U_DEV)
    local_index = jnp.arange(U_DEV)
    score = user_len * U_DEV + (U_DEV - 1 - local_index)[None, :]
    by_rank = jnp.argsort(-score, axis=1, stable=True).astype(jnp.int32)
    dp_index = jnp.arange(device_count) // blk_count
    dest_group = (local_index[None, :] + dp_index[:, None]) % group_count
    slot_index = dest_group * USER_SLOTS + local_index[None, :] // group_count
    rows_index = jnp.broadcast_to(jnp.arange(device_count)[:, None], (device_count, U_DEV))
    sending = jnp.zeros((device_count, U_DEV), jnp.int32).at[rows_index, slot_index].set(by_rank)
    return sending.reshape(USERS).astype(jnp.int32)


def draw_histories(key, part):
    key = jax.random.fold_in(key, 21)
    first_key, second_key, third_key = jax.random.split(key, 3)
    row_scale = log_scales(first_key, (USERS, LMAX, 1))
    col_scale = log_scales(second_key, (1, 1, D))
    base = jax.random.normal(third_key, (USERS, LMAX, D), jnp.float32)
    base = jnp.clip(base, -5.0, 5.0)
    return (base * row_scale * col_scale / 10.0).astype(jnp.bfloat16)


def draw_item_pool(key, part):
    key = jax.random.fold_in(key, 31)
    first_key, second_key, third_key = jax.random.split(key, 3)
    row_scale = log_scales(first_key, (ITEMS, 1))
    col_scale = log_scales(second_key, (1, D))
    base = jax.random.normal(third_key, (ITEMS, D), jnp.float32)
    base = jnp.clip(base, -5.0, 5.0)
    return (base * row_scale * col_scale / (5.0 * math.sqrt(D))).astype(jnp.bfloat16)


def place_ends(values, key, least, top_value):
    dims = values.shape
    spot = [jax.random.randint(jax.random.fold_in(key, axis), (), 0, dims[axis]) for axis in range(len(dims))]
    values = values.at[tuple(spot)].set(least)
    longest = dims.index(max(dims))
    spot[longest] = (spot[longest] + 1) % dims[longest]
    return values.at[tuple(spot)].set(top_value)


def scatter_about(key, extent, deviation, reach, kind=jnp.bfloat16):
    return jnp.clip(deviation * jax.random.normal(key, extent, jnp.float32), -reach, reach).astype(kind)


def setup_inputs(seed: int = 0) -> dict:
    key_of = jax.random.split(jax.random.key(seed), 9)
    histories = draw_histories(jax.random.fold_in(key_of[8], 71), 0)
    lengths = draw_lengths(jax.random.fold_in(key_of[8], 71), 0)
    targets = place_ends(jax.random.randint(key_of[2], (USERS, LMAX), 0, POOL), jax.random.fold_in(key_of[2], 1), 0, POOL - 1).astype(jnp.int32)
    send_list = draw_send_list(jax.random.fold_in(key_of[8], 71), 0)
    w_in = scatter_about(key_of[4], (D, 4 * D), D ** -0.5, 0.25)
    w_out = scatter_about(key_of[5], (D, D), D ** -0.5, 0.25)
    rel_bias = scatter_about(key_of[6], (HEADS, LMAX), 1.0, 4.0, jnp.float32)
    item_pool = draw_item_pool(jax.random.fold_in(key_of[8], 71), 0)
    return dict(histories=histories, lengths=lengths, targets=targets, send_list=send_list, w_in=w_in, w_out=w_out, rel_bias=rel_bias, item_pool=item_pool)


logit_scale = 20.0

def layer_norm(values, epsilon):
    center = values - lax.optimization_barrier(jnp.mean(values, axis=-1, keepdims=True))
    spread = lax.optimization_barrier(jnp.mean(center * center, axis=-1, keepdims=True))
    return center * lax.rsqrt(spread + epsilon)

def hstu_block(events, user_len, w_in, w_out, bias_full):
    batch_size = events.shape[0]
    flat_rows = events.reshape(batch_size * LMAX, D)
    normed = layer_norm(flat_rows.astype(jnp.float32), 1e-05).astype(jnp.bfloat16)
    projected = jax.nn.silu(jnp.dot(normed, w_in, preferred_element_type=jnp.float32)).astype(jnp.bfloat16)
    projected = projected.reshape(batch_size, LMAX, 4, HEADS, HDIM)
    gate_part = projected[:, :, 0]
    value_part = projected[:, :, 1]
    query_part = projected[:, :, 2]
    key_part = projected[:, :, 3]
    scores = jnp.einsum('bihe,bjhe->bhij', query_part.astype(jnp.float32), key_part.astype(jnp.float32))
    scores = scores / math.sqrt(HDIM) + bias_full[None]
    places = jnp.arange(LMAX)
    keep = (places[None, :] <= places[:, None])[None, None] & (places[None, None, None, :] < user_len[:, None, None, None])
    attn = jnp.where(keep, jax.nn.silu(scores), 0.0).astype(jnp.bfloat16)
    mixed = jnp.einsum('bhij,bjhe->bihe', attn.astype(jnp.float32), value_part.astype(jnp.float32))
    mixed = mixed.reshape(batch_size * LMAX, D)
    gated = (layer_norm(mixed, 1e-05) * gate_part.reshape(batch_size * LMAX, D).astype(jnp.float32)).astype(jnp.bfloat16)
    result = flat_rows.astype(jnp.float32) + jnp.dot(gated, w_out, preferred_element_type=jnp.float32)
    return result.astype(jnp.bfloat16).reshape(batch_size, LMAX, D)

def score_group(inputs):
    out_rows, target_ids, is_valid, pool_rows = inputs
    out_float = out_rows.astype(jnp.float32)
    queries = (out_float / jnp.sqrt(lax.optimization_barrier(jnp.sum(out_float * out_float, axis=-1, keepdims=True)) + 1e-06)).astype(jnp.bfloat16)
    pool_float = pool_rows.astype(jnp.float32)
    item_norm = jnp.sqrt(lax.optimization_barrier(jnp.sum(pool_float * pool_float, axis=-1, keepdims=True)) + 1e-06)
    unit_rows = pool_float / item_norm
    unit_bf = unit_rows.astype(jnp.bfloat16)
    logits = logit_scale * jnp.dot(queries, unit_bf.T, preferred_element_type=jnp.float32)
    total = lax.optimization_barrier(jnp.sum(jnp.exp(logits - logit_scale), axis=1))
    log_total = logit_scale + jnp.log(total)
    is_target = target_ids[:, None] == jnp.arange(POOL)[None, :]
    target_logit = lax.optimization_barrier(jnp.sum(jnp.where(is_target, logits, 0.0), axis=1))
    row_loss = jnp.where(is_valid, log_total - target_logit, 0.0)
    residual = (jnp.where(is_valid[:, None], jnp.exp(logits - log_total[:, None]), 0.0) - jnp.where(is_valid[:, None] & is_target, 1.0, 0.0)).astype(jnp.bfloat16)
    item_sum = logit_scale * jnp.dot(residual.T, queries, preferred_element_type=jnp.float32)
    pool_grad = (item_sum - unit_rows * lax.optimization_barrier(jnp.sum(unit_rows * item_sum, axis=-1, keepdims=True))) / item_norm
    return (row_loss, pool_grad)

def reference(histories, lengths, targets, send_list, w_in, w_out, rel_bias, item_pool):
    local_slots = send_list.reshape(N_DP, N_BLK, N_DP, USER_SLOTS).astype(jnp.int32)
    offsets = ((jnp.arange(N_DP)[:, None] * N_BLK + jnp.arange(N_BLK)[None, :]) * U_DEV).astype(jnp.int32)
    order = jnp.transpose(local_slots + offsets[:, :, None, None], (2, 1, 0, 3)).reshape(USERS)
    routed_hist = histories[order]
    routed_len = lengths[order]
    routed_tgt = targets[order]
    places = jnp.arange(LMAX)
    distance = jnp.clip(places[:, None] - places[None, :], 0, LMAX - 1)
    bias_full = rel_bias[:, distance]
    blocks = routed_hist.reshape(USERS // U_DEV, U_DEV, LMAX, D)
    block_len = routed_len.reshape(USERS // U_DEV, U_DEV)

    def run_block(inputs):
        return hstu_block(inputs[0], inputs[1], w_in, w_out, bias_full)
    layer_out = lax.map(run_block, (blocks, block_len))
    grouped_out = layer_out.reshape(N_DP, N_BLK * U_DEV * LMAX, D)
    is_valid = (places[None, :] < routed_len[:, None]).reshape(N_DP, N_BLK * U_DEV * LMAX)
    grouped_tgt = routed_tgt.reshape(N_DP, N_BLK * U_DEV * LMAX)
    grouped_pool = item_pool.reshape(N_DP, POOL, D)
    row_loss, pool_grad = lax.map(score_group, (grouped_out, grouped_tgt, is_valid, grouped_pool))
    return (row_loss.reshape(USERS, LMAX), pool_grad.reshape(ITEMS, D))
```

```python
import functools
import math

import jax
import jax.numpy as jnp
from jax import lax
from jax.experimental import pallas as pl
from jax.experimental.pallas import tpu as pltpu
from jax.sharding import PartitionSpec as P

logit_scale = 20.0
contract_last = (((1,), (1,)), ((), ()))


def swap(array, axis, bit):
    devices = lax.axis_size(axis)
    return lax.ppermute(array, axis, [(i, i ^ bit) for i in range(devices)])


def half_silu(half):
    return half + half * jnp.tanh(half)


def center_and_spread(values):
    center = values - jnp.mean(values, axis=-1, keepdims=True)
    return center, jnp.mean(center * center, axis=-1, keepdims=True)


def layer_rows(x, lens, w_in, w_out, bias_ref):
    length = bias_ref.shape[1]
    heads = bias_ref.shape[0]
    width = x.shape[1]
    hdim = width // heads
    center, spread = center_and_spread(x)
    half_normed = (center * (0.5 * lax.rsqrt(spread + 1e-05))).astype(jnp.bfloat16)
    parts = []
    for part in range(4):
        half = jnp.dot(
            half_normed, w_in[:, part * width : (part + 1) * width], preferred_element_type=jnp.float32
        )
        parts.append(half_silu(half).astype(jnp.bfloat16))
    gate, value, query, key = parts
    row = lax.broadcasted_iota(jnp.int32, (length, length), 0)
    col = lax.broadcasted_iota(jnp.int32, (length, length), 1)
    gated = []
    for u in range(len(lens)):
        rows = slice(u * length, (u + 1) * length)
        keep = (col <= row) & (col < lens[u])
        mixed = []
        for h in range(heads):
            cols = slice(h * hdim, (h + 1) * hdim)
            scores = lax.dot_general(
                query[rows, cols], key[rows, cols], contract_last, preferred_element_type=jnp.float32
            )
            attn = half_silu(scores * (0.5 / math.sqrt(hdim)) + bias_ref[h])
            attn = jnp.where(keep, attn, 0.0).astype(jnp.bfloat16)
            mixed.append(jnp.dot(attn, value[rows, cols], preferred_element_type=jnp.float32))
        center, spread = center_and_spread(jnp.concatenate(mixed, axis=1))
        normed = center * lax.rsqrt(spread + 1e-05)
        gated.append((normed * gate[rows].astype(jnp.float32)).astype(jnp.bfloat16))
    gated = jnp.concatenate(gated, axis=0)
    out = x + jnp.dot(gated, w_out[...], preferred_element_type=jnp.float32)
    out = out.astype(jnp.bfloat16).astype(jnp.float32)
    square = jnp.sum(out * out, axis=-1, keepdims=True)
    return (out * lax.rsqrt(square + 1e-06)).astype(jnp.bfloat16)


def users_kernel(
    per_step, blocks, scal_ref, x_ref, tgt_ref, w_in, w_out, rev_ref, unit_ref,
    loss_ref, own_ref, over_ref, side_ref, far_ref, acc_ref, bias_ref, exp_ref,
):
    step = pl.program_id(0)
    heads, length = rev_ref.shape
    width = x_ref.shape[-1]
    items = unit_ref.shape[0] // blocks

    @pl.when(step == 0)
    def _():
        acc_ref[...] = jnp.zeros_like(acc_ref)
        for h in range(heads):
            wide = jnp.broadcast_to(rev_ref[h : h + 1, :], (length, length))
            bias_ref[h] = 0.5 * pltpu.roll(wide, 0, 1, stride=1, stride_axis=0)

    lens = [scal_ref[blocks + step * per_step + u] for u in range(per_step)]
    x = x_ref[...].reshape(per_step * length, width).astype(jnp.float32)
    queries = layer_rows(x, lens, w_in, w_out, bias_ref)

    place = lax.broadcasted_iota(jnp.int32, (1, length), 1)
    valid = jnp.concatenate([place < lens[u] for u in range(per_step)], axis=1)
    target = jnp.concatenate(
        [tgt_ref[pl.ds(step * per_step + u, 1), :] for u in range(per_step)], axis=1
    )
    rows = per_step * length
    item_id = lax.broadcasted_iota(jnp.int32, (items, rows), 0)
    rate = logit_scale * math.log2(math.e)
    total = jnp.zeros((1, rows), jnp.float32)
    target_dot = jnp.zeros((1, rows), jnp.float32)
    for j in range(blocks):
        dots = lax.dot_general(
            unit_ref[j * items : (j + 1) * items], queries, contract_last, preferred_element_type=jnp.float32
        )
        exps = jnp.exp2(dots * rate - rate)
        exp_ref[j] = exps
        total += jnp.sum(exps, axis=0, keepdims=True)
        hit = item_id == target - j * items
        target_dot += jnp.sum(jnp.where(hit, dots, 0.0), axis=0, keepdims=True)
    log_total = logit_scale + jnp.log(total)
    loss = jnp.where(valid, log_total - logit_scale * target_dot, 0.0)
    for u in range(per_step):
        loss_ref[pl.ds(step * per_step + u, 1), :] = loss[:, u * length : (u + 1) * length]
    share = jnp.where(valid, 1.0 / total, 0.0)
    real_target = jnp.where(valid, target, -1)
    for j in range(blocks):
        hit = item_id == real_target - j * items
        residual = exp_ref[j] * share - jnp.where(hit, 1.0, 0.0)
        acc_ref[j] += jnp.dot(residual.astype(jnp.bfloat16), queries, preferred_element_type=jnp.float32)

    @pl.when(step == pl.num_programs(0) - 1)
    def _():
        own_ref[...] = acc_ref[scal_ref[0]]
        over_ref[...] = acc_ref[scal_ref[1]]
        side_ref[...] = acc_ref[scal_ref[2]].astype(jnp.bfloat16)
        far_ref[...] = acc_ref[scal_ref[3]].astype(jnp.bfloat16)


def users_call(events, lens, targets, w_in, w_out, reverse_bias, unit_all, block_ids):
    users, length, width = events.shape
    blocks = block_ids.shape[0]
    items = unit_all.shape[0] // blocks
    heads = reverse_bias.shape[0]
    per_step = 2 if users % 2 == 0 else 1
    whole = lambda *shape: pl.BlockSpec(shape, lambda s, scal: (0,) * len(shape))
    part = lambda dtype: jax.ShapeDtypeStruct((items, width), dtype)
    return pl.pallas_call(
        functools.partial(users_kernel, per_step, blocks),
        grid_spec=pltpu.PrefetchScalarGridSpec(
            num_scalar_prefetch=1,
            grid=(users // per_step,),
            in_specs=[
                pl.BlockSpec((per_step, length, width), lambda s, scal: (s, 0, 0)),
                whole(users, length),
                whole(*w_in.shape),
                whole(*w_out.shape),
                whole(*reverse_bias.shape),
                whole(*unit_all.shape),
            ],
            out_specs=[whole(users, length)] + [whole(items, width)] * 4,
            scratch_shapes=[
                pltpu.VMEM((blocks, items, width), jnp.float32),
                pltpu.VMEM((heads, length, length), jnp.float32),
                pltpu.VMEM((blocks, items, per_step * length), jnp.float32),
            ],
        ),
        out_shape=[
            jax.ShapeDtypeStruct((users, length), jnp.float32),
            part(jnp.float32),
            part(jnp.float32),
            part(jnp.bfloat16),
            part(jnp.bfloat16),
        ],
        compiler_params=pltpu.CompilerParams(vmem_limit_bytes=48 * 1024 * 1024),
        name="users",
    )(jnp.concatenate([block_ids, lens]), events, targets, w_in, w_out, reverse_bias, unit_all)


def shards(histories, lengths, targets, send_list, w_in, w_out, rel_bias, item_pool):
    user_count, length, feat_width = histories.shape
    pool_float = item_pool.astype(jnp.float32)
    item_norm = jnp.sqrt(jnp.sum(pool_float * pool_float, axis=-1, keepdims=True) + 1e-06)
    unit_rows = pool_float / item_norm
    unit_all = lax.all_gather(unit_rows.astype(jnp.bfloat16), "blk", axis=0, tiled=True)
    routed_hist = lax.all_to_all(histories[send_list], "dp", split_axis=0, concat_axis=0, tiled=True)
    groups = lax.axis_size("dp")
    numbers = jnp.concatenate([lengths[:, None], targets], axis=1)[send_list]
    numbers = lax.all_gather(numbers, "dp", axis=0, tiled=False)
    slots = user_count // groups
    numbers = lax.dynamic_slice_in_dim(numbers, lax.axis_index("dp") * slots, slots, axis=1)
    numbers = numbers.reshape(user_count, length + 1)
    routed_len, routed_tgt = numbers[:, 0], numbers[:, 1:]

    reverse_bias = jnp.roll(rel_bias[:, ::-1], 1, axis=1)
    mine = lax.axis_index("blk")
    block_ids = jnp.stack([mine, mine ^ 2, mine ^ 1, mine ^ 3]).astype(jnp.int32)
    row_loss, own, over, side, far = users_call(
        routed_hist, routed_len, routed_tgt, w_in, w_out, reverse_bias, unit_all, block_ids
    )
    over = over + swap(far, "blk", 1).astype(jnp.float32)
    own = own + swap(side, "blk", 1).astype(jnp.float32)
    item_sum = logit_scale * (own + swap(over.astype(jnp.bfloat16), "blk", 2).astype(jnp.float32))
    pool_grad = (
        item_sum - unit_rows * jnp.sum(unit_rows * item_sum, axis=-1, keepdims=True)
    ) / item_norm
    return (row_loss, pool_grad)


def solution(mesh):
    placed = (
        P(("dp", "blk"), None, None),
        P(("dp", "blk")),
        P(("dp", "blk"), None),
        P(("dp", "blk")),
        P(),
        P(),
        P(),
        P(("dp", "blk"), None),
    )
    return jax.shard_map(
        shards,
        mesh=mesh,
        in_specs=placed,
        out_specs=(P(("dp", "blk"), None), P(("dp", "blk"), None)),
        check_vma=False,
    )
```

```python
import functools
import math

import jax
import jax.numpy as jnp
from jax import lax
from jax.experimental import pallas as pl
from jax.experimental.pallas import tpu as pltpu
from jax.sharding import PartitionSpec as P

logit_scale = 20.0
contract_last = (((1,), (1,)), ((), ()))


def swap(array, axis, bit):
    devices = lax.axis_size(axis)
    return lax.ppermute(array, axis, [(i, i ^ bit) for i in range(devices)])


def from_behind(array, axis, by):
    devices = lax.axis_size(axis)
    return lax.ppermute(array, axis, [(i, (i + by) % devices) for i in range(devices)])


def half_silu(half):
    return half + half * jnp.tanh(half)


def center_and_spread(values):
    center = values - jnp.mean(values, axis=-1, keepdims=True)
    return center, jnp.mean(center * center, axis=-1, keepdims=True)


def layer_kernel(order, scal_ref, *refs):
    count = len(order)
    x_refs, (w_in, w_out, bias_in), q_refs = refs[:count], refs[count : count + 3], refs[count + 3 :]
    heads, length = bias_in.shape
    width = w_out.shape[0]
    hdim = width // heads
    users = scal_ref.shape[0] // 3
    lens = [scal_ref[2 * users + scal_ref[users + scal_ref[k]]] for k in order]

    x = jnp.concatenate([ref[0] for ref in x_refs], axis=0).astype(jnp.float32)
    center, spread = center_and_spread(x)
    half_normed = (center * (0.5 * lax.rsqrt(spread + 1e-05))).astype(jnp.bfloat16)
    parts = []
    for part in range(4):
        half = jnp.dot(
            half_normed, w_in[:, part * width : (part + 1) * width], preferred_element_type=jnp.float32
        )
        parts.append(half_silu(half).astype(jnp.bfloat16))
    gate, value, query, key = parts
    row = lax.broadcasted_iota(jnp.int32, (length, length), 0)
    col = lax.broadcasted_iota(jnp.int32, (length, length), 1)
    half_bias = []
    for h in range(heads):
        wide = jnp.broadcast_to(0.5 * bias_in[h : h + 1, :], (length, length))
        half_bias.append(pltpu.roll(wide, 0, 1, stride=1, stride_axis=0).T)
    gated = []
    for u in range(count):
        rows = slice(u * length, (u + 1) * length)
        keep = (col <= row) & (col < lens[u])
        mixed = []
        for h in range(heads):
            cols = slice(h * hdim, (h + 1) * hdim)
            scores = lax.dot_general(
                query[rows, cols], key[rows, cols], contract_last, preferred_element_type=jnp.float32
            )
            attn = half_silu(scores * (0.5 / math.sqrt(hdim)) + half_bias[h])
            attn = jnp.where(keep, attn, 0.0).astype(jnp.bfloat16)
            mixed.append(jnp.dot(attn, value[rows, cols], preferred_element_type=jnp.float32))
        center, spread = center_and_spread(jnp.concatenate(mixed, axis=1))
        normed = center * lax.rsqrt(spread + 1e-05)
        gated.append((normed * gate[rows].astype(jnp.float32)).astype(jnp.bfloat16))
    gated = jnp.concatenate(gated, axis=0)
    out = x + jnp.dot(gated, w_out[...], preferred_element_type=jnp.float32)
    out = out.astype(jnp.bfloat16).astype(jnp.float32)
    square = jnp.sum(out * out, axis=-1, keepdims=True)
    queries = (out * lax.rsqrt(square + 1e-06)).astype(jnp.bfloat16)
    for u in range(count):
        q_refs[u][...] = queries[u * length : (u + 1) * length]


def layer_call(scalars, order, histories, w_in, w_out, rel_bias):
    users, length, width = histories.shape
    fixed = lambda array: pl.BlockSpec(array.shape, lambda s, scal: (0,) * array.ndim)

    def event_spec(k):
        return pl.BlockSpec((1, length, width), lambda s, scal: (scal[users + scal[k]], 0, 0))

    return pl.pallas_call(
        functools.partial(layer_kernel, order),
        grid_spec=pltpu.PrefetchScalarGridSpec(
            num_scalar_prefetch=1,
            grid=(1,),
            in_specs=[event_spec(k) for k in order] + [fixed(w_in), fixed(w_out), fixed(rel_bias)],
            out_specs=[pl.BlockSpec((length, width), lambda s, scal: (0, 0)) for _ in order],
        ),
        out_shape=[jax.ShapeDtypeStruct((length, width), jnp.bfloat16) for _ in order],
        compiler_params=pltpu.CompilerParams(vmem_limit_bytes=24 * 1024 * 1024),
        name="layer",
    )(scalars, *([histories] * len(order)), w_in, w_out, rel_bias)


def loss_kernel(places, blocks, first, last, scal_ref, *refs):
    count = len(places)
    q_refs, (num_ref, unit_ref) = refs[:count], refs[count : count + 2]
    refs = refs[count + 2 :]
    if not first:
        (acc_in, loss_in), refs = refs[:2], refs[2:]
    loss_ref, sum_refs, exp_ref = refs[0], refs[1:-1], refs[-1]
    length, width = q_refs[0].shape
    items = unit_ref.shape[0] // blocks
    rows = count * length

    queries = jnp.concatenate([ref[...] for ref in q_refs], axis=0)
    spots = [scal_ref[blocks + k] for k in places]
    numbers = [num_ref[spot] for spot in spots]
    target = jnp.concatenate([number[1:2, :] for number in numbers], axis=1)
    place = lax.broadcasted_iota(jnp.int32, (1, length), 1)
    valid = jnp.concatenate([place < number[0:1, :] for number in numbers], axis=1)
    item_id = lax.broadcasted_iota(jnp.int32, (items, rows), 0)
    rate = logit_scale * math.log2(math.e)
    total = jnp.zeros((1, rows), jnp.float32)
    target_dot = jnp.zeros((1, rows), jnp.float32)
    for j in range(blocks):
        dots = lax.dot_general(
            unit_ref[j * items : (j + 1) * items], queries, contract_last, preferred_element_type=jnp.float32
        )
        exps = jnp.exp2(dots * rate - rate)
        exp_ref[j] = exps
        total += jnp.sum(exps, axis=0, keepdims=True)
        hit = item_id == target - j * items
        target_dot += jnp.sum(jnp.where(hit, dots, 0.0), axis=0, keepdims=True)
    log_total = logit_scale + jnp.log(total)
    loss = jnp.where(valid, log_total - logit_scale * target_dot, 0.0)
    if first:
        loss_ref[...] = jnp.zeros_like(loss_ref)
    else:
        loss_ref[...] = loss_in[...]
    for u in range(count):
        loss_ref[pl.ds(spots[u], 1), :] = loss[:, u * length : (u + 1) * length]
    share = jnp.where(valid, 1.0 / total, 0.0)
    real_target = jnp.where(valid, target, -1)

    def block_sum(j):
        hit = item_id == real_target - j * items
        residual = exp_ref[j] * share - jnp.where(hit, 1.0, 0.0)
        part = jnp.dot(residual.astype(jnp.bfloat16), queries, preferred_element_type=jnp.float32)
        return part if first else part + acc_in[j]

    for k in range(blocks):
        if last:
            sum_refs[k][...] = block_sum(scal_ref[k]).astype(sum_refs[k].dtype)
        else:
            sum_refs[0][k] = block_sum(k)


def loss_call(scalars, places, queries, numbers, unit_all, blocks, carried, last):
    users, _, length = numbers.shape
    width = unit_all.shape[1]
    items = unit_all.shape[0] // blocks
    fixed = lambda array: pl.BlockSpec(array.shape, lambda s, scal: (0,) * array.ndim)
    if last:
        sums = [
            jax.ShapeDtypeStruct((items, width), jnp.float32 if k < blocks // 2 else jnp.bfloat16)
            for k in range(blocks)
        ]
    else:
        sums = [jax.ShapeDtypeStruct((blocks, items, width), jnp.float32)]
    outs = [jax.ShapeDtypeStruct((users, length), jnp.float32)] + sums
    arrays = [*queries, numbers, unit_all, *carried]
    return pl.pallas_call(
        functools.partial(loss_kernel, places, blocks, not carried, last),
        grid_spec=pltpu.PrefetchScalarGridSpec(
            num_scalar_prefetch=1,
            grid=(1,),
            in_specs=[fixed(array) for array in arrays],
            out_specs=[fixed(out) for out in outs],
            scratch_shapes=[pltpu.VMEM((blocks, items, len(places) * length), jnp.float32)],
        ),
        out_shape=outs,
        compiler_params=pltpu.CompilerParams(vmem_limit_bytes=24 * 1024 * 1024),
        name="loss",
    )(scalars, *arrays)


def shards(histories, lengths, targets, send_list, w_in, w_out, rel_bias, item_pool):
    user_count, length, feat_width = histories.shape
    groups, blocks = lax.axis_size("dp"), lax.axis_size("blk")
    slots = user_count // groups
    group, mine = lax.axis_index("dp"), lax.axis_index("blk")

    work = sorted(
        ((shift, slot) for shift in range(groups) for slot in range(slots)),
        key=lambda pair: (pair[0] == 0, abs(pair[0] - groups / 2)),
    )
    shifts = jnp.array([pair[0] for pair in work], jnp.int32)
    slot_of = jnp.array([pair[1] for pair in work], jnp.int32)
    sent = ((group + shifts) % groups) * slots + slot_of
    scalars = jnp.concatenate([sent, send_list, lengths])

    pool_float = item_pool.astype(jnp.float32)
    item_norm = jnp.sqrt(jnp.sum(pool_float * pool_float, axis=-1, keepdims=True) + 1e-06)
    unit_rows = pool_float / item_norm
    unit_all = lax.all_gather(unit_rows.astype(jnp.bfloat16), "blk", axis=0, tiled=True)

    pair = 2 if user_count % 2 == 0 else 1
    arrived = [None] * user_count
    for at in range(0, user_count, pair):
        order = tuple(range(at, at + pair))
        for k, queries in zip(order, layer_call(scalars, order, histories, w_in, w_out, rel_bias)):
            arrived[k] = queries if work[k][0] == 0 else from_behind(queries, "dp", work[k][0])

    numbers = jnp.stack([jnp.broadcast_to(lengths[:, None], targets.shape), targets], axis=1)[send_list]
    numbers = lax.all_to_all(numbers, "dp", split_axis=0, concat_axis=0, tiled=True)

    came = ((group - shifts) % groups) * slots + slot_of
    block_ids = jnp.stack([mine, mine ^ 2, mine ^ 1, mine ^ 3]).astype(jnp.int32)
    scalars = jnp.concatenate([block_ids, came])
    turns = [user_count - 1, *range(user_count - 1)]
    carried = ()
    for at in range(0, user_count, pair):
        places = tuple(turns[at : at + pair])
        last = at + pair >= user_count
        outs = loss_call(
            scalars, places, [arrived[k] for k in places], numbers, unit_all, blocks, carried, last
        )
        carried = (outs[1], outs[0])
    row_loss, own, over, side, far = outs
    over = over + swap(far, "blk", 1).astype(jnp.float32)
    own = own + swap(side, "blk", 1).astype(jnp.float32)
    item_sum = logit_scale * (own + swap(over.astype(jnp.bfloat16), "blk", 2).astype(jnp.float32))
    pool_grad = (
        item_sum - unit_rows * jnp.sum(unit_rows * item_sum, axis=-1, keepdims=True)
    ) / item_norm
    return (row_loss, pool_grad)


def solution(mesh):
    placed = (
        P(("dp", "blk"), None, None),
        P(("dp", "blk")),
        P(("dp", "blk"), None),
        P(("dp", "blk")),
        P(),
        P(),
        P(),
        P(("dp", "blk"), None),
    )
    return jax.shard_map(
        shards,
        mesh=mesh,
        in_specs=placed,
        out_specs=(P(("dp", "blk"), None), P(("dp", "blk"), None)),
        check_vma=False,
    )
```

```python
import functools
import math

import jax
import jax.numpy as jnp
from jax import lax
from jax.experimental import pallas as pl
from jax.experimental.pallas import tpu as pltpu
from jax.sharding import PartitionSpec as P

logit_scale = 20.0
contract_last = (((1,), (1,)), ((), ()))
tile = 256
chunk = 16


def swap(array, axis, bit):
    devices = lax.axis_size(axis)
    return lax.ppermute(array, axis, [(i, i ^ bit) for i in range(devices)])


def half_silu(half):
    return half + half * jnp.tanh(half)


def center_and_spread(values):
    center = values - jnp.mean(values, axis=-1, keepdims=True)
    return center, jnp.mean(center * center, axis=-1, keepdims=True)


def pick_kernel(list_ref, from_ref, to_ref, sems):
    copies = [
        pltpu.make_async_copy(from_ref.at[list_ref[k]], to_ref.at[k], sems.at[k])
        for k in range(to_ref.shape[0])
    ]
    for copy in copies:
        copy.start()
    for copy in copies:
        copy.wait()


def pick(array, entries):
    return pl.pallas_call(
        pick_kernel,
        grid_spec=pltpu.PrefetchScalarGridSpec(
            num_scalar_prefetch=1,
            grid=(1,),
            in_specs=[pl.BlockSpec(memory_space=pltpu.HBM)],
            out_specs=pl.BlockSpec(memory_space=pl.ANY),
            scratch_shapes=[pltpu.SemaphoreType.DMA(entries.shape)],
        ),
        out_shape=jax.ShapeDtypeStruct(entries.shape + array.shape[1:], array.dtype),
        name="pick",
    )(entries, array)


def users_kernel(
    per_step, blocks, scal_ref, x_ref, tgt_ref, w_in, w_out, bias_in, unit_ref,
    loss_ref, own_ref, over_ref, side_ref, far_ref,
    acc, bias, exp_ref, events, gate, value, query, key, mixed, packed_tgt, packed_loss,
):
    step = pl.program_id(0)
    heads, length = bias_in.shape
    width = x_ref.shape[-1]
    hdim = width // heads
    half = length // 2
    items = unit_ref.shape[0] // blocks

    @pl.when(step == 0)
    def _():
        acc[...] = jnp.zeros_like(acc)
        for h in range(heads):
            wide = jnp.broadcast_to(0.5 * bias_in[h : h + 1, :], (length, length))
            bias[h] = pltpu.roll(wide, 0, 1, stride=1, stride_axis=0).T

    lens = [scal_ref[blocks + step * per_step + u] for u in range(per_step)]
    starts, end = [], 0
    for u in range(per_step):
        starts.append(pl.multiple_of(end, chunk) if u else 0)
        end = end + (lens[u] + chunk - 1) // chunk * chunk
    end = pl.multiple_of(end, chunk)
    tiles = (end + tile - 1) // tile
    covered = pl.multiple_of(tiles * tile, tile)

    place = lax.broadcasted_iota(jnp.int32, (1, length), 1)
    packed_tgt[...] = jnp.full_like(packed_tgt, -1)
    for u in range(per_step):
        events[pl.ds(starts[u], length), :] = x_ref[u]
        wanted = jnp.where(place < lens[u], tgt_ref[pl.ds(step * per_step + u, 1), :], -1)
        line, turn = starts[u] // length, lax.rem(starts[u], length)
        turned = pltpu.roll(wanted, turn, 1)
        packed_tgt[pl.ds(line, 1), :] = jnp.where(place >= turn, turned, packed_tgt[pl.ds(line, 1), :])
        packed_tgt[pl.ds(line + 1, 1), :] = jnp.where(
            place < turn, turned, packed_tgt[pl.ds(line + 1, 1), :]
        )
    events[pl.ds(end, tile), :] = jnp.zeros((tile, width), events.dtype)
    last_tile = pl.multiple_of(covered - tile, tile)
    mixed[pl.ds(last_tile, tile), :] = jnp.zeros((tile, width), mixed.dtype)
    for part in (value, query, key):
        part[pl.ds(covered, length), :] = jnp.zeros((length, width), part.dtype)

    def project(t, _):
        rows = pl.ds(pl.multiple_of(t * tile, tile), tile)
        center, spread = center_and_spread(events[rows, :].astype(jnp.float32))
        half_normed = (center * (0.5 * lax.rsqrt(spread + 1e-05))).astype(jnp.bfloat16)
        for index, part in enumerate((gate, value, query, key)):
            halves = jnp.dot(
                half_normed, w_in[:, index * width : (index + 1) * width], preferred_element_type=jnp.float32
            )
            part[rows, :] = half_silu(halves).astype(jnp.bfloat16)
        return 0

    lax.fori_loop(0, tiles, project, 0)

    def attend(u, first, count, seen):
        rows, sources = pl.ds(starts[u] + first, count), pl.ds(starts[u], seen)
        row = first + lax.broadcasted_iota(jnp.int32, (count, seen), 0)
        col = lax.broadcasted_iota(jnp.int32, (count, seen), 1)
        keep = (col <= row) & (col < lens[u])
        for h in range(heads):
            cols = slice(h * hdim, (h + 1) * hdim)
            scores = lax.dot_general(
                query[rows, cols], key[sources, cols], contract_last, preferred_element_type=jnp.float32
            )
            attn = half_silu(
                scores * (0.5 / math.sqrt(hdim)) + bias[h, first : first + count, :seen]
            )
            attn = jnp.where(keep, attn, 0.0).astype(jnp.bfloat16)
            mixed[rows, cols] = jnp.dot(attn, value[sources, cols], preferred_element_type=jnp.float32)

    for u in range(per_step):
        pl.when(lens[u] > half)(functools.partial(attend, u, half, length - half, length))
    for u in range(per_step):
        attend(u, 0, half, half)

    item_id = lax.broadcasted_iota(jnp.int32, (items, tile), 0)
    rate = logit_scale * math.log2(math.e)
    lines = tile // length

    def score(t, _):
        rows = pl.ds(pl.multiple_of(t * tile, tile), tile)
        center, spread = center_and_spread(mixed[rows, :])
        normed = center * lax.rsqrt(spread + 1e-05)
        gated = (normed * gate[rows, :].astype(jnp.float32)).astype(jnp.bfloat16)
        out = events[rows, :].astype(jnp.float32) + jnp.dot(
            gated, w_out[...], preferred_element_type=jnp.float32
        )
        out = out.astype(jnp.bfloat16).astype(jnp.float32)
        square = jnp.sum(out * out, axis=-1, keepdims=True)
        queries = (out * lax.rsqrt(square + 1e-06)).astype(jnp.bfloat16)

        target = jnp.concatenate([packed_tgt[pl.ds(t * lines + k, 1), :] for k in range(lines)], axis=1)
        total = jnp.zeros((1, tile), jnp.float32)
        target_dot = jnp.zeros((1, tile), jnp.float32)
        for j in range(blocks):
            dots = lax.dot_general(
                unit_ref[j * items : (j + 1) * items], queries, contract_last,
                preferred_element_type=jnp.float32,
            )
            exps = jnp.exp2(dots * rate - rate)
            exp_ref[j] = exps
            total += jnp.sum(exps, axis=0, keepdims=True)
            hit = item_id == target - j * items
            target_dot += jnp.sum(jnp.where(hit, dots, 0.0), axis=0, keepdims=True)
        loss = logit_scale + jnp.log(total) - logit_scale * target_dot
        for k in range(lines):
            packed_loss[pl.ds(t * lines + k, 1), :] = loss[:, k * length : (k + 1) * length]
        share = jnp.where(target >= 0, 1.0 / total, 0.0)
        for j in range(blocks):
            hit = item_id == target - j * items
            residual = exp_ref[j] * share - jnp.where(hit, 1.0, 0.0)
            acc[j] += jnp.dot(residual.astype(jnp.bfloat16), queries, preferred_element_type=jnp.float32)
        return 0

    lax.fori_loop(0, tiles, score, 0)

    for u in range(per_step):
        line, turn = starts[u] // length, lax.rem(starts[u], length)
        back = lax.rem(length - turn, length)
        near = pltpu.roll(packed_loss[pl.ds(line, 1), :], back, 1)
        rest = pltpu.roll(packed_loss[pl.ds(line + 1, 1), :], back, 1)
        loss = jnp.where(place < length - turn, near, rest)
        loss_ref[pl.ds(step * per_step + u, 1), :] = jnp.where(place < lens[u], loss, 0.0)

    @pl.when(step == pl.num_programs(0) - 1)
    def _():
        own_ref[...] = acc[scal_ref[0]]
        over_ref[...] = acc[scal_ref[1]]
        side_ref[...] = acc[scal_ref[2]].astype(jnp.bfloat16)
        far_ref[...] = acc[scal_ref[3]].astype(jnp.bfloat16)


def users_call(events, lens, targets, w_in, w_out, rel_bias, unit_all, block_ids):
    users, length, width = events.shape
    blocks = block_ids.shape[0]
    items = unit_all.shape[0] // blocks
    heads = rel_bias.shape[0]
    per_step = math.gcd(users, 8)
    rows = per_step * length
    lines = -(-(rows // length + 1) // 8) * 8
    whole = lambda *shape: pl.BlockSpec(shape, lambda s, scal: (0,) * len(shape))
    part = lambda dtype: jax.ShapeDtypeStruct((items, width), dtype)
    return pl.pallas_call(
        functools.partial(users_kernel, per_step, blocks),
        grid_spec=pltpu.PrefetchScalarGridSpec(
            num_scalar_prefetch=1,
            grid=(users // per_step,),
            in_specs=[
                pl.BlockSpec((per_step, length, width), lambda s, scal: (s, 0, 0)),
                whole(users, length),
                whole(*w_in.shape),
                whole(*w_out.shape),
                whole(*rel_bias.shape),
                whole(*unit_all.shape),
            ],
            out_specs=[whole(users, length)] + [whole(items, width)] * 4,
            scratch_shapes=[
                pltpu.VMEM((blocks, items, width), jnp.float32),
                pltpu.VMEM((heads, length, length), jnp.float32),
                pltpu.VMEM((blocks, items, tile), jnp.float32),
                pltpu.VMEM((rows + tile, width), jnp.bfloat16),
            ]
            + [pltpu.VMEM((rows + tile, width), jnp.bfloat16)] * 4
            + [
                pltpu.VMEM((rows + tile, width), jnp.float32),
                pltpu.VMEM((lines, length), jnp.int32),
                pltpu.VMEM((lines, length), jnp.float32),
            ],
        ),
        out_shape=[
            jax.ShapeDtypeStruct((users, length), jnp.float32),
            part(jnp.float32),
            part(jnp.float32),
            part(jnp.bfloat16),
            part(jnp.bfloat16),
        ],
        compiler_params=pltpu.CompilerParams(vmem_limit_bytes=44 * 1024 * 1024),
        name="users",
    )(jnp.concatenate([block_ids, lens]), events, targets, w_in, w_out, rel_bias, unit_all)


def gather_all(array, axis):
    devices, index = lax.axis_size(axis), lax.axis_index(axis)
    array, bit = array[None], 1
    while bit < devices:
        other = swap(array, axis, bit)
        upper = (index & bit) != 0
        array = jnp.concatenate([jnp.where(upper, other, array), jnp.where(upper, array, other)], axis=0)
        bit *= 2
    return array


def shards(histories, lengths, targets, send_list, w_in, w_out, rel_bias, item_pool):
    user_count, length, feat_width = histories.shape
    groups = lax.axis_size("dp")
    slots = user_count // groups
    picked = pick(histories, send_list)
    numbers = jnp.stack([jnp.broadcast_to(lengths[:, None], targets.shape), targets], axis=1)
    picked, numbers = lax.optimization_barrier((picked, numbers))
    routed_hist = lax.all_to_all(picked, "dp", split_axis=0, concat_axis=0, tiled=True)

    pool_float = item_pool.astype(jnp.float32)
    item_norm = jnp.sqrt(jnp.sum(pool_float * pool_float, axis=-1, keepdims=True) + 1e-06)
    unit_rows = pool_float / item_norm
    unit_all = lax.all_gather(unit_rows.astype(jnp.bfloat16), "blk", axis=0, tiled=True)

    numbers = gather_all(numbers[send_list], "dp")
    numbers = lax.dynamic_slice_in_dim(numbers, lax.axis_index("dp") * slots, slots, axis=1)
    numbers = numbers.reshape(user_count, 2, length)

    mine = lax.axis_index("blk")
    block_ids = jnp.stack([mine, mine ^ 2, mine ^ 1, mine ^ 3]).astype(jnp.int32)
    row_loss, own, over, side, far = users_call(
        routed_hist, numbers[:, 0, 0], numbers[:, 1], w_in, w_out, rel_bias, unit_all, block_ids
    )
    over = over + swap(far, "blk", 1).astype(jnp.float32)
    own = own + swap(side, "blk", 1).astype(jnp.float32)
    item_sum = logit_scale * (own + swap(over.astype(jnp.bfloat16), "blk", 2).astype(jnp.float32))
    pool_grad = (
        item_sum - unit_rows * jnp.sum(unit_rows * item_sum, axis=-1, keepdims=True)
    ) / item_norm
    return (row_loss, pool_grad)


def solution(mesh):
    placed = (
        P(("dp", "blk"), None, None),
        P(("dp", "blk")),
        P(("dp", "blk"), None),
        P(("dp", "blk")),
        P(),
        P(),
        P(),
        P(("dp", "blk"), None),
    )
    return jax.shard_map(
        shards,
        mesh=mesh,
        in_specs=placed,
        out_specs=(P(("dp", "blk"), None), P(("dp", "blk"), None)),
        check_vma=False,
    )
```

```python
import functools
import math

import jax
import jax.numpy as jnp
from jax import lax
from jax.experimental import pallas as pl
from jax.experimental.pallas import tpu as pltpu
from jax.sharding import PartitionSpec as P

logit_scale = 20.0
contract_last = (((1,), (1,)), ((), ()))
tile = 256
chunk = 16
number_rows = 8


def swap(array, axis, bit):
    devices = lax.axis_size(axis)
    return lax.ppermute(array, axis, [(i, i ^ bit) for i in range(devices)])


def half_silu(half):
    return half + half * jnp.tanh(half)


def center_and_spread(values):
    center = values - jnp.mean(values, axis=-1, keepdims=True)
    return center, jnp.mean(center * center, axis=-1, keepdims=True)


def pack_kernel(list_ref, len_ref, from_ref, tgt_ref, to_ref, buffer, in_sems, out_sems):
    users, _, width = to_ref.shape
    length = from_ref.shape[1]
    copies_in = [
        pltpu.make_async_copy(from_ref.at[list_ref[k]], buffer.at[k, pl.ds(0, length)], in_sems.at[k])
        for k in range(users)
    ]
    copies_out = [pltpu.make_async_copy(buffer.at[k], to_ref.at[k], out_sems.at[k]) for k in range(users)]
    for copy in copies_in:
        copy.start()
    shape = (number_rows, length)
    for k in range(users):
        target = tgt_ref[pl.ds(list_ref[k], 1), :]
        digits = [jnp.full((1, length), len_ref[list_ref[k]], jnp.int32), target // 256, target % 256]
        lanes = [jnp.broadcast_to(digit.astype(jnp.float32), shape) for digit in digits]
        lanes += [jnp.zeros(shape, jnp.float32)] * (width // length - 3)
        buffer[k, length:, :] = jnp.concatenate(lanes, axis=1).astype(jnp.bfloat16)
    for k in range(users):
        copies_in[k].wait()
        copies_out[k].start()
    for copy in copies_out:
        copy.wait()


def pack(histories, lengths, targets, entries):
    users, length, width = histories.shape
    shape = (users, length + number_rows, width)
    return pl.pallas_call(
        pack_kernel,
        grid_spec=pltpu.PrefetchScalarGridSpec(
            num_scalar_prefetch=2,
            grid=(1,),
            in_specs=[
                pl.BlockSpec(memory_space=pl.ANY),
                pl.BlockSpec(targets.shape, lambda s, entries, lens: (0, 0)),
            ],
            out_specs=pl.BlockSpec(memory_space=pl.ANY),
            scratch_shapes=[
                pltpu.VMEM(shape, jnp.bfloat16),
                pltpu.SemaphoreType.DMA((users,)),
                pltpu.SemaphoreType.DMA((users,)),
            ],
        ),
        out_shape=jax.ShapeDtypeStruct(shape, jnp.bfloat16),
        compiler_params=pltpu.CompilerParams(vmem_limit_bytes=16 * 1024 * 1024),
        name="pack",
    )(entries, lengths, histories, targets)


def users_kernel(
    blocks, len_ref, block_ref, x_any, w_in_any, w_out_any, bias_in, unit_any,
    loss_ref, own_ref, over_ref, side_ref, far_ref,
    acc, bias, x_ref, w_in, w_out, unit_ref, exp_ref, residual, events, starts_ref, key, value,
    packed_tgt, packed_loss, x_sems, w_sems,
):
    step = pl.program_id(0)
    heads, length = bias_in.shape
    per_step, _, width = x_ref.shape
    hdim = width // heads
    items = unit_ref.shape[0] // blocks
    lines = tile // length

    x_copies = [
        pltpu.make_async_copy(x_any.at[step * per_step + u], x_ref.at[u], x_sems.at[u])
        for u in range(per_step)
    ]
    w_copies = [
        pltpu.make_async_copy(w_in_any, w_in, w_sems.at[0]),
        pltpu.make_async_copy(w_out_any, w_out, w_sems.at[1]),
        pltpu.make_async_copy(unit_any, unit_ref, w_sems.at[2]),
    ]
    for copy in x_copies:
        copy.start()

    @pl.when(step == 0)
    def _():
        for copy in w_copies:
            copy.start()
        acc[...] = jnp.zeros_like(acc)
        for h in range(heads):
            wide = jnp.broadcast_to(0.5 * bias_in[h : h + 1, :], (length, length))
            turned = pltpu.roll(wide, 0, 1, stride=1, stride_axis=0).T
            bias[h] = jnp.concatenate([turned, turned], axis=1)

    lens = [len_ref[step * per_step + u] for u in range(per_step)]
    starts, end = [], 0
    for u in range(per_step):
        starts.append(pl.multiple_of(end, chunk) if u else 0)
        end = end + (lens[u] + chunk - 1) // chunk * chunk
    end = pl.multiple_of(end, chunk)
    tiles = (end + tile - 1) // tile

    place = lax.broadcasted_iota(jnp.int32, (1, length), 1)
    packed_tgt[...] = jnp.full_like(packed_tgt, -1)
    key[:length, :] = jnp.zeros((length, width), key.dtype)
    value[:length, :] = jnp.zeros((length, width), value.dtype)
    for u in range(per_step):
        starts_ref[pl.ds(starts[u], length), :] = jnp.full((length, length), starts[u], jnp.int32)
    for copy in x_copies:
        copy.wait()
    for u in range(per_step):
        events[pl.ds(starts[u], length), :] = x_ref[u, :length, :]
        digits = x_ref[u, length:, :].astype(jnp.float32)
        target = digits[:1, length : 2 * length] * 256.0 + digits[:1, 2 * length : 3 * length]
        wanted = jnp.where(place < lens[u], target.astype(jnp.int32), -1)
        line, turn = starts[u] // length + 1, lax.rem(starts[u], length)
        turned = pltpu.roll(wanted, turn, 1)
        packed_tgt[pl.ds(line, 1), :] = jnp.where(place >= turn, turned, packed_tgt[pl.ds(line, 1), :])
        packed_tgt[pl.ds(line + 1, 1), :] = jnp.where(
            place < turn, turned, packed_tgt[pl.ds(line + 1, 1), :]
        )
    events[pl.ds(end, tile), :] = jnp.zeros((tile, width), events.dtype)

    @pl.when(step == 0)
    def _():
        for copy in w_copies:
            copy.wait()

    row = lax.broadcasted_iota(jnp.int32, (length, length), 0)
    col = lax.broadcasted_iota(jnp.int32, (length, length), 1)
    item_id = lax.broadcasted_iota(jnp.int32, (items, tile), 0)
    rate = logit_scale * math.log2(math.e)

    def one_tile(t, _):
        first = pl.multiple_of(t * tile, tile)
        x = events[pl.ds(first, tile), :].astype(jnp.float32)
        center, spread = center_and_spread(x)
        half_normed = (center * (0.5 * lax.rsqrt(spread + 1e-05))).astype(jnp.bfloat16)
        gate, values, query, keys = [
            half_silu(
                jnp.dot(
                    half_normed, w_in[:, part * width : (part + 1) * width],
                    preferred_element_type=jnp.float32,
                )
            ).astype(jnp.bfloat16)
            for part in range(4)
        ]
        key[pl.ds(first + length, tile), :] = keys
        value[pl.ds(first + length, tile), :] = values
        mixed = []
        for k in range(lines):
            base = pl.multiple_of(first + k * length, length)
            sources = pl.ds(base, 2 * length)
            start = starts_ref[pl.ds(base, length), :]
            ahead = packed_tgt[pl.ds(t * lines + k, 1), :] >= 0
            here = packed_tgt[pl.ds(t * lines + k + 1, 1), :] >= 0
            keep_ahead = (base - length + col >= start) & ahead
            keep_here = (col <= row) & (base + col >= start) & here
            keep = jnp.concatenate([keep_ahead, keep_here], axis=1)
            by_head = []
            for h in range(heads):
                cols = slice(h * hdim, (h + 1) * hdim)
                scores = lax.dot_general(
                    query[k * length : (k + 1) * length, cols], key[sources, cols], contract_last,
                    preferred_element_type=jnp.float32,
                )
                attn = half_silu(scores * (0.5 / math.sqrt(hdim)) + bias[h])
                attn = jnp.where(keep, attn, 0.0).astype(jnp.bfloat16)
                by_head.append(jnp.dot(attn, value[sources, cols], preferred_element_type=jnp.float32))
            mixed.append(jnp.concatenate(by_head, axis=1))
        center, spread = center_and_spread(jnp.concatenate(mixed, axis=0))
        normed = center * lax.rsqrt(spread + 1e-05)
        gated = (normed * gate.astype(jnp.float32)).astype(jnp.bfloat16)
        out = x + jnp.dot(gated, w_out[...], preferred_element_type=jnp.float32)
        out = out.astype(jnp.bfloat16).astype(jnp.float32)
        square = jnp.sum(out * out, axis=-1, keepdims=True)
        queries = (out * lax.rsqrt(square + 1e-06)).astype(jnp.bfloat16)

        target = jnp.concatenate(
            [packed_tgt[pl.ds(t * lines + k + 1, 1), :] for k in range(lines)], axis=1
        )
        dots = lax.dot_general(
            unit_ref[...], queries, contract_last, preferred_element_type=jnp.float32
        )
        total = jnp.zeros((1, tile), jnp.float32)
        target_dot = jnp.zeros((1, tile), jnp.float32)
        for j in range(blocks):
            part = dots[j * items : (j + 1) * items]
            exps = jnp.exp2(part * rate - rate)
            exp_ref[j] = exps
            total += jnp.sum(exps, axis=0, keepdims=True)
            hit = item_id == target - j * items
            target_dot += jnp.sum(jnp.where(hit, part, 0.0), axis=0, keepdims=True)
        loss = logit_scale + jnp.log(total) - logit_scale * target_dot
        for k in range(lines):
            packed_loss[pl.ds(t * lines + k, 1), :] = loss[:, k * length : (k + 1) * length]
        share = jnp.where(target >= 0, 1.0 / total, 0.0)
        for j in range(blocks):
            hit = item_id == target - j * items
            left = exp_ref[j] * share - jnp.where(hit, 1.0, 0.0)
            residual[j * items : (j + 1) * items, :] = left.astype(jnp.bfloat16)
        acc[...] += jnp.dot(residual[...], queries, preferred_element_type=jnp.float32)
        return 0

    lax.fori_loop(0, tiles, one_tile, 0)

    for u in range(per_step):
        line, turn = starts[u] // length, lax.rem(starts[u], length)
        back = lax.rem(length - turn, length)
        near = pltpu.roll(packed_loss[pl.ds(line, 1), :], back, 1)
        rest = pltpu.roll(packed_loss[pl.ds(line + 1, 1), :], back, 1)
        loss = jnp.where(place < length - turn, near, rest)
        loss_ref[pl.ds(step * per_step + u, 1), :] = jnp.where(place < lens[u], loss, 0.0)

    @pl.when(step == pl.num_programs(0) - 1)
    def _():
        for k, out_ref in enumerate((own_ref, over_ref, side_ref, far_ref)):
            rows = pl.ds(pl.multiple_of(block_ref[k] * items, items), items)
            out_ref[...] = acc[rows, :].astype(out_ref.dtype)


def users_call(packed, lens, w_in, w_out, rel_bias, unit_all, block_ids):
    users, packed_rows, width = packed.shape
    heads, length = rel_bias.shape
    blocks = block_ids.shape[0]
    items = unit_all.shape[0] // blocks
    per_step = math.gcd(users, 8)
    rows = per_step * length
    lines = -(-(rows // length + 2) // 8) * 8
    whole = lambda *shape: pl.BlockSpec(shape, lambda s, lens, ids: (0,) * len(shape))
    anywhere = pl.BlockSpec(memory_space=pl.ANY)
    part = lambda dtype: jax.ShapeDtypeStruct((items, width), dtype)
    return pl.pallas_call(
        functools.partial(users_kernel, blocks),
        grid_spec=pltpu.PrefetchScalarGridSpec(
            num_scalar_prefetch=2,
            grid=(users // per_step,),
            in_specs=[anywhere, anywhere, anywhere, whole(heads, length), anywhere],
            out_specs=[whole(users, length)] + [whole(items, width)] * 4,
            scratch_shapes=[
                pltpu.VMEM((blocks * items, width), jnp.float32),
                pltpu.VMEM((heads, length, 2 * length), jnp.float32),
                pltpu.VMEM((per_step, packed_rows, width), jnp.bfloat16),
                pltpu.VMEM(w_in.shape, jnp.bfloat16),
                pltpu.VMEM(w_out.shape, jnp.bfloat16),
                pltpu.VMEM(unit_all.shape, jnp.bfloat16),
                pltpu.VMEM((blocks, items, tile), jnp.float32),
                pltpu.VMEM((blocks * items, tile), jnp.bfloat16),
                pltpu.VMEM((rows + tile, width), jnp.bfloat16),
                pltpu.VMEM((rows + tile, length), jnp.int32),
                pltpu.VMEM((length + rows + tile, width), jnp.bfloat16),
                pltpu.VMEM((length + rows + tile, width), jnp.bfloat16),
                pltpu.VMEM((lines, length), jnp.int32),
                pltpu.VMEM((lines, length), jnp.float32),
                pltpu.SemaphoreType.DMA((per_step,)),
                pltpu.SemaphoreType.DMA((3,)),
            ],
        ),
        out_shape=[
            jax.ShapeDtypeStruct((users, length), jnp.float32),
            part(jnp.float32),
            part(jnp.float32),
            part(jnp.bfloat16),
            part(jnp.bfloat16),
        ],
        compiler_params=pltpu.CompilerParams(vmem_limit_bytes=36 * 1024 * 1024),
        name="users",
    )(lens, block_ids, packed, w_in, w_out, rel_bias, unit_all)


def shards(histories, lengths, targets, send_list, w_in, w_out, rel_bias, item_pool):
    length = histories.shape[1]
    packed = pack(histories, lengths, targets, send_list)
    packed = lax.all_to_all(packed, "dp", split_axis=0, concat_axis=0, tiled=True)

    pool_float = item_pool.astype(jnp.float32)
    item_norm = jnp.sqrt(jnp.sum(pool_float * pool_float, axis=-1, keepdims=True) + 1e-06)
    unit_rows = pool_float / item_norm
    unit_all = lax.all_gather(unit_rows.astype(jnp.bfloat16), "blk", axis=0, tiled=True)

    mine = lax.axis_index("blk")
    block_ids = jnp.stack([mine, mine ^ 2, mine ^ 1, mine ^ 3]).astype(jnp.int32)
    lens = packed[:, length, 0].astype(jnp.int32)
    row_loss, own, over, side, far = users_call(packed, lens, w_in, w_out, rel_bias, unit_all, block_ids)
    over = over + swap(far, "blk", 1).astype(jnp.float32)
    own = own + swap(side, "blk", 1).astype(jnp.float32)
    item_sum = logit_scale * (own + swap(over.astype(jnp.bfloat16), "blk", 2).astype(jnp.float32))
    pool_grad = (
        item_sum - unit_rows * jnp.sum(unit_rows * item_sum, axis=-1, keepdims=True)
    ) / item_norm
    return (row_loss, pool_grad)


def solution(mesh):
    placed = (
        P(("dp", "blk"), None, None),
        P(("dp", "blk")),
        P(("dp", "blk"), None),
        P(("dp", "blk")),
        P(),
        P(),
        P(),
        P(("dp", "blk"), None),
    )
    return jax.shard_map(
        shards,
        mesh=mesh,
        in_specs=placed,
        out_specs=(P(("dp", "blk"), None), P(("dp", "blk"), None)),
        check_vma=False,
    )
```

```python
import functools
import math

import jax
import jax.numpy as jnp
from jax import lax
from jax.experimental import pallas as pl
from jax.experimental.pallas import tpu as pltpu
from jax.sharding import PartitionSpec as P

logit_scale = 20.0
contract_last = (((1,), (1,)), ((), ()))
tile = 256
chunk = 16
number_rows = 8


def swap(array, axis, bit):
    devices = lax.axis_size(axis)
    return lax.ppermute(array, axis, [(i, i ^ bit) for i in range(devices)])


def in_hbm(array):
    return pltpu.with_memory_space_constraint(array, pltpu.HBM)


def half_silu(half):
    return half + half * jnp.tanh(half)


def center_and_spread(values):
    center = values - jnp.mean(values, axis=-1, keepdims=True)
    return center, jnp.mean(center * center, axis=-1, keepdims=True)


def pack_kernel(
    list_any, len_any, from_any, tgt_any, pool_any, to_any, unit_any,
    entries, lens, targets, pool, unit, buffer, sems, in_sems, out_sems,
):
    users = buffer.shape[0]
    _, length, width = from_any.shape
    pieces = width // length
    small = [
        pltpu.make_async_copy(source, target, sems.at[k])
        for k, (source, target) in enumerate(
            ((list_any, entries), (len_any, lens), (tgt_any, targets), (pool_any, pool))
        )
    ]
    for copy in small:
        copy.start()
    small[0].wait()
    copies_in = [
        [
            pltpu.make_async_copy(
                from_any.at[entries[k], :, pl.ds(c * length, length)],
                buffer.at[k, pl.ds(c * length, length)],
                in_sems.at[k, c],
            )
            for c in range(pieces)
        ]
        for k in range(users)
    ]
    for copies in copies_in:
        for copy in copies:
            copy.start()
    small[3].wait()
    rows = pool[...].astype(jnp.float32)
    unit[...] = (rows * lax.rsqrt(jnp.sum(rows * rows, axis=-1, keepdims=True) + 1e-06)).astype(jnp.bfloat16)
    unit_out = pltpu.make_async_copy(unit, unit_any, sems.at[4])
    unit_out.start()
    small[1].wait()
    small[2].wait()
    row = lax.broadcasted_iota(jnp.int32, (number_rows, length), 0)
    for k in range(users):
        target = targets[pl.ds(entries[k], 1), :]
        numbers = jnp.where(row == 0, lens[entries[k]], jnp.where(row == 1, target // 256, target % 256))
        buffer[k, width:, :] = numbers.astype(jnp.float32).astype(jnp.bfloat16)
    copies_out = [pltpu.make_async_copy(buffer.at[k], to_any.at[k], out_sems.at[k]) for k in range(users)]
    for k in range(users):
        for copy in copies_in[k]:
            copy.wait()
        copies_out[k].start()
    unit_out.wait()
    for copy in copies_out:
        copy.wait()


def pack(histories, lengths, targets, entries, item_pool):
    users, length, width = histories.shape
    shape = (users, width + number_rows, length)
    return pl.pallas_call(
        pack_kernel,
        in_specs=[pl.BlockSpec(memory_space=pltpu.HBM)] * 5,
        out_specs=[pl.BlockSpec(memory_space=pltpu.HBM)] * 2,
        scratch_shapes=[
            pltpu.SMEM(entries.shape, jnp.int32),
            pltpu.SMEM(lengths.shape, jnp.int32),
            pltpu.VMEM(targets.shape, jnp.int32),
            pltpu.VMEM(item_pool.shape, jnp.bfloat16),
            pltpu.VMEM(item_pool.shape, jnp.bfloat16),
            pltpu.VMEM(shape, jnp.bfloat16),
            pltpu.SemaphoreType.DMA((5,)),
            pltpu.SemaphoreType.DMA((users, width // length)),
            pltpu.SemaphoreType.DMA((users,)),
        ],
        out_shape=[
            jax.ShapeDtypeStruct(shape, jnp.bfloat16),
            jax.ShapeDtypeStruct(item_pool.shape, jnp.bfloat16),
        ],
        compiler_params=pltpu.CompilerParams(vmem_limit_bytes=16 * 1024 * 1024),
        name="pack",
    )(*[in_hbm(array) for array in (entries, lengths, histories, targets, item_pool)])


def users_kernel(
    blocks, len_ref, block_ref, x_any, w_in_any, w_out_any, bias_in, unit_any,
    loss_ref, own_ref, over_ref, side_ref, far_ref,
    acc, bias, x_ref, w_in, w_out, unit_ref, exp_ref, residual, events, starts_ref, key, value,
    packed_tgt, packed_loss, x_sems, w_sems,
):
    step = pl.program_id(0)
    heads, length = bias_in.shape
    per_step = x_ref.shape[0]
    width = w_out.shape[0]
    hdim = width // heads
    items = unit_ref.shape[0] // blocks
    lines = tile // length

    x_copies = [
        pltpu.make_async_copy(x_any.at[step * per_step + u], x_ref.at[u], x_sems.at[u])
        for u in range(per_step)
    ]
    w_copies = [
        pltpu.make_async_copy(w_in_any, w_in, w_sems.at[0]),
        pltpu.make_async_copy(w_out_any, w_out, w_sems.at[1]),
        pltpu.make_async_copy(unit_any, unit_ref, w_sems.at[2]),
    ]
    for copy in x_copies:
        copy.start()

    @pl.when(step == 0)
    def _():
        for copy in w_copies:
            copy.start()
        acc[...] = jnp.zeros_like(acc)
        for h in range(heads):
            wide = jnp.broadcast_to(0.5 * bias_in[h : h + 1, :], (length, length))
            turned = pltpu.roll(wide, 0, 1, stride=1, stride_axis=0).T
            bias[h] = jnp.concatenate([turned, turned], axis=1)

    lens = [len_ref[step * per_step + u] for u in range(per_step)]
    starts, end = [], 0
    for u in range(per_step):
        starts.append(pl.multiple_of(end, chunk) if u else 0)
        end = end + (lens[u] + chunk - 1) // chunk * chunk
    end = pl.multiple_of(end, chunk)
    tiles = (end + tile - 1) // tile

    place = lax.broadcasted_iota(jnp.int32, (1, length), 1)
    packed_tgt[...] = jnp.full_like(packed_tgt, -1)
    key[:length, :] = jnp.zeros((length, width), key.dtype)
    value[:length, :] = jnp.zeros((length, width), value.dtype)
    for u in range(per_step):
        starts_ref[pl.ds(starts[u], length), :] = jnp.full((length, length), starts[u], jnp.int32)
    for copy in x_copies:
        copy.wait()
    for u in range(per_step):
        for c in range(0, width, length):
            events[pl.ds(starts[u], length), c : c + length] = x_ref[u, c : c + length, :]
        digits = x_ref[u, width:, :].astype(jnp.float32)
        target = digits[1:2, :] * 256.0 + digits[2:3, :]
        wanted = jnp.where(place < lens[u], target.astype(jnp.int32), -1)
        line, turn = starts[u] // length + 1, lax.rem(starts[u], length)
        turned = pltpu.roll(wanted, turn, 1)
        packed_tgt[pl.ds(line, 1), :] = jnp.where(place >= turn, turned, packed_tgt[pl.ds(line, 1), :])
        packed_tgt[pl.ds(line + 1, 1), :] = jnp.where(
            place < turn, turned, packed_tgt[pl.ds(line + 1, 1), :]
        )
    events[pl.ds(end, tile), :] = jnp.zeros((tile, width), events.dtype)

    @pl.when(step == 0)
    def _():
        for copy in w_copies:
            copy.wait()

    row = lax.broadcasted_iota(jnp.int32, (length, length), 0)
    col = lax.broadcasted_iota(jnp.int32, (length, length), 1)
    item_id = lax.broadcasted_iota(jnp.int32, (items, tile), 0)
    rate = logit_scale * math.log2(math.e)

    def one_tile(t, _):
        first = pl.multiple_of(t * tile, tile)
        x = events[pl.ds(first, tile), :].astype(jnp.float32)
        center, spread = center_and_spread(x)
        half_normed = (center * (0.5 * lax.rsqrt(spread + 1e-05))).astype(jnp.bfloat16)
        gate, values, query, keys = [
            half_silu(
                jnp.dot(
                    half_normed, w_in[:, part * width : (part + 1) * width],
                    preferred_element_type=jnp.float32,
                )
            ).astype(jnp.bfloat16)
            for part in range(4)
        ]
        key[pl.ds(first + length, tile), :] = keys
        value[pl.ds(first + length, tile), :] = values
        mixed = []
        for k in range(lines):
            base = pl.multiple_of(first + k * length, length)
            sources = pl.ds(base, 2 * length)
            start = starts_ref[pl.ds(base, length), :]
            ahead = packed_tgt[pl.ds(t * lines + k, 1), :] >= 0
            here = packed_tgt[pl.ds(t * lines + k + 1, 1), :] >= 0
            keep_ahead = (base - length + col >= start) & ahead
            keep_here = (col <= row) & (base + col >= start) & here
            keep = jnp.concatenate([keep_ahead, keep_here], axis=1)
            by_head = []
            for h in range(heads):
                cols = slice(h * hdim, (h + 1) * hdim)
                scores = lax.dot_general(
                    query[k * length : (k + 1) * length, cols], key[sources, cols], contract_last,
                    preferred_element_type=jnp.float32,
                )
                attn = half_silu(scores * (0.5 / math.sqrt(hdim)) + bias[h])
                attn = jnp.where(keep, attn, 0.0).astype(jnp.bfloat16)
                by_head.append(jnp.dot(attn, value[sources, cols], preferred_element_type=jnp.float32))
            mixed.append(jnp.concatenate(by_head, axis=1))
        center, spread = center_and_spread(jnp.concatenate(mixed, axis=0))
        normed = center * lax.rsqrt(spread + 1e-05)
        gated = (normed * gate.astype(jnp.float32)).astype(jnp.bfloat16)
        out = x + jnp.dot(gated, w_out[...], preferred_element_type=jnp.float32)
        out = out.astype(jnp.bfloat16).astype(jnp.float32)
        square = jnp.sum(out * out, axis=-1, keepdims=True)
        queries = (out * lax.rsqrt(square + 1e-06)).astype(jnp.bfloat16)

        target = jnp.concatenate(
            [packed_tgt[pl.ds(t * lines + k + 1, 1), :] for k in range(lines)], axis=1
        )
        dots = lax.dot_general(
            unit_ref[...], queries, contract_last, preferred_element_type=jnp.float32
        )
        total = jnp.zeros((1, tile), jnp.float32)
        target_dot = jnp.zeros((1, tile), jnp.float32)
        for j in range(blocks):
            part = dots[j * items : (j + 1) * items]
            exps = jnp.exp2(part * rate - rate)
            exp_ref[j] = exps
            total += jnp.sum(exps, axis=0, keepdims=True)
            hit = item_id == target - j * items
            target_dot += jnp.sum(jnp.where(hit, part, 0.0), axis=0, keepdims=True)
        loss = logit_scale + jnp.log(total) - logit_scale * target_dot
        for k in range(lines):
            packed_loss[pl.ds(t * lines + k, 1), :] = loss[:, k * length : (k + 1) * length]
        share = jnp.where(target >= 0, 1.0 / total, 0.0)
        for j in range(blocks):
            hit = item_id == target - j * items
            left = exp_ref[j] * share - jnp.where(hit, 1.0, 0.0)
            residual[j * items : (j + 1) * items, :] = left.astype(jnp.bfloat16)
        acc[...] += jnp.dot(residual[...], queries, preferred_element_type=jnp.float32)
        return 0

    lax.fori_loop(0, tiles, one_tile, 0)

    for u in range(per_step):
        line, turn = starts[u] // length, lax.rem(starts[u], length)
        back = lax.rem(length - turn, length)
        near = pltpu.roll(packed_loss[pl.ds(line, 1), :], back, 1)
        rest = pltpu.roll(packed_loss[pl.ds(line + 1, 1), :], back, 1)
        loss = jnp.where(place < length - turn, near, rest)
        loss_ref[pl.ds(step * per_step + u, 1), :] = jnp.where(place < lens[u], loss, 0.0)

    @pl.when(step == pl.num_programs(0) - 1)
    def _():
        for k, out_ref in enumerate((own_ref, over_ref, side_ref, far_ref)):
            rows = pl.ds(pl.multiple_of(block_ref[k] * items, items), items)
            out_ref[...] = acc[rows, :].astype(out_ref.dtype)


def users_call(packed, lens, w_in, w_out, rel_bias, unit_all, block_ids):
    users, packed_rows, length = packed.shape
    heads, width = rel_bias.shape[0], w_out.shape[0]
    blocks = block_ids.shape[0]
    items = unit_all.shape[0] // blocks
    per_step = math.gcd(users, 8)
    rows = per_step * length
    lines = -(-(rows // length + 2) // 8) * 8
    whole = lambda *shape: pl.BlockSpec(shape, lambda s, lens, ids: (0,) * len(shape))
    anywhere, hbm = pl.BlockSpec(memory_space=pl.ANY), pl.BlockSpec(memory_space=pltpu.HBM)
    part = lambda dtype: jax.ShapeDtypeStruct((items, width), dtype)
    return pl.pallas_call(
        functools.partial(users_kernel, blocks),
        grid_spec=pltpu.PrefetchScalarGridSpec(
            num_scalar_prefetch=2,
            grid=(users // per_step,),
            in_specs=[anywhere, anywhere, hbm, whole(heads, length), hbm],
            out_specs=[whole(users, length)] + [whole(items, width)] * 4,
            scratch_shapes=[
                pltpu.VMEM((blocks * items, width), jnp.float32),
                pltpu.VMEM((heads, length, 2 * length), jnp.float32),
                pltpu.VMEM((per_step, packed_rows, length), jnp.bfloat16),
                pltpu.VMEM(w_in.shape, jnp.bfloat16),
                pltpu.VMEM(w_out.shape, jnp.bfloat16),
                pltpu.VMEM(unit_all.shape, jnp.bfloat16),
                pltpu.VMEM((blocks, items, tile), jnp.float32),
                pltpu.VMEM((blocks * items, tile), jnp.bfloat16),
                pltpu.VMEM((rows + tile, width), jnp.bfloat16),
                pltpu.VMEM((rows + tile, length), jnp.int32),
                pltpu.VMEM((length + rows + tile, width), jnp.bfloat16),
                pltpu.VMEM((length + rows + tile, width), jnp.bfloat16),
                pltpu.VMEM((lines, length), jnp.int32),
                pltpu.VMEM((lines, length), jnp.float32),
                pltpu.SemaphoreType.DMA((per_step,)),
                pltpu.SemaphoreType.DMA((3,)),
            ],
        ),
        out_shape=[
            jax.ShapeDtypeStruct((users, length), jnp.float32),
            part(jnp.float32),
            part(jnp.float32),
            part(jnp.bfloat16),
            part(jnp.bfloat16),
        ],
        compiler_params=pltpu.CompilerParams(vmem_limit_bytes=36 * 1024 * 1024),
        name="users",
    )(lens, block_ids, packed, w_in, in_hbm(w_out), rel_bias, in_hbm(unit_all))


def shards(histories, lengths, targets, send_list, w_in, w_out, rel_bias, item_pool):
    packed, unit_bf = pack(histories, lengths, targets, send_list, item_pool)
    packed = lax.all_to_all(packed, "dp", split_axis=0, concat_axis=0, tiled=True)
    unit_all = lax.all_gather(unit_bf, "blk", axis=0, tiled=True)

    pool_float = item_pool.astype(jnp.float32)
    item_norm = jnp.sqrt(jnp.sum(pool_float * pool_float, axis=-1, keepdims=True) + 1e-06)
    unit_rows = pool_float / item_norm

    mine = lax.axis_index("blk")
    block_ids = jnp.stack([mine, mine ^ 2, mine ^ 1, mine ^ 3]).astype(jnp.int32)
    lens = packed[:, histories.shape[2], 0].astype(jnp.int32)
    row_loss, own, over, side, far = users_call(packed, lens, w_in, w_out, rel_bias, unit_all, block_ids)
    over = over + swap(far, "blk", 1).astype(jnp.float32)
    own = own + swap(side, "blk", 1).astype(jnp.float32)
    item_sum = logit_scale * (own + swap(over.astype(jnp.bfloat16), "blk", 2).astype(jnp.float32))
    pool_grad = (
        item_sum - unit_rows * jnp.sum(unit_rows * item_sum, axis=-1, keepdims=True)
    ) / item_norm
    return (row_loss, pool_grad)


def solution(mesh):
    placed = (
        P(("dp", "blk"), None, None),
        P(("dp", "blk")),
        P(("dp", "blk"), None),
        P(("dp", "blk")),
        P(),
        P(),
        P(),
        P(("dp", "blk"), None),
    )
    return jax.shard_map(
        shards,
        mesh=mesh,
        in_specs=placed,
        out_specs=(P(("dp", "blk"), None), P(("dp", "blk"), None)),
        check_vma=False,
    )
```

```python
import functools
import math

import jax
import jax.numpy as jnp
from jax import lax
from jax.experimental import pallas as pl
from jax.experimental.pallas import tpu as pltpu
from jax.sharding import PartitionSpec as P

logit_scale = 20.0
contract_last = (((1,), (1,)), ((), ()))
tile = 512
chunk = 16
number_rows = 8


def swap(array, axis, bit):
    devices = lax.axis_size(axis)
    return lax.ppermute(array, axis, [(i, i ^ bit) for i in range(devices)])


def in_hbm(array):
    return pltpu.with_memory_space_constraint(array, pltpu.HBM)


def half_silu(half):
    return half + half * jnp.tanh(half)


def center_and_spread(values):
    center = values - jnp.mean(values, axis=-1, keepdims=True)
    return center, jnp.mean(center * center, axis=-1, keepdims=True)


def pack_kernel(
    list_any, len_any, from_any, tgt_any, pool_any, to_any, unit_any,
    entries, lens, targets, pool, unit, buffer, sems, in_sems, out_sems,
):
    users, length, width = from_any.shape
    pieces = width // length
    small = [
        pltpu.make_async_copy(source, target, sems.at[k])
        for k, (source, target) in enumerate(
            ((list_any, entries), (len_any, lens), (tgt_any, targets), (pool_any, pool))
        )
    ]
    for copy in small:
        copy.start()
    copies_in = [
        [
            pltpu.make_async_copy(
                from_any.at[u, :, pl.ds(c * length, length)],
                buffer.at[u, pl.ds(c * length, length)],
                in_sems.at[u, c],
            )
            for c in range(pieces)
        ]
        for u in range(users)
    ]
    for copies in copies_in:
        for copy in copies:
            copy.start()
    small[3].wait()
    rows = pool[...].astype(jnp.float32)
    unit[...] = (rows * lax.rsqrt(jnp.sum(rows * rows, axis=-1, keepdims=True) + 1e-06)).astype(jnp.bfloat16)
    unit_out = pltpu.make_async_copy(unit, unit_any, sems.at[4])
    unit_out.start()
    small[1].wait()
    small[2].wait()
    row = lax.broadcasted_iota(jnp.int32, (number_rows, length), 0)
    for u in range(users):
        target = targets[u : u + 1, :]
        numbers = jnp.where(row == 0, lens[u], jnp.where(row == 1, target // 256, target % 256))
        buffer[u, width:, :] = numbers.astype(jnp.float32).astype(jnp.bfloat16)
    small[0].wait()
    for copies in copies_in:
        for copy in copies:
            copy.wait()
    copies_out = [
        pltpu.make_async_copy(buffer.at[entries[k]], to_any.at[k], out_sems.at[k]) for k in range(users)
    ]
    for copy in copies_out:
        copy.start()
    unit_out.wait()
    for copy in copies_out:
        copy.wait()


def pack(histories, lengths, targets, entries, item_pool):
    users, length, width = histories.shape
    shape = (users, width + number_rows, length)
    return pl.pallas_call(
        pack_kernel,
        in_specs=[pl.BlockSpec(memory_space=pltpu.HBM)] * 5,
        out_specs=[pl.BlockSpec(memory_space=pltpu.HBM)] * 2,
        scratch_shapes=[
            pltpu.SMEM(entries.shape, jnp.int32),
            pltpu.SMEM(lengths.shape, jnp.int32),
            pltpu.VMEM(targets.shape, jnp.int32),
            pltpu.VMEM(item_pool.shape, jnp.bfloat16),
            pltpu.VMEM(item_pool.shape, jnp.bfloat16),
            pltpu.VMEM(shape, jnp.bfloat16),
            pltpu.SemaphoreType.DMA((5,)),
            pltpu.SemaphoreType.DMA((users, width // length)),
            pltpu.SemaphoreType.DMA((users,)),
        ],
        out_shape=[
            pltpu.HBM(shape, jnp.bfloat16),
            pltpu.HBM(item_pool.shape, jnp.bfloat16),
        ],
        compiler_params=pltpu.CompilerParams(vmem_limit_bytes=16 * 1024 * 1024),
        name="pack",
    )(*[in_hbm(array) for array in (entries, lengths, histories, targets, item_pool)])


def users_kernel(
    blocks, per_step, len_ref, block_ref, x_ref, w_in, w_out, bias_in, unit_any,
    loss_ref, own_ref, over_ref, side_ref, far_ref,
    acc, bias, exp_ref, residual, events, starts_ref, key, value, packed_tgt, packed_loss,
    unit_ref, unit_sems,
):
    heads, length = bias_in.shape
    items = unit_ref.shape[0] // blocks
    unit_copies = [
        pltpu.make_async_copy(
            unit_any.at[pl.ds(k * items, items)], unit_ref.at[pl.ds(k * items, items)], unit_sems.at[k]
        )
        for k in range(blocks)
    ]
    for copy in unit_copies:
        copy.start()
    acc[...] = jnp.zeros_like(acc)
    for h in range(heads):
        wide = jnp.broadcast_to(0.5 * bias_in[h : h + 1, :], (length, length))
        turned = pltpu.roll(wide, 0, 1, stride=1, stride_axis=0).T
        bias[h] = jnp.concatenate([turned, turned], axis=1)

    def units_arrive():
        for copy in unit_copies:
            copy.wait()

    def one_step(step, _):
        users_step(
            step, units_arrive if steps == 1 else None, blocks, per_step, len_ref, x_ref, w_in, w_out, unit_ref, loss_ref,
            acc, bias, exp_ref, residual, events, starts_ref, key, value, packed_tgt, packed_loss,
        )
        return 0

    steps = x_ref.shape[0] // per_step
    if steps == 1:
        one_step(0, 0)
    else:
        units_arrive()
        lax.fori_loop(0, steps, one_step, 0)

    for k, out_ref in enumerate((own_ref, over_ref, side_ref, far_ref)):
        rows = pl.ds(pl.multiple_of(block_ref[k] * items, items), items)
        out_ref[...] = acc[rows, :].astype(out_ref.dtype)


def users_step(
    step, units_arrive, blocks, per_step, len_ref, x_ref, w_in, w_out, unit_ref, loss_ref,
    acc, bias, exp_ref, residual, events, starts_ref, key, value, packed_tgt, packed_loss,
):
    heads, length, _ = bias.shape
    width = w_out.shape[0]
    hdim = width // heads
    items = unit_ref.shape[0] // blocks
    lines = tile // length

    lens = [len_ref[step * per_step + u] for u in range(per_step)]
    starts, end = [], 0
    for u in range(per_step):
        starts.append(pl.multiple_of(end, chunk) if u else 0)
        end = end + (lens[u] + chunk - 1) // chunk * chunk
    end = pl.multiple_of(end, chunk)
    tiles = (end + tile - 1) // tile

    place = lax.broadcasted_iota(jnp.int32, (1, length), 1)
    packed_tgt[...] = jnp.full_like(packed_tgt, -1)
    key[:length, :] = jnp.zeros((length, width), key.dtype)
    value[:length, :] = jnp.zeros((length, width), value.dtype)
    for u in range(per_step):
        starts_ref[pl.ds(starts[u], length), :] = jnp.full((length, length), starts[u], jnp.int32)
    for u in range(per_step):
        for c in range(0, width, length):
            events[pl.ds(starts[u], length), c : c + length] = x_ref[step * per_step + u, c : c + length, :]
        digits = x_ref[step * per_step + u, width:, :].astype(jnp.float32)
        target = digits[1:2, :] * 256.0 + digits[2:3, :]
        wanted = jnp.where(place < lens[u], target.astype(jnp.int32), -1)
        line, turn = starts[u] // length + 1, lax.rem(starts[u], length)
        turned = pltpu.roll(wanted, turn, 1)
        packed_tgt[pl.ds(line, 1), :] = jnp.where(place >= turn, turned, packed_tgt[pl.ds(line, 1), :])
        packed_tgt[pl.ds(line + 1, 1), :] = jnp.where(
            place < turn, turned, packed_tgt[pl.ds(line + 1, 1), :]
        )
    events[pl.ds(end, tile), :] = jnp.zeros((tile, width), events.dtype)

    if units_arrive:
        units_arrive()
    row = lax.broadcasted_iota(jnp.int32, (length, length), 0)
    col = lax.broadcasted_iota(jnp.int32, (length, length), 1)
    item_id = lax.broadcasted_iota(jnp.int32, (items, tile), 0)
    rate = logit_scale * math.log2(math.e)

    def one_tile(t, _):
        first = pl.multiple_of(t * tile, tile)
        x = events[pl.ds(first, tile), :].astype(jnp.float32)
        center, spread = center_and_spread(x)
        half_normed = (center * (0.5 * lax.rsqrt(spread + 1e-05))).astype(jnp.bfloat16)
        gate, values, query, keys = [
            half_silu(
                jnp.dot(
                    half_normed, w_in[:, part * width : (part + 1) * width],
                    preferred_element_type=jnp.float32,
                )
            ).astype(jnp.bfloat16)
            for part in range(4)
        ]
        key[pl.ds(first + length, tile), :] = keys
        value[pl.ds(first + length, tile), :] = values
        mixed = []
        for k in range(lines):
            base = pl.multiple_of(first + k * length, length)
            sources = pl.ds(base, 2 * length)
            start = starts_ref[pl.ds(base, length), :]
            ahead = packed_tgt[pl.ds(t * lines + k, 1), :] >= 0
            here = packed_tgt[pl.ds(t * lines + k + 1, 1), :] >= 0
            keep_ahead = (base - length + col >= start) & ahead
            keep_here = (col <= row) & (base + col >= start) & here
            keep = jnp.concatenate([keep_ahead, keep_here], axis=1)
            by_head = []
            for h in range(heads):
                cols = slice(h * hdim, (h + 1) * hdim)
                scores = lax.dot_general(
                    query[k * length : (k + 1) * length, cols], key[sources, cols], contract_last,
                    preferred_element_type=jnp.float32,
                )
                attn = half_silu(scores * (0.5 / math.sqrt(hdim)) + bias[h])
                attn = jnp.where(keep, attn, 0.0).astype(jnp.bfloat16)
                by_head.append(jnp.dot(attn, value[sources, cols], preferred_element_type=jnp.float32))
            mixed.append(jnp.concatenate(by_head, axis=1))
        center, spread = center_and_spread(jnp.concatenate(mixed, axis=0))
        normed = center * lax.rsqrt(spread + 1e-05)
        gated = (normed * gate.astype(jnp.float32)).astype(jnp.bfloat16)
        out = x + jnp.dot(gated, w_out[...], preferred_element_type=jnp.float32)
        out = out.astype(jnp.bfloat16).astype(jnp.float32)
        square = jnp.sum(out * out, axis=-1, keepdims=True)
        queries = (out * lax.rsqrt(square + 1e-06)).astype(jnp.bfloat16)

        target = jnp.concatenate(
            [packed_tgt[pl.ds(t * lines + k + 1, 1), :] for k in range(lines)], axis=1
        )
        dots = lax.dot_general(
            unit_ref[...], queries, contract_last, preferred_element_type=jnp.float32
        )
        total = jnp.zeros((1, tile), jnp.float32)
        target_dot = jnp.zeros((1, tile), jnp.float32)
        for j in range(blocks):
            part = dots[j * items : (j + 1) * items]
            exps = jnp.exp2(part * rate - rate)
            exp_ref[j] = exps
            total += jnp.sum(exps, axis=0, keepdims=True)
            hit = item_id == target - j * items
            target_dot += jnp.sum(jnp.where(hit, part, 0.0), axis=0, keepdims=True)
        loss = logit_scale + jnp.log(total) - logit_scale * target_dot
        for k in range(lines):
            packed_loss[pl.ds(t * lines + k, 1), :] = loss[:, k * length : (k + 1) * length]
        share = jnp.where(target >= 0, 1.0 / total, 0.0)
        for j in range(blocks):
            hit = item_id == target - j * items
            left = exp_ref[j] * share - jnp.where(hit, 1.0, 0.0)
            residual[j * items : (j + 1) * items, :] = left.astype(jnp.bfloat16)
        acc[...] += jnp.dot(residual[...], queries, preferred_element_type=jnp.float32)
        return 0

    lax.fori_loop(0, tiles, one_tile, 0)

    for u in range(per_step):
        line, turn = starts[u] // length, lax.rem(starts[u], length)
        back = lax.rem(length - turn, length)
        near = pltpu.roll(packed_loss[pl.ds(line, 1), :], back, 1)
        rest = pltpu.roll(packed_loss[pl.ds(line + 1, 1), :], back, 1)
        loss = jnp.where(place < length - turn, near, rest)
        loss_ref[pl.ds(step * per_step + u, 1), :] = jnp.where(place < lens[u], loss, 0.0)


def users_call(packed, lens, w_in, w_out, rel_bias, unit_all, block_ids):
    users, _, length = packed.shape
    heads, width = rel_bias.shape[0], w_out.shape[0]
    blocks = block_ids.shape[0]
    items = unit_all.shape[0] // blocks
    per_step = math.gcd(users, 8)
    rows = -(-per_step * length // tile) * tile
    lines = -(-(rows // length + 2) // 8) * 8
    scalar, whole = pl.BlockSpec(memory_space=pltpu.SMEM), pl.BlockSpec(memory_space=pltpu.VMEM)
    part = lambda dtype: pltpu.VMEM((items, width), dtype)
    in_vmem = lambda array: pltpu.with_memory_space_constraint(array, pltpu.VMEM)
    return pl.pallas_call(
        functools.partial(users_kernel, blocks, per_step),
        in_specs=[scalar, scalar, whole, whole, whole, whole, pl.BlockSpec(memory_space=pltpu.HBM)],
        out_specs=[whole] * 5,
        scratch_shapes=[
            pltpu.VMEM((blocks * items, width), jnp.float32),
            pltpu.VMEM((heads, length, 2 * length), jnp.float32),
            pltpu.VMEM((blocks, items, tile), jnp.float32),
            pltpu.VMEM((blocks * items, tile), jnp.bfloat16),
            pltpu.VMEM((rows + tile, width), jnp.bfloat16),
            pltpu.VMEM((rows + tile, length), jnp.int32),
            pltpu.VMEM((length + rows + tile, width), jnp.bfloat16),
            pltpu.VMEM((length + rows + tile, width), jnp.bfloat16),
            pltpu.VMEM((lines, length), jnp.int32),
            pltpu.VMEM((lines, length), jnp.float32),
            pltpu.VMEM(unit_all.shape, jnp.bfloat16),
            pltpu.SemaphoreType.DMA((blocks,)),
        ],
        out_shape=[
            jax.ShapeDtypeStruct((users, length), jnp.float32),
            part(jnp.float32),
            part(jnp.float32),
            part(jnp.bfloat16),
            part(jnp.bfloat16),
        ],
        compiler_params=pltpu.CompilerParams(vmem_limit_bytes=32 * 1024 * 1024),
        name="users",
    )(lens, block_ids, *[in_vmem(array) for array in (packed, w_in, w_out, rel_bias)], in_hbm(unit_all))


def shards(histories, lengths, targets, send_list, w_in, w_out, rel_bias, item_pool):
    packed, unit_bf = pack(histories, lengths, targets, send_list, item_pool)
    packed = lax.all_to_all(packed, "dp", split_axis=0, concat_axis=0, tiled=True)
    unit_all = lax.all_gather(unit_bf, "blk", axis=0, tiled=True)

    pool_float = item_pool.astype(jnp.float32)
    item_norm = jnp.sqrt(jnp.sum(pool_float * pool_float, axis=-1, keepdims=True) + 1e-06)
    unit_rows = pool_float / item_norm

    mine = lax.axis_index("blk")
    block_ids = jnp.stack([mine, mine ^ 2, mine ^ 1, mine ^ 3]).astype(jnp.int32)
    lens = packed[:, histories.shape[2], 0].astype(jnp.int32)
    row_loss, own, over, side, far = users_call(packed, lens, w_in, w_out, rel_bias, unit_all, block_ids)
    over = over + swap(far, "blk", 1).astype(jnp.float32)
    own = own + swap(side, "blk", 1).astype(jnp.float32)
    item_sum = logit_scale * (own + swap(over.astype(jnp.bfloat16), "blk", 2).astype(jnp.float32))
    pool_grad = (
        item_sum - unit_rows * jnp.sum(unit_rows * item_sum, axis=-1, keepdims=True)
    ) / item_norm
    return (row_loss, pool_grad)


def solution(mesh):
    placed = (
        P(("dp", "blk"), None, None),
        P(("dp", "blk")),
        P(("dp", "blk"), None),
        P(("dp", "blk")),
        P(),
        P(),
        P(),
        P(("dp", "blk"), None),
    )
    return jax.shard_map(
        shards,
        mesh=mesh,
        in_specs=placed,
        out_specs=(P(("dp", "blk"), None), P(("dp", "blk"), None)),
        check_vma=False,
    )
```

```python
import functools
import math

import jax
import jax.numpy as jnp
from jax import lax
from jax.experimental import pallas as pl
from jax.experimental.pallas import tpu as pltpu
from jax.sharding import PartitionSpec as P

logit_scale = 20.0
contract_last = (((1,), (1,)), ((), ()))
tile = 256
chunk = 16
number_rows = 8


def swap(array, axis, bit):
    devices = lax.axis_size(axis)
    return lax.ppermute(array, axis, [(i, i ^ bit) for i in range(devices)])


def from_behind(array, axis, by):
    devices = lax.axis_size(axis)
    return lax.ppermute(array, axis, [(i, (i + by) % devices) for i in range(devices)])


def in_vmem(array):
    return pltpu.with_memory_space_constraint(array, pltpu.VMEM)


def in_hbm(array):
    return pltpu.with_memory_space_constraint(array, pltpu.HBM)


def half_silu(half):
    return half + half * jnp.tanh(half)


def center_and_spread(values):
    center = values - jnp.mean(values, axis=-1, keepdims=True)
    return center, jnp.mean(center * center, axis=-1, keepdims=True)


def pack_kernel(
    work, groups, group_ref, list_any, len_any, from_any, tgt_any, pool_any, *refs,
):
    users = from_any.shape[0]
    to_refs, unit_any = refs[:users], refs[users]
    entries, lens, targets, pool, unit, buffer, sems, in_sems, out_sems = refs[users + 1 :]
    users, length, width = from_any.shape
    pieces = width // length
    small = [
        pltpu.make_async_copy(source, target, sems.at[k])
        for k, (source, target) in enumerate(
            ((list_any, entries), (len_any, lens), (tgt_any, targets), (pool_any, pool))
        )
    ]
    for copy in small:
        copy.start()
    copies_in = [
        [
            pltpu.make_async_copy(
                from_any.at[u, :, pl.ds(c * length, length)],
                buffer.at[u, pl.ds(c * length, length)],
                in_sems.at[u, c],
            )
            for c in range(pieces)
        ]
        for u in range(users)
    ]
    for copies in copies_in:
        for copy in copies:
            copy.start()
    small[3].wait()
    rows = pool[...].astype(jnp.float32)
    unit[...] = (rows * lax.rsqrt(jnp.sum(rows * rows, axis=-1, keepdims=True) + 1e-06)).astype(jnp.bfloat16)
    unit_out = pltpu.make_async_copy(unit, unit_any, sems.at[4])
    unit_out.start()
    small[1].wait()
    small[2].wait()
    row = lax.broadcasted_iota(jnp.int32, (number_rows, length), 0)
    for u in range(users):
        target = targets[u : u + 1, :]
        numbers = jnp.where(row == 0, lens[u], jnp.where(row == 1, target // 256, target % 256))
        buffer[u, width:, :] = numbers.astype(jnp.float32).astype(jnp.bfloat16)
    small[0].wait()
    copies_out = []
    for k, (shift, slot) in enumerate(work):
        user = entries[(group_ref[0] + shift) % groups * (users // groups) + slot]
        for c in range(pieces):
            pltpu.make_async_copy(
                from_any.at[user, :, pl.ds(c * length, length)],
                buffer.at[user, pl.ds(c * length, length)],
                in_sems.at[user, c],
            ).wait()
        copies_out.append(pltpu.make_async_copy(buffer.at[user], to_refs[k], out_sems.at[k]))
        copies_out[k].start()
    unit_out.wait()
    for copy in copies_out:
        copy.wait()


def pack(histories, lengths, targets, entries, item_pool, work, groups, group):
    users, length, width = histories.shape
    shape = (users, width + number_rows, length)
    hbm = pl.BlockSpec(memory_space=pltpu.HBM)
    return pl.pallas_call(
        functools.partial(pack_kernel, work, groups),
        in_specs=[pl.BlockSpec(memory_space=pltpu.SMEM)] + [hbm] * 5,
        out_specs=[hbm] * (users + 1),
        scratch_shapes=[
            pltpu.SMEM(entries.shape, jnp.int32),
            pltpu.SMEM(lengths.shape, jnp.int32),
            pltpu.VMEM(targets.shape, jnp.int32),
            pltpu.VMEM(item_pool.shape, jnp.bfloat16),
            pltpu.VMEM(item_pool.shape, jnp.bfloat16),
            pltpu.VMEM(shape, jnp.bfloat16),
            pltpu.SemaphoreType.DMA((5,)),
            pltpu.SemaphoreType.DMA((users, width // length)),
            pltpu.SemaphoreType.DMA((users,)),
        ],
        out_shape=[pltpu.HBM(shape[1:], jnp.bfloat16)] * users + [pltpu.HBM(item_pool.shape, jnp.bfloat16)],
        compiler_params=pltpu.CompilerParams(vmem_limit_bytes=16 * 1024 * 1024),
        name="pack",
    )(group, *[in_hbm(array) for array in (entries, lengths, histories, targets, item_pool)])


def users_kernel(
    places, blocks, first, last, id_ref, w_in, w_out, bias_in, *refs,
):
    count = len(places)
    x_refs, unit_refs, refs = refs[:count], refs[count : count + blocks], refs[count + blocks :]
    if not first:
        loss_in, sums_in, refs = refs[0], refs[1 : 1 + blocks], refs[1 + blocks :]
    loss_ref, out_refs, refs = refs[0], refs[1 : 1 + blocks], refs[1 + blocks :]
    wide_sums, bias, scratch = refs[0], refs[1], refs[2:]
    heads, length = bias_in.shape
    sums = [
        ref if ref.dtype == jnp.float32 else wide_sums.at[k - blocks // 2] for k, ref in enumerate(out_refs)
    ]
    loss_ref[...] = jnp.zeros_like(loss_ref) if first else loss_in[...]
    for k in range(blocks):
        sums[k][...] = jnp.zeros_like(sums[k]) if first else sums_in[k][...]
    for h in range(heads):
        wide = jnp.broadcast_to(0.5 * bias_in[h : h + 1, :], (length, length))
        turned = pltpu.roll(wide, 0, 1, stride=1, stride_axis=0).T
        bias[h] = jnp.concatenate([turned, turned], axis=1)
    for at in range(0, count, 8):
        users_step(
            x_refs[at : at + 8], [id_ref[blocks + k] for k in places[at : at + 8]],
            [id_ref[k] for k in range(blocks)], w_in, w_out, unit_refs, loss_ref, sums, bias, *scratch,
        )
    for k in range(blocks):
        if sums[k] is not out_refs[k]:
            out_refs[k][...] = sums[k][...].astype(out_refs[k].dtype)


def users_step(
    x_refs, spots, block_ids, w_in, w_out, unit_refs, loss_ref, sums, bias,
    exp_ref, residual, events, starts_ref, key, value, packed_tgt, packed_loss,
):
    heads, length, _ = bias.shape
    width = w_out.shape[0]
    hdim = width // heads
    items = unit_refs[0].shape[0]
    lines = tile // length
    per_step = len(x_refs)

    digits = [ref[width:, :].astype(jnp.float32) for ref in x_refs]
    lens = [jnp.max(digit[:1, :]).astype(jnp.int32) for digit in digits]
    starts, end = [], 0
    for u in range(per_step):
        starts.append(pl.multiple_of(end, chunk) if u else 0)
        end = end + (lens[u] + chunk - 1) // chunk * chunk
    end = pl.multiple_of(end, chunk)
    tiles = (end + tile - 1) // tile

    place = lax.broadcasted_iota(jnp.int32, (1, length), 1)
    packed_tgt[...] = jnp.full_like(packed_tgt, -1)
    key[:length, :] = jnp.zeros((length, width), key.dtype)
    value[:length, :] = jnp.zeros((length, width), value.dtype)
    for u in range(per_step):
        starts_ref[pl.ds(starts[u], length), :] = jnp.full((length, length), starts[u], jnp.int32)
    for u in range(per_step):
        for c in range(0, width, length):
            events[pl.ds(starts[u], length), c : c + length] = x_refs[u][c : c + length, :]
        target = digits[u][1:2, :] * 256.0 + digits[u][2:3, :]
        wanted = jnp.where(place < lens[u], target.astype(jnp.int32), -1)
        line, turn = starts[u] // length + 1, lax.rem(starts[u], length)
        turned = pltpu.roll(wanted, turn, 1)
        packed_tgt[pl.ds(line, 1), :] = jnp.where(place >= turn, turned, packed_tgt[pl.ds(line, 1), :])
        packed_tgt[pl.ds(line + 1, 1), :] = jnp.where(
            place < turn, turned, packed_tgt[pl.ds(line + 1, 1), :]
        )
    events[pl.ds(end, tile), :] = jnp.zeros((tile, width), events.dtype)

    row = lax.broadcasted_iota(jnp.int32, (length, length), 0)
    col = lax.broadcasted_iota(jnp.int32, (length, length), 1)
    item_id = lax.broadcasted_iota(jnp.int32, (items, tile), 0)
    rate = logit_scale * math.log2(math.e)

    def one_tile(t, _):
        first = pl.multiple_of(t * tile, tile)
        x = events[pl.ds(first, tile), :].astype(jnp.float32)
        center, spread = center_and_spread(x)
        half_normed = (center * (0.5 * lax.rsqrt(spread + 1e-05))).astype(jnp.bfloat16)
        gate, values, query, keys = [
            half_silu(
                jnp.dot(
                    half_normed, w_in[:, part * width : (part + 1) * width],
                    preferred_element_type=jnp.float32,
                )
            ).astype(jnp.bfloat16)
            for part in range(4)
        ]
        key[pl.ds(first + length, tile), :] = keys
        value[pl.ds(first + length, tile), :] = values
        mixed = []
        for k in range(lines):
            base = pl.multiple_of(first + k * length, length)
            sources = pl.ds(base, 2 * length)
            start = starts_ref[pl.ds(base, length), :]
            ahead = packed_tgt[pl.ds(t * lines + k, 1), :] >= 0
            here = packed_tgt[pl.ds(t * lines + k + 1, 1), :] >= 0
            keep_ahead = (base - length + col >= start) & ahead
            keep_here = (col <= row) & (base + col >= start) & here
            keep = jnp.concatenate([keep_ahead, keep_here], axis=1)
            by_head = []
            for h in range(heads):
                cols = slice(h * hdim, (h + 1) * hdim)
                scores = lax.dot_general(
                    query[k * length : (k + 1) * length, cols], key[sources, cols], contract_last,
                    preferred_element_type=jnp.float32,
                )
                attn = half_silu(scores * (0.5 / math.sqrt(hdim)) + bias[h])
                attn = jnp.where(keep, attn, 0.0).astype(jnp.bfloat16)
                by_head.append(jnp.dot(attn, value[sources, cols], preferred_element_type=jnp.float32))
            mixed.append(jnp.concatenate(by_head, axis=1))
        center, spread = center_and_spread(jnp.concatenate(mixed, axis=0))
        normed = center * lax.rsqrt(spread + 1e-05)
        gated = (normed * gate.astype(jnp.float32)).astype(jnp.bfloat16)
        out = x + jnp.dot(gated, w_out[...], preferred_element_type=jnp.float32)
        out = out.astype(jnp.bfloat16).astype(jnp.float32)
        square = jnp.sum(out * out, axis=-1, keepdims=True)
        queries = (out * lax.rsqrt(square + 1e-06)).astype(jnp.bfloat16)

        target = jnp.concatenate(
            [packed_tgt[pl.ds(t * lines + k + 1, 1), :] for k in range(lines)], axis=1
        )
        total = jnp.zeros((1, tile), jnp.float32)
        target_dot = jnp.zeros((1, tile), jnp.float32)
        for j, block in enumerate(block_ids):
            dots = lax.dot_general(
                unit_refs[j][...], queries, contract_last, preferred_element_type=jnp.float32
            )
            exps = jnp.exp2(dots * rate - rate)
            exp_ref[j] = exps
            total += jnp.sum(exps, axis=0, keepdims=True)
            hit = item_id == target - block * items
            target_dot += jnp.sum(jnp.where(hit, dots, 0.0), axis=0, keepdims=True)
        loss = logit_scale + jnp.log(total) - logit_scale * target_dot
        for k in range(lines):
            packed_loss[pl.ds(t * lines + k, 1), :] = loss[:, k * length : (k + 1) * length]
        share = jnp.where(target >= 0, 1.0 / total, 0.0)
        for j, block in enumerate(block_ids):
            hit = item_id == target - block * items
            left = exp_ref[j] * share - jnp.where(hit, 1.0, 0.0)
            residual[j] = left.astype(jnp.bfloat16)
        for j in range(len(block_ids)):
            sums[j][...] += jnp.dot(residual[j], queries, preferred_element_type=jnp.float32)
        return 0

    lax.fori_loop(0, tiles, one_tile, 0)

    for u in range(per_step):
        line, turn = starts[u] // length, lax.rem(starts[u], length)
        back = lax.rem(length - turn, length)
        near = pltpu.roll(packed_loss[pl.ds(line, 1), :], back, 1)
        rest = pltpu.roll(packed_loss[pl.ds(line + 1, 1), :], back, 1)
        loss = jnp.where(place < length - turn, near, rest)
        loss_ref[pl.ds(spots[u], 1), :] = jnp.where(place < lens[u], loss, 0.0)


def users_call(ids, places, users, packed, units, w_in, w_out, rel_bias, carried, last):
    heads, length = rel_bias.shape
    width = w_out.shape[0]
    blocks = len(units)
    items = units[0].shape[0]
    rows = -(-min(len(places), 8) * length // tile) * tile
    lines = -(-(rows // length + 2) // 8) * 8
    whole = pl.BlockSpec(memory_space=pltpu.VMEM)
    arrays = [w_in, w_out, rel_bias, *packed, *units, *carried]
    narrow = lambda k: last and k >= blocks // 2
    return pl.pallas_call(
        functools.partial(users_kernel, places, blocks, not carried, last),
        in_specs=[pl.BlockSpec(memory_space=pltpu.SMEM)] + [whole] * len(arrays),
        out_specs=[whole] * (1 + blocks),
        scratch_shapes=[
            pltpu.VMEM((blocks // 2, items, width), jnp.float32),
            pltpu.VMEM((heads, length, 2 * length), jnp.float32),
            pltpu.VMEM((blocks, items, tile), jnp.float32),
            pltpu.VMEM((blocks, items, tile), jnp.bfloat16),
            pltpu.VMEM((rows + tile, width), jnp.bfloat16),
            pltpu.VMEM((rows + tile, length), jnp.int32),
            pltpu.VMEM((length + rows + tile, width), jnp.bfloat16),
            pltpu.VMEM((length + rows + tile, width), jnp.bfloat16),
            pltpu.VMEM((lines, length), jnp.int32),
            pltpu.VMEM((lines, length), jnp.float32),
        ],
        out_shape=[pltpu.VMEM((users, length), jnp.float32)]
        + [
            pltpu.VMEM((items, width), jnp.bfloat16 if narrow(k) else jnp.float32) for k in range(blocks)
        ],
        compiler_params=pltpu.CompilerParams(vmem_limit_bytes=24 * 1024 * 1024),
        name="users",
    )(ids, *[in_vmem(array) for array in arrays])


def shards(histories, lengths, targets, send_list, w_in, w_out, rel_bias, item_pool):
    user_count = histories.shape[0]
    groups = lax.axis_size("dp")
    slots = user_count // groups
    group, mine = lax.axis_index("dp").astype(jnp.int32), lax.axis_index("blk").astype(jnp.int32)

    work = sorted(
        ((shift, slot) for shift in range(groups) for slot in range(slots)),
        key=lambda pair: (pair[0] != 0, abs(pair[0] - groups / 2)),
    )
    *packed, unit = pack(
        histories, lengths, targets, send_list, item_pool, work, groups, group.reshape(1)
    )
    over_unit = swap(unit, "blk", 2)
    packed = [
        users if shift == 0 else from_behind(users, "dp", shift) for users, (shift, _) in zip(packed, work)
    ]
    units = [unit, over_unit, swap(unit, "blk", 1), swap(over_unit, "blk", 1)]

    pool_float = item_pool.astype(jnp.float32)
    item_norm = jnp.sqrt(jnp.sum(pool_float * pool_float, axis=-1, keepdims=True) + 1e-06)
    unit_rows = pool_float / item_norm

    came = [((group - shift) % groups) * slots + slot for shift, slot in work]
    ids = jnp.stack([mine, mine ^ 2, mine ^ 1, mine ^ 3, *came])
    half = user_count // 2
    order = tuple(range(user_count))
    carried = users_call(
        ids, order[:half], user_count, packed[:half], units, w_in, w_out, rel_bias, (), False
    )
    row_loss, own, over, side, far = users_call(
        ids, order[half:], user_count, packed[half:], units, w_in, w_out, rel_bias, carried, True
    )
    over = over + swap(far, "blk", 1).astype(jnp.float32)
    own = own + swap(side, "blk", 1).astype(jnp.float32)
    item_sum = logit_scale * (own + swap(over.astype(jnp.bfloat16), "blk", 2).astype(jnp.float32))
    pool_grad = (
        item_sum - unit_rows * jnp.sum(unit_rows * item_sum, axis=-1, keepdims=True)
    ) / item_norm
    return (row_loss, pool_grad)


def solution(mesh):
    placed = (
        P(("dp", "blk"), None, None),
        P(("dp", "blk")),
        P(("dp", "blk"), None),
        P(("dp", "blk")),
        P(),
        P(),
        P(),
        P(("dp", "blk"), None),
    )
    return jax.shard_map(
        shards,
        mesh=mesh,
        in_specs=placed,
        out_specs=(P(("dp", "blk"), None), P(("dp", "blk"), None)),
        check_vma=False,
    )
```

```python
import functools
import math

import jax
import jax.numpy as jnp
from jax import lax
from jax.experimental import pallas as pl
from jax.experimental.pallas import tpu as pltpu
from jax.sharding import PartitionSpec as P

logit_scale = 20.0
contract_last = (((1,), (1,)), ((), ()))
tile = 256
chunk = 16
number_rows = 8


def swap(array, axis, bit):
    devices = lax.axis_size(axis)
    return lax.ppermute(array, axis, [(i, i ^ bit) for i in range(devices)])


def in_vmem(array):
    return pltpu.with_memory_space_constraint(array, pltpu.VMEM)


def in_hbm(array):
    return pltpu.with_memory_space_constraint(array, pltpu.HBM)


def half_silu(half):
    return half + half * jnp.tanh(half)


def center_and_spread(values):
    center = values - jnp.mean(values, axis=-1, keepdims=True)
    return center, jnp.mean(center * center, axis=-1, keepdims=True)


def pack_kernel(
    group_ref, list_any, len_any, from_any, tgt_any, pool_any, to_any, own_any, unit_any,
    entries, lens, targets, pool, unit, buffer, sems, in_sems, out_sems, own_sems,
):
    users, length, width = from_any.shape
    pieces = width // length
    small = [
        pltpu.make_async_copy(source, target, sems.at[k])
        for k, (source, target) in enumerate(
            ((list_any, entries), (len_any, lens), (tgt_any, targets), (pool_any, pool))
        )
    ]
    for copy in small:
        copy.start()
    copies_in = [
        [
            pltpu.make_async_copy(
                from_any.at[u, :, pl.ds(c * length, length)],
                buffer.at[u, pl.ds(c * length, length)],
                in_sems.at[u, c],
            )
            for c in range(pieces)
        ]
        for u in range(users)
    ]
    for copies in copies_in:
        for copy in copies:
            copy.start()
    small[3].wait()
    rows = pool[...].astype(jnp.float32)
    unit[...] = (rows * lax.rsqrt(jnp.sum(rows * rows, axis=-1, keepdims=True) + 1e-06)).astype(jnp.bfloat16)
    unit_out = pltpu.make_async_copy(unit, unit_any, sems.at[4])
    unit_out.start()
    small[1].wait()
    small[2].wait()
    row = lax.broadcasted_iota(jnp.int32, (number_rows, length), 0)
    for u in range(users):
        target = targets[u : u + 1, :]
        numbers = jnp.where(row == 0, lens[u], jnp.where(row == 1, target // 256, target % 256))
        buffer[u, width:, :] = numbers.astype(jnp.float32).astype(jnp.bfloat16)
    small[0].wait()
    copies_out = []
    for k in range(users):
        user = entries[k]
        for c in range(pieces):
            pltpu.make_async_copy(
                from_any.at[user, :, pl.ds(c * length, length)],
                buffer.at[user, pl.ds(c * length, length)],
                in_sems.at[user, c],
            ).wait()
        copies_out.append(pltpu.make_async_copy(buffer.at[user], to_any.at[k], out_sems.at[k]))
        copies_out[k].start()
    own_slots = own_any.shape[0]
    copies_own = [
        pltpu.make_async_copy(
            buffer.at[entries[group_ref[0] * own_slots + k]], own_any.at[k], own_sems.at[k]
        )
        for k in range(own_slots)
    ]
    for copy in copies_own:
        copy.start()
    unit_out.wait()
    for copy in copies_out + copies_own:
        copy.wait()


def pack(histories, lengths, targets, entries, item_pool, group, own_slots):
    users, length, width = histories.shape
    shape = (users, width + number_rows, length)
    hbm = pl.BlockSpec(memory_space=pltpu.HBM)
    return pl.pallas_call(
        pack_kernel,
        in_specs=[pl.BlockSpec(memory_space=pltpu.SMEM)] + [hbm] * 5,
        out_specs=[hbm] * 3,
        scratch_shapes=[
            pltpu.SMEM(entries.shape, jnp.int32),
            pltpu.SMEM(lengths.shape, jnp.int32),
            pltpu.VMEM(targets.shape, jnp.int32),
            pltpu.VMEM(item_pool.shape, jnp.bfloat16),
            pltpu.VMEM(item_pool.shape, jnp.bfloat16),
            pltpu.VMEM(shape, jnp.bfloat16),
            pltpu.SemaphoreType.DMA((5,)),
            pltpu.SemaphoreType.DMA((users, width // length)),
            pltpu.SemaphoreType.DMA((users,)),
            pltpu.SemaphoreType.DMA((own_slots,)),
        ],
        out_shape=[
            pltpu.HBM(shape, jnp.bfloat16),
            pltpu.HBM((own_slots,) + shape[1:], jnp.bfloat16),
            pltpu.HBM(item_pool.shape, jnp.bfloat16),
        ],
        compiler_params=pltpu.CompilerParams(vmem_limit_bytes=16 * 1024 * 1024),
        name="pack",
    )(group, *[in_hbm(array) for array in (entries, lengths, histories, targets, item_pool)])


def users_kernel(blocks, own_slots, first, id_ref, x_ref, w_in, w_out, bias_in, *refs):
    count = x_ref.shape[0]
    unit_refs, refs = refs[:blocks], refs[blocks:]
    if not first:
        loss_in, sums_in, refs = refs[0], refs[1 : 1 + blocks], refs[1 + blocks :]
    loss_ref, out_refs, refs = refs[0], refs[1 : 1 + blocks], refs[1 + blocks :]
    wide_sums, bias, scratch = refs[0], refs[1], refs[2:]
    heads, length = bias_in.shape
    sums = [
        ref if ref.dtype == jnp.float32 else wide_sums.at[k - blocks // 2] for k, ref in enumerate(out_refs)
    ]
    loss_ref[...] = jnp.zeros_like(loss_ref) if first else loss_in[...]
    for k in range(blocks):
        sums[k][...] = jnp.zeros_like(sums[k]) if first else sums_in[k][...]
    for h in range(heads):
        wide = jnp.broadcast_to(0.5 * bias_in[h : h + 1, :], (length, length))
        turned = pltpu.roll(wide, 0, 1, stride=1, stride_axis=0).T
        bias[h] = jnp.concatenate([turned, turned], axis=1)
    own = id_ref[blocks]
    for at in range(0, count, 8):
        users = range(at, min(at + 8, count))
        users_step(
            [x_ref.at[u] for u in users],
            [own + u if first else u for u in users],
            [1 if first else jnp.where((u >= own) & (u < own + own_slots), 0, 1) for u in users],
            [id_ref[k] for k in range(blocks)], w_in, w_out, unit_refs, loss_ref, sums, bias, *scratch,
        )
    for k in range(blocks):
        if sums[k] is not out_refs[k]:
            out_refs[k][...] = sums[k][...].astype(out_refs[k].dtype)


def users_step(
    x_refs, spots, to_do, block_ids, w_in, w_out, unit_refs, loss_ref, sums, bias,
    exp_ref, residual, events, starts_ref, key, value, packed_tgt, packed_loss,
):
    heads, length, _ = bias.shape
    width = w_out.shape[0]
    hdim = width // heads
    items = unit_refs[0].shape[0]
    per_step = len(x_refs)

    digits = [ref[width:, :].astype(jnp.float32) for ref in x_refs]
    lens = [jnp.max(digit[:1, :]).astype(jnp.int32) * flag for digit, flag in zip(digits, to_do)]
    starts, end = [], 0
    for u in range(per_step):
        starts.append(pl.multiple_of(end, chunk) if u else 0)
        end = end + (lens[u] + chunk - 1) // chunk * chunk
    end = pl.multiple_of(end, chunk)
    strips = (end + length - 1) // length

    place = lax.broadcasted_iota(jnp.int32, (1, length), 1)
    packed_tgt[...] = jnp.full_like(packed_tgt, -1)
    key[:length, :] = jnp.zeros((length, width), key.dtype)
    value[:length, :] = jnp.zeros((length, width), value.dtype)
    for u in range(per_step):
        starts_ref[pl.ds(starts[u], length), :] = jnp.full((length, length), starts[u], jnp.int32)
    for u in range(per_step):
        for c in range(0, width, length):
            events[pl.ds(starts[u], length), c : c + length] = x_refs[u][c : c + length, :]
        target = digits[u][1:2, :] * 256.0 + digits[u][2:3, :]
        wanted = jnp.where(place < lens[u], target.astype(jnp.int32), -1)
        line, turn = starts[u] // length + 1, lax.rem(starts[u], length)
        turned = pltpu.roll(wanted, turn, 1)
        packed_tgt[pl.ds(line, 1), :] = jnp.where(place >= turn, turned, packed_tgt[pl.ds(line, 1), :])
        packed_tgt[pl.ds(line + 1, 1), :] = jnp.where(
            place < turn, turned, packed_tgt[pl.ds(line + 1, 1), :]
        )
    events[pl.ds(end, tile), :] = jnp.zeros((tile, width), events.dtype)

    row = lax.broadcasted_iota(jnp.int32, (length, length), 0)
    col = lax.broadcasted_iota(jnp.int32, (length, length), 1)
    rate = logit_scale * math.log2(math.e)

    def one_tile(strip, lines):
        tile = lines * length
        first = pl.multiple_of(strip * length, length)
        item_id = lax.broadcasted_iota(jnp.int32, (items, tile), 0)
        x = events[pl.ds(first, tile), :].astype(jnp.float32)
        center, spread = center_and_spread(x)
        half_normed = (center * (0.5 * lax.rsqrt(spread + 1e-05))).astype(jnp.bfloat16)
        gate, values, query, keys = [
            half_silu(
                jnp.dot(
                    half_normed, w_in[:, part * width : (part + 1) * width],
                    preferred_element_type=jnp.float32,
                )
            ).astype(jnp.bfloat16)
            for part in range(4)
        ]
        key[pl.ds(first + length, tile), :] = keys
        value[pl.ds(first + length, tile), :] = values
        mixed = []
        for k in range(lines):
            base = pl.multiple_of(first + k * length, length)
            sources = pl.ds(base, 2 * length)
            start = starts_ref[pl.ds(base, length), :]
            ahead = packed_tgt[pl.ds(strip + k, 1), :] >= 0
            here = packed_tgt[pl.ds(strip + k + 1, 1), :] >= 0
            keep_ahead = (base - length + col >= start) & ahead
            keep_here = (col <= row) & (base + col >= start) & here
            keep = jnp.concatenate([keep_ahead, keep_here], axis=1)
            by_head = []
            for h in range(heads):
                cols = slice(h * hdim, (h + 1) * hdim)
                scores = lax.dot_general(
                    query[k * length : (k + 1) * length, cols], key[sources, cols], contract_last,
                    preferred_element_type=jnp.float32,
                )
                attn = half_silu(scores * (0.5 / math.sqrt(hdim)) + bias[h])
                attn = jnp.where(keep, attn, 0.0).astype(jnp.bfloat16)
                by_head.append(jnp.dot(attn, value[sources, cols], preferred_element_type=jnp.float32))
            mixed.append(jnp.concatenate(by_head, axis=1))
        center, spread = center_and_spread(jnp.concatenate(mixed, axis=0))
        normed = center * lax.rsqrt(spread + 1e-05)
        gated = (normed * gate.astype(jnp.float32)).astype(jnp.bfloat16)
        out = x + jnp.dot(gated, w_out[...], preferred_element_type=jnp.float32)
        out = out.astype(jnp.bfloat16).astype(jnp.float32)
        square = jnp.sum(out * out, axis=-1, keepdims=True)
        queries = (out * lax.rsqrt(square + 1e-06)).astype(jnp.bfloat16)

        target = jnp.concatenate(
            [packed_tgt[pl.ds(strip + k + 1, 1), :] for k in range(lines)], axis=1
        )
        total = jnp.zeros((1, tile), jnp.float32)
        target_dot = jnp.zeros((1, tile), jnp.float32)
        for j, block in enumerate(block_ids):
            dots = lax.dot_general(
                unit_refs[j][...], queries, contract_last, preferred_element_type=jnp.float32
            )
            exps = jnp.exp2(dots * rate - rate)
            exp_ref[j, :, :tile] = exps
            total += jnp.sum(exps, axis=0, keepdims=True)
            hit = item_id == target - block * items
            target_dot += jnp.sum(jnp.where(hit, dots, 0.0), axis=0, keepdims=True)
        loss = logit_scale + jnp.log(total) - logit_scale * target_dot
        for k in range(lines):
            packed_loss[pl.ds(strip + k, 1), :] = loss[:, k * length : (k + 1) * length]
        share = jnp.where(target >= 0, 1.0 / total, 0.0)
        for j, block in enumerate(block_ids):
            hit = item_id == target - block * items
            left = exp_ref[j, :, :tile] * share - jnp.where(hit, 1.0, 0.0)
            residual[j, :, :tile] = left.astype(jnp.bfloat16)
        for j in range(len(block_ids)):
            sums[j][...] += jnp.dot(residual[j, :, :tile], queries, preferred_element_type=jnp.float32)

    def full_tile(t, _):
        one_tile(t * (tile // length), tile // length)
        return 0

    full = strips // (tile // length)
    lax.fori_loop(0, full, full_tile, 0)
    pl.when(strips % (tile // length) != 0)(lambda: one_tile(full * (tile // length), 1))

    for u in range(per_step):
        line, turn = starts[u] // length, lax.rem(starts[u], length)
        back = lax.rem(length - turn, length)
        near = pltpu.roll(packed_loss[pl.ds(line, 1), :], back, 1)
        rest = pltpu.roll(packed_loss[pl.ds(line + 1, 1), :], back, 1)
        loss = jnp.where(place < length - turn, near, rest)
        loss_ref[pl.ds(spots[u], 1), :] += jnp.where(place < lens[u], loss, 0.0)


def users_call(ids, users, packed, units, w_in, w_out, rel_bias, own_slots, carried):
    heads, length = rel_bias.shape
    width = w_out.shape[0]
    blocks = len(units)
    items = units[0].shape[0]
    rows = -(-min(packed.shape[0], 8) * length // tile) * tile
    lines = -(-(rows // length + 2) // 8) * 8
    whole = pl.BlockSpec(memory_space=pltpu.VMEM)
    arrays = [packed, w_in, w_out, rel_bias, *units, *carried]
    dtype_of = lambda k: jnp.bfloat16 if carried and k >= blocks // 2 else jnp.float32
    return pl.pallas_call(
        functools.partial(users_kernel, blocks, own_slots, not carried),
        in_specs=[pl.BlockSpec(memory_space=pltpu.SMEM)] + [whole] * len(arrays),
        out_specs=[whole] * (1 + blocks),
        scratch_shapes=[
            pltpu.VMEM((blocks // 2, items, width), jnp.float32),
            pltpu.VMEM((heads, length, 2 * length), jnp.float32),
            pltpu.VMEM((blocks, items, tile), jnp.float32),
            pltpu.VMEM((blocks, items, tile), jnp.bfloat16),
            pltpu.VMEM((rows + tile, width), jnp.bfloat16),
            pltpu.VMEM((rows + tile, length), jnp.int32),
            pltpu.VMEM((length + rows + tile, width), jnp.bfloat16),
            pltpu.VMEM((length + rows + tile, width), jnp.bfloat16),
            pltpu.VMEM((lines, length), jnp.int32),
            pltpu.VMEM((lines, length), jnp.float32),
        ],
        out_shape=[pltpu.VMEM((users, length), jnp.float32)]
        + [pltpu.VMEM((items, width), dtype_of(k)) for k in range(blocks)],
        compiler_params=pltpu.CompilerParams(vmem_limit_bytes=24 * 1024 * 1024),
        name="users",
    )(ids, *[in_vmem(array) for array in arrays])


def shards(histories, lengths, targets, send_list, w_in, w_out, rel_bias, item_pool):
    user_count = histories.shape[0]
    own_slots = user_count // lax.axis_size("dp")
    group, mine = lax.axis_index("dp").astype(jnp.int32), lax.axis_index("blk").astype(jnp.int32)
    packed, own_users, unit = pack(
        histories, lengths, targets, send_list, item_pool, group.reshape(1), own_slots
    )
    routed = lax.all_to_all(packed, "dp", split_axis=0, concat_axis=0, tiled=True)
    over_unit = swap(unit, "blk", 2)
    units = [unit, over_unit, swap(unit, "blk", 1), swap(over_unit, "blk", 1)]

    pool_float = item_pool.astype(jnp.float32)
    item_norm = jnp.sqrt(jnp.sum(pool_float * pool_float, axis=-1, keepdims=True) + 1e-06)
    unit_rows = pool_float / item_norm

    ids = jnp.stack([mine, mine ^ 2, mine ^ 1, mine ^ 3, group * own_slots])
    carried = users_call(ids, user_count, own_users, units, w_in, w_out, rel_bias, own_slots, ())
    row_loss, own, over, side, far = users_call(
        ids, user_count, routed, units, w_in, w_out, rel_bias, own_slots, carried
    )
    over = over + swap(far, "blk", 1).astype(jnp.float32)
    own = own + swap(side, "blk", 1).astype(jnp.float32)
    item_sum = logit_scale * (own + swap(over.astype(jnp.bfloat16), "blk", 2).astype(jnp.float32))
    pool_grad = (
        item_sum - unit_rows * jnp.sum(unit_rows * item_sum, axis=-1, keepdims=True)
    ) / item_norm
    return (row_loss, pool_grad)


def solution(mesh):
    placed = (
        P(("dp", "blk"), None, None),
        P(("dp", "blk")),
        P(("dp", "blk"), None),
        P(("dp", "blk")),
        P(),
        P(),
        P(),
        P(("dp", "blk"), None),
    )
    return jax.shard_map(
        shards,
        mesh=mesh,
        in_specs=placed,
        out_specs=(P(("dp", "blk"), None), P(("dp", "blk"), None)),
        check_vma=False,
    )
```

```python
import functools
import math

import jax
import jax.numpy as jnp
from jax import lax
from jax.experimental import pallas as pl
from jax.experimental.pallas import tpu as pltpu
from jax.sharding import PartitionSpec as P

logit_scale = 20.0
contract_last = (((1,), (1,)), ((), ()))
tile = 256
chunk = 16
number_rows = 8


def swap(array, axis, bit):
    devices = lax.axis_size(axis)
    return lax.ppermute(array, axis, [(i, i ^ bit) for i in range(devices)])


def from_behind(array, axis, by):
    devices = lax.axis_size(axis)
    return lax.ppermute(array, axis, [(i, (i + by) % devices) for i in range(devices)])


def in_vmem(array):
    return pltpu.with_memory_space_constraint(array, pltpu.VMEM)


def in_hbm(array):
    return pltpu.with_memory_space_constraint(array, pltpu.HBM)


def half_silu(half):
    return half + half * jnp.tanh(half)


def center_and_spread(values):
    center = values - jnp.mean(values, axis=-1, keepdims=True)
    return center, jnp.mean(center * center, axis=-1, keepdims=True)


def pack_kernel(
    work, groups, group_ref, list_any, len_any, from_any, tgt_any, pool_any, *refs,
):
    users = from_any.shape[0]
    to_refs, unit_any = refs[:users], refs[users]
    entries, lens, targets, pool, unit, buffer, sems, in_sems, out_sems = refs[users + 1 :]
    users, length, width = from_any.shape
    pieces = width // length
    small = [
        pltpu.make_async_copy(source, target, sems.at[k])
        for k, (source, target) in enumerate(
            ((list_any, entries), (len_any, lens), (tgt_any, targets), (pool_any, pool))
        )
    ]
    for copy in small:
        copy.start()
    copies_in = [
        [
            pltpu.make_async_copy(
                from_any.at[u, :, pl.ds(c * length, length)],
                buffer.at[u, pl.ds(c * length, length)],
                in_sems.at[u, c],
            )
            for c in range(pieces)
        ]
        for u in range(users)
    ]
    for copies in copies_in:
        for copy in copies:
            copy.start()
    small[3].wait()
    rows = pool[...].astype(jnp.float32)
    unit[...] = (rows * lax.rsqrt(jnp.sum(rows * rows, axis=-1, keepdims=True) + 1e-06)).astype(jnp.bfloat16)
    units_out = [
        pltpu.make_async_copy(unit, unit_any.at[k], sems.at[4 + k]) for k in range(unit_any.shape[0])
    ]
    for copy in units_out:
        copy.start()
    small[1].wait()
    small[2].wait()
    row = lax.broadcasted_iota(jnp.int32, (number_rows, length), 0)
    for u in range(users):
        target = targets[u : u + 1, :]
        numbers = jnp.where(row == 0, lens[u], jnp.where(row == 1, target // 256, target % 256))
        buffer[u, width:, :] = numbers.astype(jnp.float32).astype(jnp.bfloat16)
    small[0].wait()
    copies_out = []
    for k, (shift, slot) in enumerate(work):
        user = entries[(group_ref[0] + shift) % groups * (users // groups) + slot]
        for c in range(pieces):
            pltpu.make_async_copy(
                from_any.at[user, :, pl.ds(c * length, length)],
                buffer.at[user, pl.ds(c * length, length)],
                in_sems.at[user, c],
            ).wait()
        copies_out.append(pltpu.make_async_copy(buffer.at[user], to_refs[k], out_sems.at[k]))
        copies_out[k].start()
    for copy in units_out + copies_out:
        copy.wait()


def pack(histories, lengths, targets, entries, item_pool, work, groups, group, blocks):
    users, length, width = histories.shape
    shape = (users, width + number_rows, length)
    hbm = pl.BlockSpec(memory_space=pltpu.HBM)
    return pl.pallas_call(
        functools.partial(pack_kernel, work, groups),
        in_specs=[pl.BlockSpec(memory_space=pltpu.SMEM)] + [hbm] * 5,
        out_specs=[hbm] * (users + 1),
        scratch_shapes=[
            pltpu.SMEM(entries.shape, jnp.int32),
            pltpu.SMEM(lengths.shape, jnp.int32),
            pltpu.VMEM(targets.shape, jnp.int32),
            pltpu.VMEM(item_pool.shape, jnp.bfloat16),
            pltpu.VMEM(item_pool.shape, jnp.bfloat16),
            pltpu.VMEM(shape, jnp.bfloat16),
            pltpu.SemaphoreType.DMA((4 + blocks,)),
            pltpu.SemaphoreType.DMA((users, width // length)),
            pltpu.SemaphoreType.DMA((users,)),
        ],
        out_shape=[pltpu.HBM(shape[1:], jnp.bfloat16)] * users
        + [pltpu.HBM((blocks,) + item_pool.shape, jnp.bfloat16)],
        compiler_params=pltpu.CompilerParams(vmem_limit_bytes=16 * 1024 * 1024),
        name="pack",
    )(group, *[in_hbm(array) for array in (entries, lengths, histories, targets, item_pool)])


def users_kernel(places, blocks, id_ref, x_refs, w_in, w_out, unit_ref, sums, loss_ref, bias, scratch):
    count = len(places)
    units = [unit_ref.at[id_ref[k]] for k in range(blocks)]
    for at in range(0, count, 8):
        users_step(
            x_refs[at : at + 8], [id_ref[blocks + k] for k in places[at : at + 8]],
            [id_ref[k] for k in range(blocks)], w_in, w_out, units, loss_ref, sums, bias, *scratch,
        )


def first_kernel(
    places, blocks, own_count, id_ref, w_in_any, w_out_any, rel_any, unit_ref, *refs
):
    count = len(places)
    x_any, refs = refs[:count], refs[count:]
    loss_ref, sums, bias, refs = refs[0], refs[1 : 1 + blocks], refs[1 + blocks], refs[2 + blocks :]
    w_in, w_out, rel, own_x, sems = refs[:5]
    heads, length = rel.shape
    moves = [(rel_any, rel), (w_in_any, w_in), (w_out_any, w_out)]
    moves += [(x_any[k], own_x.at[k]) for k in range(own_count)]
    copies = [pltpu.make_async_copy(*move, sems.at[k]) for k, move in enumerate(moves)]
    for copy in copies:
        copy.start()
    loss_ref[...] = jnp.zeros_like(loss_ref)
    for ref in sums:
        ref[...] = jnp.zeros_like(ref)
    copies[0].wait()
    for h in range(heads):
        wide = jnp.broadcast_to(0.5 * rel[h : h + 1, :], (length, length))
        turned = pltpu.roll(wide, 0, 1, stride=1, stride_axis=0).T
        bias[h] = jnp.concatenate([turned, turned], axis=1)
    for copy in copies[1:]:
        copy.wait()
    x_refs = [own_x.at[k] for k in range(own_count)] + list(x_any[own_count:])
    users_kernel(places, blocks, id_ref, x_refs, w_in, w_out, unit_ref, sums, loss_ref, bias, refs[5:])


def second_kernel(places, blocks, id_ref, w_in, w_out, bias, unit_ref, loss_in, *refs):
    count = len(places)
    sums_in, x_refs, refs = refs[:blocks], refs[blocks : blocks + count], refs[blocks + count :]
    loss_ref, out_refs, wide_sums = refs[0], refs[1 : 1 + blocks], refs[1 + blocks]
    sums = [out_refs[k] if k < blocks // 2 else wide_sums.at[k - blocks // 2] for k in range(blocks)]
    loss_ref[...] = loss_in[...]
    for k in range(blocks):
        sums[k][...] = sums_in[k][...]
    users_kernel(
        places, blocks, id_ref, x_refs, w_in, w_out, unit_ref, sums, loss_ref, bias, refs[2 + blocks :]
    )
    for k in range(blocks // 2, blocks):
        out_refs[k][...] = sums[k][...].astype(out_refs[k].dtype)


def users_step(
    x_refs, spots, block_ids, w_in, w_out, unit_refs, loss_ref, sums, bias,
    exp_ref, residual, events, starts_ref, key, value, packed_tgt, packed_loss,
):
    heads, length, _ = bias.shape
    width = w_out.shape[0]
    hdim = width // heads
    items = unit_refs[0].shape[0]
    per_step = len(x_refs)

    digits = [ref[width:, :].astype(jnp.float32) for ref in x_refs]
    lens = [jnp.max(digit[:1, :]).astype(jnp.int32) for digit in digits]
    starts, end = [], 0
    for u in range(per_step):
        starts.append(pl.multiple_of(end, chunk) if u else 0)
        end = end + (lens[u] + chunk - 1) // chunk * chunk
    end = pl.multiple_of(end, chunk)
    strips = (end + length - 1) // length

    place = lax.broadcasted_iota(jnp.int32, (1, length), 1)
    packed_tgt[...] = jnp.full_like(packed_tgt, -1)
    key[:length, :] = jnp.zeros((length, width), key.dtype)
    value[:length, :] = jnp.zeros((length, width), value.dtype)
    for u in range(per_step):
        starts_ref[pl.ds(starts[u], length), :] = jnp.full((length, length), starts[u], jnp.int32)
    for u in range(per_step):
        for c in range(0, width, length):
            events[pl.ds(starts[u], length), c : c + length] = x_refs[u][c : c + length, :]
        target = digits[u][1:2, :] * 256.0 + digits[u][2:3, :]
        wanted = jnp.where(place < lens[u], target.astype(jnp.int32), -1)
        line, turn = starts[u] // length + 1, lax.rem(starts[u], length)
        turned = pltpu.roll(wanted, turn, 1)
        packed_tgt[pl.ds(line, 1), :] = jnp.where(place >= turn, turned, packed_tgt[pl.ds(line, 1), :])
        packed_tgt[pl.ds(line + 1, 1), :] = jnp.where(
            place < turn, turned, packed_tgt[pl.ds(line + 1, 1), :]
        )
    events[pl.ds(end, tile), :] = jnp.zeros((tile, width), events.dtype)

    row = lax.broadcasted_iota(jnp.int32, (length, length), 0)
    col = lax.broadcasted_iota(jnp.int32, (length, length), 1)
    rate = logit_scale * math.log2(math.e)

    def one_tile(strip, lines):
        tile = lines * length
        first = pl.multiple_of(strip * length, length)
        item_id = lax.broadcasted_iota(jnp.int32, (items, tile), 0)
        x = events[pl.ds(first, tile), :].astype(jnp.float32)
        center, spread = center_and_spread(x)
        half_normed = (center * (0.5 * lax.rsqrt(spread + 1e-05))).astype(jnp.bfloat16)
        gate, values, query, keys = [
            half_silu(
                jnp.dot(
                    half_normed, w_in[:, part * width : (part + 1) * width],
                    preferred_element_type=jnp.float32,
                )
            ).astype(jnp.bfloat16)
            for part in range(4)
        ]
        key[pl.ds(first + length, tile), :] = keys
        value[pl.ds(first + length, tile), :] = values
        mixed = []
        for k in range(lines):
            base = pl.multiple_of(first + k * length, length)
            sources = pl.ds(base, 2 * length)
            start = starts_ref[pl.ds(base, length), :]
            ahead = packed_tgt[pl.ds(strip + k, 1), :] >= 0
            here = packed_tgt[pl.ds(strip + k + 1, 1), :] >= 0
            keep_ahead = (base - length + col >= start) & ahead
            keep_here = (col <= row) & (base + col >= start) & here
            keep = jnp.concatenate([keep_ahead, keep_here], axis=1)
            by_head = []
            for h in range(heads):
                cols = slice(h * hdim, (h + 1) * hdim)
                scores = lax.dot_general(
                    query[k * length : (k + 1) * length, cols], key[sources, cols], contract_last,
                    preferred_element_type=jnp.float32,
                )
                attn = half_silu(scores * (0.5 / math.sqrt(hdim)) + bias[h])
                attn = jnp.where(keep, attn, 0.0).astype(jnp.bfloat16)
                by_head.append(jnp.dot(attn, value[sources, cols], preferred_element_type=jnp.float32))
            mixed.append(jnp.concatenate(by_head, axis=1))
        center, spread = center_and_spread(jnp.concatenate(mixed, axis=0))
        normed = center * lax.rsqrt(spread + 1e-05)
        gated = (normed * gate.astype(jnp.float32)).astype(jnp.bfloat16)
        out = x + jnp.dot(gated, w_out[...], preferred_element_type=jnp.float32)
        out = out.astype(jnp.bfloat16).astype(jnp.float32)
        square = jnp.sum(out * out, axis=-1, keepdims=True)
        queries = (out * lax.rsqrt(square + 1e-06)).astype(jnp.bfloat16)

        target = jnp.concatenate(
            [packed_tgt[pl.ds(strip + k + 1, 1), :] for k in range(lines)], axis=1
        )
        total = jnp.zeros((1, tile), jnp.float32)
        target_dot = jnp.zeros((1, tile), jnp.float32)
        for j, block in enumerate(block_ids):
            dots = lax.dot_general(
                unit_refs[j][...], queries, contract_last, preferred_element_type=jnp.float32
            )
            exps = jnp.exp2(dots * rate - rate)
            exp_ref[j, :, :tile] = exps
            total += jnp.sum(exps, axis=0, keepdims=True)
            hit = item_id == target - block * items
            target_dot += jnp.sum(jnp.where(hit, dots, 0.0), axis=0, keepdims=True)
        loss = logit_scale + jnp.log(total) - logit_scale * target_dot
        for k in range(lines):
            packed_loss[pl.ds(strip + k, 1), :] = loss[:, k * length : (k + 1) * length]
        share = jnp.where(target >= 0, 1.0 / total, 0.0)
        for j, block in enumerate(block_ids):
            hit = item_id == target - block * items
            left = exp_ref[j, :, :tile] * share - jnp.where(hit, 1.0, 0.0)
            residual[j, :, :tile] = left.astype(jnp.bfloat16)
        for j in range(len(block_ids)):
            sums[j][...] += jnp.dot(residual[j, :, :tile], queries, preferred_element_type=jnp.float32)

    def full_tile(t, _):
        one_tile(t * (tile // length), tile // length)
        return 0

    full = strips // (tile // length)
    lax.fori_loop(0, full, full_tile, 0)
    pl.when(strips % (tile // length) != 0)(lambda: one_tile(full * (tile // length), 1))

    for u in range(per_step):
        line, turn = starts[u] // length, lax.rem(starts[u], length)
        back = lax.rem(length - turn, length)
        near = pltpu.roll(packed_loss[pl.ds(line, 1), :], back, 1)
        rest = pltpu.roll(packed_loss[pl.ds(line + 1, 1), :], back, 1)
        loss = jnp.where(place < length - turn, near, rest)
        loss_ref[pl.ds(spots[u], 1), :] = jnp.where(place < lens[u], loss, 0.0)


def step_scratch(places, length, width, blocks, items):
    rows = -(-min(len(places), 8) * length // tile) * tile
    lines = -(-(rows // length + 2) // 8) * 8
    return [
        pltpu.VMEM((blocks, items, tile), jnp.float32),
        pltpu.VMEM((blocks, items, tile), jnp.bfloat16),
        pltpu.VMEM((rows + tile, width), jnp.bfloat16),
        pltpu.VMEM((rows + tile, length), jnp.int32),
        pltpu.VMEM((length + rows + tile, width), jnp.bfloat16),
        pltpu.VMEM((length + rows + tile, width), jnp.bfloat16),
        pltpu.VMEM((lines, length), jnp.int32),
        pltpu.VMEM((lines, length), jnp.float32),
    ]


scalars = pl.BlockSpec(memory_space=pltpu.SMEM)
whole = pl.BlockSpec(memory_space=pltpu.VMEM)
far_off = pl.BlockSpec(memory_space=pltpu.HBM)


def first_call(ids, places, own_count, users, packed, units, w_in, w_out, rel_bias):
    heads, length = rel_bias.shape
    width, (blocks, items, _) = w_out.shape[0], units.shape
    table = (heads, length, 2 * length)
    return pl.pallas_call(
        functools.partial(first_kernel, places, blocks, own_count),
        in_specs=[scalars] + [far_off] * 3 + [whole]
        + [far_off] * own_count + [whole] * (len(places) - own_count),
        out_specs=[whole] * (2 + blocks),
        scratch_shapes=[
            pltpu.VMEM(w_in.shape, jnp.bfloat16),
            pltpu.VMEM(w_out.shape, jnp.bfloat16),
            pltpu.VMEM(rel_bias.shape, jnp.float32),
            pltpu.VMEM((own_count,) + packed[0].shape, jnp.bfloat16),
            pltpu.SemaphoreType.DMA((3 + own_count,)),
        ]
        + step_scratch(places, length, width, blocks, items),
        out_shape=[pltpu.VMEM((users, length), jnp.float32)]
        + [pltpu.VMEM((items, width), jnp.float32)] * blocks
        + [pltpu.VMEM(table, jnp.float32)],
        compiler_params=pltpu.CompilerParams(vmem_limit_bytes=24 * 1024 * 1024),
        name="first_users",
    )(
        ids, *[in_hbm(array) for array in (w_in, w_out, rel_bias)], in_vmem(units),
        *[in_hbm(array) for array in packed[:own_count]], *[in_vmem(array) for array in packed[own_count:]],
    )


def second_call(ids, places, packed, units, w_in, w_out, loss, sums, bias):
    items, width = sums[0].shape
    length, blocks = bias.shape[1], len(sums)
    arrays = [w_in, w_out, bias, units, loss, *sums, *packed]
    return pl.pallas_call(
        functools.partial(second_kernel, places, blocks),
        in_specs=[scalars] + [whole] * len(arrays),
        out_specs=[whole] * (1 + blocks),
        scratch_shapes=[pltpu.VMEM((blocks - blocks // 2, items, width), jnp.float32)]
        + step_scratch(places, length, width, blocks, items),
        out_shape=[jax.ShapeDtypeStruct(loss.shape, jnp.float32)]
        + [
            pltpu.VMEM((items, width), jnp.float32 if k < blocks // 2 else jnp.bfloat16)
            for k in range(blocks)
        ],
        compiler_params=pltpu.CompilerParams(vmem_limit_bytes=24 * 1024 * 1024),
        name="second_users",
    )(ids, *[in_vmem(array) for array in arrays])


def shards(histories, lengths, targets, send_list, w_in, w_out, rel_bias, item_pool):
    user_count = histories.shape[0]
    groups, blocks = lax.axis_size("dp"), lax.axis_size("blk")
    slots = user_count // groups
    group, mine = lax.axis_index("dp").astype(jnp.int32), lax.axis_index("blk").astype(jnp.int32)

    work = sorted(
        ((shift, slot) for shift in range(groups) for slot in range(slots)),
        key=lambda pair: (pair[0] != 0, abs(pair[0] - groups / 2)),
    )
    *packed, units = pack(
        histories, lengths, targets, send_list, item_pool, work, groups, group.reshape(1), blocks
    )
    packed = [
        users if shift == 0 else from_behind(users, "dp", shift) for users, (shift, _) in zip(packed, work)
    ]
    units = lax.all_to_all(units, "blk", split_axis=0, concat_axis=0, tiled=True)

    pool_float = item_pool.astype(jnp.float32)
    item_norm = jnp.sqrt(jnp.sum(pool_float * pool_float, axis=-1, keepdims=True) + 1e-06)
    unit_rows = pool_float / item_norm

    came = [((group - shift) % groups) * slots + slot for shift, slot in work]
    ids = jnp.stack([mine, mine ^ 2, mine ^ 1, mine ^ 3, *came])
    half = user_count // 2
    order = tuple(range(user_count))
    loss, *sums, bias = first_call(
        ids, order[:half], slots, user_count, packed[:half], units, w_in, w_out, rel_bias
    )
    row_loss, own, over, side, far = second_call(
        ids, order[half:], packed[half:], units, w_in, w_out, loss, sums, bias
    )
    over = over + swap(far, "blk", 1).astype(jnp.float32)
    own = own + swap(side, "blk", 1).astype(jnp.float32)
    item_sum = logit_scale * (own + swap(over.astype(jnp.bfloat16), "blk", 2).astype(jnp.float32))
    pool_grad = (
        item_sum - unit_rows * jnp.sum(unit_rows * item_sum, axis=-1, keepdims=True)
    ) / item_norm
    return (row_loss, pool_grad)


def solution(mesh):
    placed = (
        P(("dp", "blk"), None, None),
        P(("dp", "blk")),
        P(("dp", "blk"), None),
        P(("dp", "blk")),
        P(),
        P(),
        P(),
        P(("dp", "blk"), None),
    )
    return jax.shard_map(
        shards,
        mesh=mesh,
        in_specs=placed,
        out_specs=(P(("dp", "blk"), None), P(("dp", "blk"), None)),
        check_vma=False,
    )
```

```python
import functools
import math

import jax
import jax.numpy as jnp
from jax import lax
from jax.experimental import pallas as pl
from jax.experimental.pallas import tpu as pltpu
from jax.sharding import PartitionSpec as P

logit_scale = 20.0
contract_last = (((1,), (1,)), ((), ()))
tile = 256
chunk = 16
number_rows = 8


def swap(array, axis, bit):
    devices = lax.axis_size(axis)
    return lax.ppermute(array, axis, [(i, i ^ bit) for i in range(devices)])


def from_behind(array, axis, by):
    devices = lax.axis_size(axis)
    return lax.ppermute(array, axis, [(i, (i + by) % devices) for i in range(devices)])


def in_vmem(array):
    return pltpu.with_memory_space_constraint(array, pltpu.VMEM)


def in_hbm(array):
    return pltpu.with_memory_space_constraint(array, pltpu.HBM)


def half_silu(half):
    return half + half * jnp.tanh(half)


def center_and_spread(values):
    center = values - jnp.mean(values, axis=-1, keepdims=True)
    return center, jnp.mean(center * center, axis=-1, keepdims=True)


def pack_kernel(
    work, groups, group_ref, list_any, len_any, from_any, tgt_any, pool_any, *refs,
):
    users, length, width = from_any.shape
    to_refs, unit_any = refs[:users], refs[users]
    entries, lens, targets, pool, unit, sems, in_sems = refs[users + 1 :]
    pieces = width // length
    small = [
        pltpu.make_async_copy(source, target, sems.at[k])
        for k, (source, target) in enumerate(
            ((list_any, entries), (len_any, lens), (tgt_any, targets), (pool_any, pool))
        )
    ]
    for copy in small:
        copy.start()
    small[0].wait()
    slots = users // groups
    order = [entries[(group_ref[0] + shift) % groups * slots + slot] for shift, slot in work]
    copies_in = [
        pltpu.make_async_copy(
            from_any.at[order[k], :, pl.ds(c * length, length)],
            to_refs[k].at[pl.ds(c * length, length)],
            in_sems.at[k, c],
        )
        for k in range(users)
        for c in range(pieces)
    ]
    for copy in copies_in:
        copy.start()
    small[3].wait()
    rows = pool[...].astype(jnp.float32)
    unit[...] = (rows * lax.rsqrt(jnp.sum(rows * rows, axis=-1, keepdims=True) + 1e-06)).astype(jnp.bfloat16)
    units_out = [
        pltpu.make_async_copy(unit, unit_any.at[k], sems.at[4 + k]) for k in range(unit_any.shape[0])
    ]
    for copy in units_out:
        copy.start()
    small[1].wait()
    small[2].wait()
    row = lax.broadcasted_iota(jnp.int32, (number_rows, length), 0)
    for k in range(users):
        target = targets[pl.ds(order[k], 1), :]
        numbers = jnp.where(row == 0, lens[order[k]], jnp.where(row == 1, target // 256, target % 256))
        to_refs[k][width:, :] = numbers.astype(jnp.float32).astype(jnp.bfloat16)
    for copy in copies_in + units_out:
        copy.wait()


def pack(histories, lengths, targets, entries, item_pool, work, groups, group, blocks):
    users, length, width = histories.shape
    shape = (width + number_rows, length)
    hbm = pl.BlockSpec(memory_space=pltpu.HBM)
    return pl.pallas_call(
        functools.partial(pack_kernel, work, groups),
        in_specs=[pl.BlockSpec(memory_space=pltpu.SMEM)] + [hbm] * 5,
        out_specs=[pl.BlockSpec(memory_space=pltpu.VMEM)] * users + [hbm],
        scratch_shapes=[
            pltpu.SMEM(entries.shape, jnp.int32),
            pltpu.SMEM(lengths.shape, jnp.int32),
            pltpu.VMEM(targets.shape, jnp.int32),
            pltpu.VMEM(item_pool.shape, jnp.bfloat16),
            pltpu.VMEM(item_pool.shape, jnp.bfloat16),
            pltpu.SemaphoreType.DMA((4 + blocks,)),
            pltpu.SemaphoreType.DMA((users, width // length)),
        ],
        out_shape=[pltpu.VMEM(shape, jnp.bfloat16)] * users
        + [pltpu.HBM((blocks,) + item_pool.shape, jnp.bfloat16)],
        compiler_params=pltpu.CompilerParams(vmem_limit_bytes=16 * 1024 * 1024),
        name="pack",
    )(group, *[in_hbm(array) for array in (entries, lengths, histories, targets, item_pool)])


def users_kernel(places, blocks, id_ref, x_refs, w_in, w_out, unit_ref, sums, loss_ref, bias, scratch):
    count = len(places)
    units = [unit_ref.at[id_ref[k]] for k in range(blocks)]
    for at in range(0, count, 8):
        users_step(
            x_refs[at : at + 8], [id_ref[blocks + k] for k in places[at : at + 8]],
            [id_ref[k] for k in range(blocks)], w_in, w_out, units, loss_ref, sums, bias, *scratch,
        )


def first_kernel(
    places, blocks, id_ref, w_in_any, w_out_any, rel_any, unit_ref, *refs
):
    count = len(places)
    x_refs, refs = refs[:count], refs[count:]
    loss_ref, sums, bias, refs = refs[0], refs[1 : 1 + blocks], refs[1 + blocks], refs[2 + blocks :]
    w_in, w_out, rel, sems = refs[:4]
    heads, length = rel.shape
    moves = [(rel_any, rel), (w_in_any, w_in), (w_out_any, w_out)]
    copies = [pltpu.make_async_copy(*move, sems.at[k]) for k, move in enumerate(moves)]
    for copy in copies:
        copy.start()
    loss_ref[...] = jnp.zeros_like(loss_ref)
    for ref in sums:
        ref[...] = jnp.zeros_like(ref)
    copies[0].wait()
    for h in range(heads):
        wide = jnp.broadcast_to(0.5 * rel[h : h + 1, :], (length, length))
        turned = pltpu.roll(wide, 0, 1, stride=1, stride_axis=0).T
        bias[h] = jnp.concatenate([turned, turned], axis=1)
    for copy in copies[1:]:
        copy.wait()
    users_kernel(places, blocks, id_ref, x_refs, w_in, w_out, unit_ref, sums, loss_ref, bias, refs[4:])


def second_kernel(places, blocks, id_ref, w_in, w_out, bias, unit_ref, loss_in, *refs):
    count = len(places)
    sums_in, x_refs, refs = refs[:blocks], refs[blocks : blocks + count], refs[blocks + count :]
    loss_ref, out_refs, wide_sums = refs[0], refs[1 : 1 + blocks], refs[1 + blocks]
    sums = [out_refs[k] if k < blocks // 2 else wide_sums.at[k - blocks // 2] for k in range(blocks)]
    loss_ref[...] = loss_in[...]
    for k in range(blocks):
        sums[k][...] = sums_in[k][...]
    users_kernel(
        places, blocks, id_ref, x_refs, w_in, w_out, unit_ref, sums, loss_ref, bias, refs[2 + blocks :]
    )
    for k in range(blocks // 2, blocks):
        out_refs[k][...] = sums[k][...].astype(out_refs[k].dtype)


def users_step(
    x_refs, spots, block_ids, w_in, w_out, unit_refs, loss_ref, sums, bias,
    exp_ref, residual, events, starts_ref, key, value, packed_tgt, packed_loss,
):
    heads, length, _ = bias.shape
    width = w_out.shape[0]
    hdim = width // heads
    items = unit_refs[0].shape[0]
    per_step = len(x_refs)

    digits = [ref[width:, :].astype(jnp.float32) for ref in x_refs]
    lens = [jnp.max(digit[:1, :]).astype(jnp.int32) for digit in digits]
    starts, end = [], 0
    for u in range(per_step):
        starts.append(pl.multiple_of(end, chunk) if u else 0)
        end = end + (lens[u] + chunk - 1) // chunk * chunk
    end = pl.multiple_of(end, chunk)
    strips = (end + length - 1) // length

    place = lax.broadcasted_iota(jnp.int32, (1, length), 1)
    packed_tgt[...] = jnp.full_like(packed_tgt, -1)
    key[:length, :] = jnp.zeros((length, width), key.dtype)
    value[:length, :] = jnp.zeros((length, width), value.dtype)
    for u in range(per_step):
        starts_ref[pl.ds(starts[u], length), :] = jnp.full((length, length), starts[u], jnp.int32)
    for u in range(per_step):
        for c in range(0, width, length):
            events[pl.ds(starts[u], length), c : c + length] = x_refs[u][c : c + length, :]
        target = digits[u][1:2, :] * 256.0 + digits[u][2:3, :]
        wanted = jnp.where(place < lens[u], target.astype(jnp.int32), -1)
        line, turn = starts[u] // length + 1, lax.rem(starts[u], length)
        turned = pltpu.roll(wanted, turn, 1)
        packed_tgt[pl.ds(line, 1), :] = jnp.where(place >= turn, turned, packed_tgt[pl.ds(line, 1), :])
        packed_tgt[pl.ds(line + 1, 1), :] = jnp.where(
            place < turn, turned, packed_tgt[pl.ds(line + 1, 1), :]
        )
    events[pl.ds(end, tile), :] = jnp.zeros((tile, width), events.dtype)

    row = lax.broadcasted_iota(jnp.int32, (length, length), 0)
    col = lax.broadcasted_iota(jnp.int32, (length, length), 1)
    rate = logit_scale * math.log2(math.e)

    def one_tile(strip, lines):
        tile = lines * length
        first = pl.multiple_of(strip * length, length)
        item_id = lax.broadcasted_iota(jnp.int32, (items, tile), 0)
        x = events[pl.ds(first, tile), :].astype(jnp.float32)
        center, spread = center_and_spread(x)
        half_normed = (center * (0.5 * lax.rsqrt(spread + 1e-05))).astype(jnp.bfloat16)
        gate, values, query, keys = [
            half_silu(
                jnp.dot(
                    half_normed, w_in[:, part * width : (part + 1) * width],
                    preferred_element_type=jnp.float32,
                )
            ).astype(jnp.bfloat16)
            for part in range(4)
        ]
        key[pl.ds(first + length, tile), :] = keys
        value[pl.ds(first + length, tile), :] = values
        mixed = []
        for k in range(lines):
            base = pl.multiple_of(first + k * length, length)
            sources = pl.ds(base, 2 * length)
            start = starts_ref[pl.ds(base, length), :]
            ahead = packed_tgt[pl.ds(strip + k, 1), :] >= 0
            here = packed_tgt[pl.ds(strip + k + 1, 1), :] >= 0
            keep_ahead = (base - length + col >= start) & ahead
            keep_here = (col <= row) & (base + col >= start) & here
            keep = jnp.concatenate([keep_ahead, keep_here], axis=1)
            by_head = []
            for h in range(heads):
                cols = slice(h * hdim, (h + 1) * hdim)
                scores = lax.dot_general(
                    query[k * length : (k + 1) * length, cols], key[sources, cols], contract_last,
                    preferred_element_type=jnp.float32,
                )
                attn = half_silu(scores * (0.5 / math.sqrt(hdim)) + bias[h])
                attn = jnp.where(keep, attn, 0.0).astype(jnp.bfloat16)
                by_head.append(jnp.dot(attn, value[sources, cols], preferred_element_type=jnp.float32))
            mixed.append(jnp.concatenate(by_head, axis=1))
        center, spread = center_and_spread(jnp.concatenate(mixed, axis=0))
        normed = center * lax.rsqrt(spread + 1e-05)
        gated = (normed * gate.astype(jnp.float32)).astype(jnp.bfloat16)
        out = x + jnp.dot(gated, w_out[...], preferred_element_type=jnp.float32)
        out = out.astype(jnp.bfloat16).astype(jnp.float32)
        square = jnp.sum(out * out, axis=-1, keepdims=True)
        queries = (out * lax.rsqrt(square + 1e-06)).astype(jnp.bfloat16)

        target = jnp.concatenate(
            [packed_tgt[pl.ds(strip + k + 1, 1), :] for k in range(lines)], axis=1
        )
        total = jnp.zeros((1, tile), jnp.float32)
        target_dot = jnp.zeros((1, tile), jnp.float32)
        for j, block in enumerate(block_ids):
            dots = lax.dot_general(
                unit_refs[j][...], queries, contract_last, preferred_element_type=jnp.float32
            )
            exps = jnp.exp2(dots * rate - rate)
            exp_ref[j, :, :tile] = exps
            total += jnp.sum(exps, axis=0, keepdims=True)
            hit = item_id == target - block * items
            target_dot += jnp.sum(jnp.where(hit, dots, 0.0), axis=0, keepdims=True)
        loss = logit_scale + jnp.log(total) - logit_scale * target_dot
        for k in range(lines):
            packed_loss[pl.ds(strip + k, 1), :] = loss[:, k * length : (k + 1) * length]
        share = jnp.where(target >= 0, 1.0 / total, 0.0)
        for j, block in enumerate(block_ids):
            hit = item_id == target - block * items
            left = exp_ref[j, :, :tile] * share - jnp.where(hit, 1.0, 0.0)
            residual[j, :, :tile] = left.astype(jnp.bfloat16)
        for j in range(len(block_ids)):
            sums[j][...] += jnp.dot(residual[j, :, :tile], queries, preferred_element_type=jnp.float32)

    def full_tile(t, _):
        one_tile(t * (tile // length), tile // length)
        return 0

    full = strips // (tile // length)
    lax.fori_loop(0, full, full_tile, 0)
    pl.when(strips % (tile // length) != 0)(lambda: one_tile(full * (tile // length), 1))

    for u in range(per_step):
        line, turn = starts[u] // length, lax.rem(starts[u], length)
        back = lax.rem(length - turn, length)
        near = pltpu.roll(packed_loss[pl.ds(line, 1), :], back, 1)
        rest = pltpu.roll(packed_loss[pl.ds(line + 1, 1), :], back, 1)
        loss = jnp.where(place < length - turn, near, rest)
        loss_ref[pl.ds(spots[u], 1), :] = jnp.where(place < lens[u], loss, 0.0)


def step_scratch(places, length, width, blocks, items):
    rows = -(-min(len(places), 8) * length // tile) * tile
    lines = -(-(rows // length + 2) // 8) * 8
    return [
        pltpu.VMEM((blocks, items, tile), jnp.float32),
        pltpu.VMEM((blocks, items, tile), jnp.bfloat16),
        pltpu.VMEM((rows + tile, width), jnp.bfloat16),
        pltpu.VMEM((rows + tile, length), jnp.int32),
        pltpu.VMEM((length + rows + tile, width), jnp.bfloat16),
        pltpu.VMEM((length + rows + tile, width), jnp.bfloat16),
        pltpu.VMEM((lines, length), jnp.int32),
        pltpu.VMEM((lines, length), jnp.float32),
    ]


scalars = pl.BlockSpec(memory_space=pltpu.SMEM)
whole = pl.BlockSpec(memory_space=pltpu.VMEM)
far_off = pl.BlockSpec(memory_space=pltpu.HBM)


def first_call(ids, places, users, packed, units, w_in, w_out, rel_bias):
    heads, length = rel_bias.shape
    width, (blocks, items, _) = w_out.shape[0], units.shape
    table = (heads, length, 2 * length)
    return pl.pallas_call(
        functools.partial(first_kernel, places, blocks),
        in_specs=[scalars] + [far_off] * 3 + [whole] * (1 + len(places)),
        out_specs=[whole] * (2 + blocks),
        scratch_shapes=[
            pltpu.VMEM(w_in.shape, jnp.bfloat16),
            pltpu.VMEM(w_out.shape, jnp.bfloat16),
            pltpu.VMEM(rel_bias.shape, jnp.float32),
            pltpu.SemaphoreType.DMA((3,)),
        ]
        + step_scratch(places, length, width, blocks, items),
        out_shape=[pltpu.VMEM((users, length), jnp.float32)]
        + [pltpu.VMEM((items, width), jnp.float32)] * blocks
        + [pltpu.VMEM(table, jnp.float32)],
        compiler_params=pltpu.CompilerParams(vmem_limit_bytes=24 * 1024 * 1024),
        name="first_users",
    )(
        ids, *[in_hbm(array) for array in (w_in, w_out, rel_bias)], in_vmem(units),
        *[in_vmem(array) for array in packed],
    )


def second_call(ids, places, packed, units, w_in, w_out, loss, sums, bias):
    items, width = sums[0].shape
    length, blocks = bias.shape[1], len(sums)
    arrays = [w_in, w_out, bias, units, loss, *sums, *packed]
    return pl.pallas_call(
        functools.partial(second_kernel, places, blocks),
        in_specs=[scalars] + [whole] * len(arrays),
        out_specs=[whole] * (1 + blocks),
        scratch_shapes=[pltpu.VMEM((blocks - blocks // 2, items, width), jnp.float32)]
        + step_scratch(places, length, width, blocks, items),
        out_shape=[jax.ShapeDtypeStruct(loss.shape, jnp.float32)]
        + [
            pltpu.VMEM((items, width), jnp.float32 if k < blocks // 2 else jnp.bfloat16)
            for k in range(blocks)
        ],
        compiler_params=pltpu.CompilerParams(vmem_limit_bytes=24 * 1024 * 1024),
        name="second_users",
    )(ids, *[in_vmem(array) for array in arrays])


def shards(histories, lengths, targets, send_list, w_in, w_out, rel_bias, item_pool):
    user_count = histories.shape[0]
    groups, blocks = lax.axis_size("dp"), lax.axis_size("blk")
    slots = user_count // groups
    group, mine = lax.axis_index("dp").astype(jnp.int32), lax.axis_index("blk").astype(jnp.int32)

    by_distance = sorted(range(1, groups), key=lambda shift: abs(shift - groups / 2))
    early = [groups - by_distance[-1], *by_distance[: groups // 2 - 2]]
    late = [shift for shift in by_distance if shift not in early]
    work = [(shift, slot) for shift in [0, *early, *late] for slot in range(slots)]
    *packed, units = pack(
        histories, lengths, targets, send_list, item_pool, work, groups, group.reshape(1), blocks
    )
    half = user_count // 2
    for k in range(slots, user_count):
        if k >= half:
            before = slots * (1 if work[k][0] == late[1] else 2)
            packed[before], packed[k] = lax.optimization_barrier((packed[before], packed[k]))
        packed[k] = from_behind(packed[k], "dp", work[k][0])
    units = lax.all_to_all(units, "blk", split_axis=0, concat_axis=0, tiled=True)

    pool_float = item_pool.astype(jnp.float32)
    item_norm = jnp.sqrt(jnp.sum(pool_float * pool_float, axis=-1, keepdims=True) + 1e-06)
    unit_rows = pool_float / item_norm

    came = [((group - shift) % groups) * slots + slot for shift, slot in work]
    ids = jnp.stack([mine, mine ^ 2, mine ^ 1, mine ^ 3, *came])
    order = tuple(range(user_count))
    loss, *sums, bias = first_call(
        ids, order[:half], user_count, packed[:half], units, w_in, w_out, rel_bias
    )
    row_loss, own, over, side, far = second_call(
        ids, order[half:], packed[half:], units, w_in, w_out, loss, sums, bias
    )
    over = over + swap(far, "blk", 1).astype(jnp.float32)
    own = own + swap(side, "blk", 1).astype(jnp.float32)
    item_sum = logit_scale * (own + swap(over.astype(jnp.bfloat16), "blk", 2).astype(jnp.float32))
    pool_grad = (
        item_sum - unit_rows * jnp.sum(unit_rows * item_sum, axis=-1, keepdims=True)
    ) / item_norm
    return (row_loss, pool_grad)


def solution(mesh):
    placed = (
        P(("dp", "blk"), None, None),
        P(("dp", "blk")),
        P(("dp", "blk"), None),
        P(("dp", "blk")),
        P(),
        P(),
        P(),
        P(("dp", "blk"), None),
    )
    return jax.shard_map(
        shards,
        mesh=mesh,
        in_specs=placed,
        out_specs=(P(("dp", "blk"), None), P(("dp", "blk"), None)),
        check_vma=False,
    )
```

```python
import functools
import math

import jax
import jax.numpy as jnp
from jax import lax
from jax.experimental import pallas as pl
from jax.experimental.pallas import tpu as pltpu
from jax.sharding import PartitionSpec as P

logit_scale = 20.0
contract_last = (((1,), (1,)), ((), ()))
tile = 256
chunk = 16
number_rows = 8


def swap(array, axis, bit):
    devices = lax.axis_size(axis)
    return lax.ppermute(array, axis, [(i, i ^ bit) for i in range(devices)])


def from_behind(array, axis, by):
    devices = lax.axis_size(axis)
    return lax.ppermute(array, axis, [(i, (i + by) % devices) for i in range(devices)])


def in_vmem(array):
    return pltpu.with_memory_space_constraint(array, pltpu.VMEM)


def in_hbm(array):
    return pltpu.with_memory_space_constraint(array, pltpu.HBM)


def half_silu(half):
    return half + half * jnp.tanh(half)


def center_and_spread(values):
    center = values - jnp.mean(values, axis=-1, keepdims=True)
    return center, jnp.mean(center * center, axis=-1, keepdims=True)


def pack_kernel(
    work, groups, group_ref, list_any, len_any, from_any, tgt_any, pool_any, *refs,
):
    users, length, width = from_any.shape
    to_refs, unit_any = refs[:users], refs[users]
    entries, lens, targets, pool, unit, sems, in_sems = refs[users + 1 :]
    pieces = width // length
    small = [
        pltpu.make_async_copy(source, target, sems.at[k])
        for k, (source, target) in enumerate(
            ((list_any, entries), (len_any, lens), (tgt_any, targets), (pool_any, pool))
        )
    ]
    for copy in small:
        copy.start()
    small[0].wait()
    slots = users // groups
    order = [entries[(group_ref[0] + shift) % groups * slots + slot] for shift, slot in work]
    copies_in = [
        pltpu.make_async_copy(
            from_any.at[order[k], :, pl.ds(c * length, length)],
            to_refs[k].at[pl.ds(c * length, length)],
            in_sems.at[k, c],
        )
        for k in range(users)
        for c in range(pieces)
    ]
    for copy in copies_in:
        copy.start()
    small[3].wait()
    rows = pool[...].astype(jnp.float32)
    unit[...] = (rows * lax.rsqrt(jnp.sum(rows * rows, axis=-1, keepdims=True) + 1e-06)).astype(jnp.bfloat16)
    units_out = [
        pltpu.make_async_copy(unit, unit_any.at[k], sems.at[4 + k]) for k in range(unit_any.shape[0])
    ]
    for copy in units_out:
        copy.start()
    small[1].wait()
    small[2].wait()
    row = lax.broadcasted_iota(jnp.int32, (number_rows, length), 0)
    for k in range(users):
        target = targets[pl.ds(order[k], 1), :]
        numbers = jnp.where(row == 0, lens[order[k]], jnp.where(row == 1, target // 256, target % 256))
        to_refs[k][width:, :] = numbers.astype(jnp.float32).astype(jnp.bfloat16)
    for copy in copies_in + units_out:
        copy.wait()


def pack(histories, lengths, targets, entries, item_pool, work, groups, group, blocks):
    users, length, width = histories.shape
    shape = (width + number_rows, length)
    hbm = pl.BlockSpec(memory_space=pltpu.HBM)
    return pl.pallas_call(
        functools.partial(pack_kernel, work, groups),
        in_specs=[pl.BlockSpec(memory_space=pltpu.SMEM)] + [hbm] * 5,
        out_specs=[pl.BlockSpec(memory_space=pltpu.VMEM)] * users + [hbm],
        scratch_shapes=[
            pltpu.SMEM(entries.shape, jnp.int32),
            pltpu.SMEM(lengths.shape, jnp.int32),
            pltpu.VMEM(targets.shape, jnp.int32),
            pltpu.VMEM(item_pool.shape, jnp.bfloat16),
            pltpu.VMEM(item_pool.shape, jnp.bfloat16),
            pltpu.SemaphoreType.DMA((4 + blocks,)),
            pltpu.SemaphoreType.DMA((users, width // length)),
        ],
        out_shape=[pltpu.VMEM(shape, jnp.bfloat16)] * users
        + [pltpu.HBM((blocks,) + item_pool.shape, jnp.bfloat16)],
        compiler_params=pltpu.CompilerParams(vmem_limit_bytes=16 * 1024 * 1024),
        name="pack",
    )(group, *[in_hbm(array) for array in (entries, lengths, histories, targets, item_pool)])


def users_kernel(places, blocks, id_ref, x_refs, w_in, w_out, unit_ref, sums, loss_ref, bias, scratch):
    count = len(places)
    units = [unit_ref.at[id_ref[k]] for k in range(blocks)]
    for at in range(0, count, 8):
        users_step(
            x_refs[at : at + 8], [id_ref[blocks + k] for k in places[at : at + 8]],
            [id_ref[k] for k in range(blocks)], w_in, w_out, units, loss_ref, sums, bias, *scratch,
        )


def load_kernel(w_in_any, w_out_any, rel, w_in, w_out, bias, sems):
    copies = [
        pltpu.make_async_copy(w_in_any, w_in, sems.at[0]),
        pltpu.make_async_copy(w_out_any, w_out, sems.at[1]),
    ]
    for copy in copies:
        copy.start()
    heads, length = rel.shape
    for h in range(heads):
        wide = jnp.broadcast_to(0.5 * rel[h : h + 1, :], (length, length))
        turned = pltpu.roll(wide, 0, 1, stride=1, stride_axis=0).T
        bias[h] = jnp.concatenate([turned, turned], axis=1)
    for copy in copies:
        copy.wait()


def first_kernel(places, blocks, id_ref, w_in, w_out, bias, unit_ref, *refs):
    count = len(places)
    x_refs, refs = refs[:count], refs[count:]
    loss_ref, sums, scratch = refs[0], refs[1 : 1 + blocks], refs[1 + blocks :]
    loss_ref[...] = jnp.zeros_like(loss_ref)
    for ref in sums:
        ref[...] = jnp.zeros_like(ref)
    users_kernel(places, blocks, id_ref, x_refs, w_in, w_out, unit_ref, sums, loss_ref, bias, scratch)


def second_kernel(places, blocks, id_ref, w_in, w_out, bias, unit_ref, loss_in, *refs):
    count = len(places)
    sums_in, x_refs, refs = refs[:blocks], refs[blocks : blocks + count], refs[blocks + count :]
    loss_ref, out_refs, wide_sums = refs[0], refs[1 : 1 + blocks], refs[1 + blocks]
    sums = [out_refs[k] if k < blocks // 2 else wide_sums.at[k - blocks // 2] for k in range(blocks)]
    loss_ref[...] = loss_in[...]
    for k in range(blocks):
        sums[k][...] = sums_in[k][...]
    users_kernel(
        places, blocks, id_ref, x_refs, w_in, w_out, unit_ref, sums, loss_ref, bias, refs[2 + blocks :]
    )
    for k in range(blocks // 2, blocks):
        out_refs[k][...] = sums[k][...].astype(out_refs[k].dtype)


def users_step(
    x_refs, spots, block_ids, w_in, w_out, unit_refs, loss_ref, sums, bias,
    exp_ref, residual, events, starts_ref, key, value, packed_tgt, packed_loss,
):
    heads, length, _ = bias.shape
    width = w_out.shape[0]
    hdim = width // heads
    items = unit_refs[0].shape[0]
    per_step = len(x_refs)

    digits = [ref[width:, :].astype(jnp.float32) for ref in x_refs]
    lens = [jnp.max(digit[:1, :]).astype(jnp.int32) for digit in digits]
    starts, end = [], 0
    for u in range(per_step):
        starts.append(pl.multiple_of(end, chunk) if u else 0)
        end = end + (lens[u] + chunk - 1) // chunk * chunk
    end = pl.multiple_of(end, chunk)
    strips = (end + length - 1) // length

    place = lax.broadcasted_iota(jnp.int32, (1, length), 1)
    packed_tgt[...] = jnp.full_like(packed_tgt, -1)
    key[:length, :] = jnp.zeros((length, width), key.dtype)
    value[:length, :] = jnp.zeros((length, width), value.dtype)
    for u in range(per_step):
        starts_ref[pl.ds(starts[u], length), :] = jnp.full((length, length), starts[u], jnp.int32)
    for u in range(per_step):
        for c in range(0, width, length):
            events[pl.ds(starts[u], length), c : c + length] = x_refs[u][c : c + length, :]
        target = digits[u][1:2, :] * 256.0 + digits[u][2:3, :]
        wanted = jnp.where(place < lens[u], target.astype(jnp.int32), -1)
        line, turn = starts[u] // length + 1, lax.rem(starts[u], length)
        turned = pltpu.roll(wanted, turn, 1)
        packed_tgt[pl.ds(line, 1), :] = jnp.where(place >= turn, turned, packed_tgt[pl.ds(line, 1), :])
        packed_tgt[pl.ds(line + 1, 1), :] = jnp.where(
            place < turn, turned, packed_tgt[pl.ds(line + 1, 1), :]
        )
    events[pl.ds(end, tile), :] = jnp.zeros((tile, width), events.dtype)

    row = lax.broadcasted_iota(jnp.int32, (length, length), 0)
    col = lax.broadcasted_iota(jnp.int32, (length, length), 1)
    rate = logit_scale * math.log2(math.e)

    def one_tile(strip, lines):
        tile = lines * length
        first = pl.multiple_of(strip * length, length)
        item_id = lax.broadcasted_iota(jnp.int32, (items, tile), 0)
        x = events[pl.ds(first, tile), :].astype(jnp.float32)
        center, spread = center_and_spread(x)
        half_normed = (center * (0.5 * lax.rsqrt(spread + 1e-05))).astype(jnp.bfloat16)
        gate, values, query, keys = [
            half_silu(
                jnp.dot(
                    half_normed, w_in[:, part * width : (part + 1) * width],
                    preferred_element_type=jnp.float32,
                )
            ).astype(jnp.bfloat16)
            for part in range(4)
        ]
        key[pl.ds(first + length, tile), :] = keys
        value[pl.ds(first + length, tile), :] = values
        mixed = []
        for k in range(lines):
            base = pl.multiple_of(first + k * length, length)
            sources = pl.ds(base, 2 * length)
            start = starts_ref[pl.ds(base, length), :]
            ahead = packed_tgt[pl.ds(strip + k, 1), :] >= 0
            here = packed_tgt[pl.ds(strip + k + 1, 1), :] >= 0
            keep_ahead = (base - length + col >= start) & ahead
            keep_here = (col <= row) & (base + col >= start) & here
            keep = jnp.concatenate([keep_ahead, keep_here], axis=1)
            by_head = []
            for h in range(heads):
                cols = slice(h * hdim, (h + 1) * hdim)
                scores = lax.dot_general(
                    query[k * length : (k + 1) * length, cols], key[sources, cols], contract_last,
                    preferred_element_type=jnp.float32,
                )
                attn = half_silu(scores * (0.5 / math.sqrt(hdim)) + bias[h])
                attn = jnp.where(keep, attn, 0.0).astype(jnp.bfloat16)
                by_head.append(jnp.dot(attn, value[sources, cols], preferred_element_type=jnp.float32))
            mixed.append(jnp.concatenate(by_head, axis=1))
        center, spread = center_and_spread(jnp.concatenate(mixed, axis=0))
        normed = center * lax.rsqrt(spread + 1e-05)
        gated = (normed * gate.astype(jnp.float32)).astype(jnp.bfloat16)
        out = x + jnp.dot(gated, w_out[...], preferred_element_type=jnp.float32)
        out = out.astype(jnp.bfloat16).astype(jnp.float32)
        square = jnp.sum(out * out, axis=-1, keepdims=True)
        queries = (out * lax.rsqrt(square + 1e-06)).astype(jnp.bfloat16)

        target = jnp.concatenate(
            [packed_tgt[pl.ds(strip + k + 1, 1), :] for k in range(lines)], axis=1
        )
        total = jnp.zeros((1, tile), jnp.float32)
        target_dot = jnp.zeros((1, tile), jnp.float32)
        for j, block in enumerate(block_ids):
            dots = lax.dot_general(
                unit_refs[j][...], queries, contract_last, preferred_element_type=jnp.float32
            )
            exps = jnp.exp2(dots * rate - rate)
            exp_ref[j, :, :tile] = exps
            total += jnp.sum(exps, axis=0, keepdims=True)
            hit = item_id == target - block * items
            target_dot += jnp.sum(jnp.where(hit, dots, 0.0), axis=0, keepdims=True)
        loss = logit_scale + jnp.log(total) - logit_scale * target_dot
        for k in range(lines):
            packed_loss[pl.ds(strip + k, 1), :] = loss[:, k * length : (k + 1) * length]
        share = jnp.where(target >= 0, 1.0 / total, 0.0)
        for j, block in enumerate(block_ids):
            hit = item_id == target - block * items
            left = exp_ref[j, :, :tile] * share - jnp.where(hit, 1.0, 0.0)
            residual[j, :, :tile] = left.astype(jnp.bfloat16)
        for j in range(len(block_ids)):
            sums[j][...] += jnp.dot(residual[j, :, :tile], queries, preferred_element_type=jnp.float32)

    def full_tile(t, _):
        one_tile(t * (tile // length), tile // length)
        return 0

    full = strips // (tile // length)
    lax.fori_loop(0, full, full_tile, 0)
    pl.when(strips % (tile // length) != 0)(lambda: one_tile(full * (tile // length), 1))

    for u in range(per_step):
        line, turn = starts[u] // length, lax.rem(starts[u], length)
        back = lax.rem(length - turn, length)
        near = pltpu.roll(packed_loss[pl.ds(line, 1), :], back, 1)
        rest = pltpu.roll(packed_loss[pl.ds(line + 1, 1), :], back, 1)
        loss = jnp.where(place < length - turn, near, rest)
        loss_ref[pl.ds(spots[u], 1), :] = jnp.where(place < lens[u], loss, 0.0)


def step_scratch(places, length, width, blocks, items):
    rows = -(-min(len(places), 8) * length // tile) * tile
    lines = -(-(rows // length + 2) // 8) * 8
    return [
        pltpu.VMEM((blocks, items, tile), jnp.float32),
        pltpu.VMEM((blocks, items, tile), jnp.bfloat16),
        pltpu.VMEM((rows + tile, width), jnp.bfloat16),
        pltpu.VMEM((rows + tile, length), jnp.int32),
        pltpu.VMEM((length + rows + tile, width), jnp.bfloat16),
        pltpu.VMEM((length + rows + tile, width), jnp.bfloat16),
        pltpu.VMEM((lines, length), jnp.int32),
        pltpu.VMEM((lines, length), jnp.float32),
    ]


scalars = pl.BlockSpec(memory_space=pltpu.SMEM)
whole = pl.BlockSpec(memory_space=pltpu.VMEM)
far_off = pl.BlockSpec(memory_space=pltpu.HBM)


def load_call(w_in, w_out, rel_bias):
    heads, length = rel_bias.shape
    return pl.pallas_call(
        load_kernel,
        in_specs=[far_off, far_off, whole],
        out_specs=[whole] * 3,
        scratch_shapes=[pltpu.SemaphoreType.DMA((2,))],
        out_shape=[
            pltpu.VMEM(w_in.shape, jnp.bfloat16),
            pltpu.VMEM(w_out.shape, jnp.bfloat16),
            pltpu.VMEM((heads, length, 2 * length), jnp.float32),
        ],
        name="load",
    )(in_hbm(w_in), in_hbm(w_out), rel_bias)


def first_call(ids, places, users, packed, units, w_in, w_out, bias):
    length = bias.shape[1]
    width, (blocks, items, _) = w_out.shape[0], units.shape
    arrays = [w_in, w_out, bias, units, *packed]
    return pl.pallas_call(
        functools.partial(first_kernel, places, blocks),
        in_specs=[scalars] + [whole] * len(arrays),
        out_specs=[whole] * (1 + blocks),
        scratch_shapes=step_scratch(places, length, width, blocks, items),
        out_shape=[pltpu.VMEM((users, length), jnp.float32)]
        + [pltpu.VMEM((items, width), jnp.float32)] * blocks,
        compiler_params=pltpu.CompilerParams(vmem_limit_bytes=24 * 1024 * 1024),
        name="first_users",
    )(ids, *[in_vmem(array) for array in arrays])


def second_call(ids, places, packed, units, w_in, w_out, loss, sums, bias):
    items, width = sums[0].shape
    length, blocks = bias.shape[1], len(sums)
    arrays = [w_in, w_out, bias, units, loss, *sums, *packed]
    return pl.pallas_call(
        functools.partial(second_kernel, places, blocks),
        in_specs=[scalars] + [whole] * len(arrays),
        out_specs=[whole] * (1 + blocks),
        scratch_shapes=[pltpu.VMEM((blocks - blocks // 2, items, width), jnp.float32)]
        + step_scratch(places, length, width, blocks, items),
        out_shape=[jax.ShapeDtypeStruct(loss.shape, jnp.float32)]
        + [
            pltpu.VMEM((items, width), jnp.float32 if k < blocks // 2 else jnp.bfloat16)
            for k in range(blocks)
        ],
        compiler_params=pltpu.CompilerParams(vmem_limit_bytes=24 * 1024 * 1024),
        name="second_users",
    )(ids, *[in_vmem(array) for array in arrays])


def shards(histories, lengths, targets, send_list, w_in, w_out, rel_bias, item_pool):
    user_count = histories.shape[0]
    groups, blocks = lax.axis_size("dp"), lax.axis_size("blk")
    slots = user_count // groups
    group, mine = lax.axis_index("dp").astype(jnp.int32), lax.axis_index("blk").astype(jnp.int32)

    work = sorted(
        ((shift, slot) for shift in range(groups) for slot in range(slots)),
        key=lambda pair: (pair[0] != 0, abs(pair[0] - groups / 2)),
    )
    *packed, units = pack(
        histories, lengths, targets, send_list, item_pool, work, groups, group.reshape(1), blocks
    )
    half = user_count // 2
    for k in range(slots, user_count):
        if k == user_count - 2 * slots:
            packed[slots], w_in = lax.optimization_barrier((packed[slots], w_in))
            w_in, w_out, bias = load_call(w_in, w_out, rel_bias)
        if k >= user_count - 2 * slots:
            packed[k], w_out = lax.optimization_barrier((packed[k], w_out))
        packed[k] = from_behind(packed[k], "dp", work[k][0])
    units = lax.all_to_all(units, "blk", split_axis=0, concat_axis=0, tiled=True)

    pool_float = item_pool.astype(jnp.float32)
    item_norm = jnp.sqrt(jnp.sum(pool_float * pool_float, axis=-1, keepdims=True) + 1e-06)
    unit_rows = pool_float / item_norm

    came = [((group - shift) % groups) * slots + slot for shift, slot in work]
    ids = jnp.stack([mine, mine ^ 2, mine ^ 1, mine ^ 3, *came])
    order = tuple(range(user_count))
    loss, *sums = first_call(ids, order[:half], user_count, packed[:half], units, w_in, w_out, bias)
    row_loss, own, over, side, far = second_call(
        ids, order[half:], packed[half:], units, w_in, w_out, loss, sums, bias
    )
    over = over + swap(far, "blk", 1).astype(jnp.float32)
    own = own + swap(side, "blk", 1).astype(jnp.float32)
    item_sum = logit_scale * (own + swap(over.astype(jnp.bfloat16), "blk", 2).astype(jnp.float32))
    pool_grad = (
        item_sum - unit_rows * jnp.sum(unit_rows * item_sum, axis=-1, keepdims=True)
    ) / item_norm
    return (row_loss, pool_grad)


def solution(mesh):
    placed = (
        P(("dp", "blk"), None, None),
        P(("dp", "blk")),
        P(("dp", "blk"), None),
        P(("dp", "blk")),
        P(),
        P(),
        P(),
        P(("dp", "blk"), None),
    )
    return jax.shard_map(
        shards,
        mesh=mesh,
        in_specs=placed,
        out_specs=(P(("dp", "blk"), None), P(("dp", "blk"), None)),
        check_vma=False,
    )
```

```python
import functools
import math

import jax
import jax.numpy as jnp
from jax import lax
from jax.experimental import pallas as pl
from jax.experimental.pallas import tpu as pltpu
from jax.sharding import PartitionSpec as P

logit_scale = 20.0
contract_last = (((1,), (1,)), ((), ()))
tile = 256
chunk = 16
number_rows = 8


def swap(array, axis, bit):
    devices = lax.axis_size(axis)
    return lax.ppermute(array, axis, [(i, i ^ bit) for i in range(devices)])


def from_behind(array, axis, by):
    devices = lax.axis_size(axis)
    return lax.ppermute(array, axis, [(i, (i + by) % devices) for i in range(devices)])


def in_vmem(array):
    return pltpu.with_memory_space_constraint(array, pltpu.VMEM)


def in_hbm(array):
    return pltpu.with_memory_space_constraint(array, pltpu.HBM)


def half_silu(half):
    return half + half * jnp.tanh(half)


def center_and_spread(values):
    center = values - jnp.mean(values, axis=-1, keepdims=True)
    return center, jnp.mean(center * center, axis=-1, keepdims=True)


def pack_kernel(
    work, groups, group_ref, list_any, len_any, from_any, tgt_any, pool_any, *refs,
):
    users, length, width = from_any.shape
    to_refs, unit_any = refs[:users], refs[users]
    entries, lens, targets, pool, unit, sems, in_sems = refs[users + 1 :]
    pieces = width // length
    small = [
        pltpu.make_async_copy(source, target, sems.at[k])
        for k, (source, target) in enumerate(
            ((list_any, entries), (len_any, lens), (tgt_any, targets), (pool_any, pool))
        )
    ]
    for copy in small:
        copy.start()
    small[0].wait()
    slots = users // groups
    order = [entries[(group_ref[0] + shift) % groups * slots + slot] for shift, slot in work]
    copies_in = [
        pltpu.make_async_copy(
            from_any.at[order[k], :, pl.ds(c * length, length)],
            to_refs[k].at[pl.ds(c * length, length)],
            in_sems.at[k, c],
        )
        for k in range(users)
        for c in range(pieces)
    ]
    for copy in copies_in:
        copy.start()
    small[3].wait()
    rows = pool[...].astype(jnp.float32)
    unit[...] = (rows * lax.rsqrt(jnp.sum(rows * rows, axis=-1, keepdims=True) + 1e-06)).astype(jnp.bfloat16)
    units_out = [
        pltpu.make_async_copy(unit, unit_any.at[k], sems.at[4 + k]) for k in range(unit_any.shape[0])
    ]
    for copy in units_out:
        copy.start()
    small[1].wait()
    small[2].wait()
    row = lax.broadcasted_iota(jnp.int32, (number_rows, length), 0)
    for k in range(users):
        target = targets[pl.ds(order[k], 1), :]
        numbers = jnp.where(row == 0, lens[order[k]], jnp.where(row == 1, target // 256, target % 256))
        to_refs[k][width:, :] = numbers.astype(jnp.float32).astype(jnp.bfloat16)
    for copy in copies_in + units_out:
        copy.wait()


def pack(histories, lengths, targets, entries, item_pool, work, groups, group, blocks):
    users, length, width = histories.shape
    shape = (width + number_rows, length)
    hbm = pl.BlockSpec(memory_space=pltpu.HBM)
    return pl.pallas_call(
        functools.partial(pack_kernel, work, groups),
        in_specs=[pl.BlockSpec(memory_space=pltpu.SMEM)] + [hbm] * 5,
        out_specs=[pl.BlockSpec(memory_space=pltpu.VMEM)] * users + [hbm],
        scratch_shapes=[
            pltpu.SMEM(entries.shape, jnp.int32),
            pltpu.SMEM(lengths.shape, jnp.int32),
            pltpu.VMEM(targets.shape, jnp.int32),
            pltpu.VMEM(item_pool.shape, jnp.bfloat16),
            pltpu.VMEM(item_pool.shape, jnp.bfloat16),
            pltpu.SemaphoreType.DMA((4 + blocks,)),
            pltpu.SemaphoreType.DMA((users, width // length)),
        ],
        out_shape=[pltpu.VMEM(shape, jnp.bfloat16)] * users
        + [pltpu.HBM((blocks,) + item_pool.shape, jnp.bfloat16)],
        compiler_params=pltpu.CompilerParams(vmem_limit_bytes=16 * 1024 * 1024),
        name="pack",
    )(group, *[in_hbm(array) for array in (entries, lengths, histories, targets, item_pool)])


def users_kernel(places, blocks, id_ref, x_refs, w_in, w_out, unit_ref, sums, loss_ref, bias, scratch):
    count = len(places)
    units = [unit_ref.at[id_ref[k]] for k in range(blocks)]
    for at in range(0, count, 8):
        users_step(
            x_refs[at : at + 8], [id_ref[blocks + k] for k in places[at : at + 8]],
            [id_ref[k] for k in range(blocks)], w_in, w_out, units, loss_ref, sums, bias, *scratch,
        )


def first_kernel(
    places, blocks, id_ref, w_in_any, w_out_any, rel_any, unit_ref, *refs
):
    count = len(places)
    x_refs, refs = refs[:count], refs[count:]
    loss_ref, sums, bias, refs = refs[0], refs[1 : 1 + blocks], refs[1 + blocks], refs[2 + blocks :]
    w_in, w_out, rel, sems = refs[:4]
    heads, length = rel.shape
    moves = [(rel_any, rel), (w_in_any, w_in), (w_out_any, w_out)]
    copies = [pltpu.make_async_copy(*move, sems.at[k]) for k, move in enumerate(moves)]
    for copy in copies:
        copy.start()
    loss_ref[...] = jnp.zeros_like(loss_ref)
    for ref in sums:
        ref[...] = jnp.zeros_like(ref)
    copies[0].wait()
    for h in range(heads):
        wide = jnp.broadcast_to(0.5 * rel[h : h + 1, :], (length, length))
        turned = pltpu.roll(wide, 0, 1, stride=1, stride_axis=0).T
        bias[h] = jnp.concatenate([turned, turned], axis=1)
    for copy in copies[1:]:
        copy.wait()
    users_kernel(places, blocks, id_ref, x_refs, w_in, w_out, unit_ref, sums, loss_ref, bias, refs[4:])


def second_kernel(places, blocks, id_ref, w_in, w_out, bias, unit_ref, loss_in, *refs):
    count = len(places)
    sums_in, x_refs, refs = refs[:blocks], refs[blocks : blocks + count], refs[blocks + count :]
    loss_ref, out_refs, wide_sums = refs[0], refs[1 : 1 + blocks], refs[1 + blocks]
    sums = [out_refs[k] if k < blocks // 2 else wide_sums.at[k - blocks // 2] for k in range(blocks)]
    loss_ref[...] = loss_in[...]
    for k in range(blocks):
        sums[k][...] = sums_in[k][...]
    users_kernel(
        places, blocks, id_ref, x_refs, w_in, w_out, unit_ref, sums, loss_ref, bias, refs[2 + blocks :]
    )
    for k in range(blocks // 2, blocks):
        out_refs[k][...] = sums[k][...].astype(out_refs[k].dtype)


def users_step(
    x_refs, spots, block_ids, w_in, w_out, unit_refs, loss_ref, sums, bias,
    exp_ref, residual, events, starts_ref, key, value, packed_tgt, packed_loss,
):
    heads, length, _ = bias.shape
    width = w_out.shape[0]
    hdim = width // heads
    items = unit_refs[0].shape[0]
    per_step = len(x_refs)

    digits = [ref[width:, :].astype(jnp.float32) for ref in x_refs]
    lens = [jnp.max(digit[:1, :]).astype(jnp.int32) for digit in digits]
    starts, end = [], 0
    for u in range(per_step):
        starts.append(pl.multiple_of(end, chunk) if u else 0)
        end = end + (lens[u] + chunk - 1) // chunk * chunk
    end = pl.multiple_of(end, chunk)
    tiles = (end + tile - 1) // tile

    place = lax.broadcasted_iota(jnp.int32, (1, length), 1)
    packed_tgt[...] = jnp.full_like(packed_tgt, -1)
    key[:length, :] = jnp.zeros((length, width), key.dtype)
    value[:length, :] = jnp.zeros((length, width), value.dtype)
    for u in range(per_step):
        starts_ref[pl.ds(starts[u], length), :] = jnp.full((length, length), starts[u], jnp.int32)
    for u in range(per_step):
        for c in range(0, width, length):
            events[pl.ds(starts[u], length), c : c + length] = x_refs[u][c : c + length, :]
        target = digits[u][1:2, :] * 256.0 + digits[u][2:3, :]
        wanted = jnp.where(place < lens[u], target.astype(jnp.int32), -1)
        line, turn = starts[u] // length + 1, lax.rem(starts[u], length)
        turned = pltpu.roll(wanted, turn, 1)
        packed_tgt[pl.ds(line, 1), :] = jnp.where(place >= turn, turned, packed_tgt[pl.ds(line, 1), :])
        packed_tgt[pl.ds(line + 1, 1), :] = jnp.where(
            place < turn, turned, packed_tgt[pl.ds(line + 1, 1), :]
        )
    events[pl.ds(end, tile), :] = jnp.zeros((tile, width), events.dtype)

    row = lax.broadcasted_iota(jnp.int32, (length, length), 0)
    col = lax.broadcasted_iota(jnp.int32, (length, length), 1)
    rate = logit_scale * math.log2(math.e)

    lines = tile // length

    def one_tile(t, _):
        first, strip = pl.multiple_of(t * tile, tile), t * lines
        item_id = lax.broadcasted_iota(jnp.int32, (items, tile), 0)
        x = events[pl.ds(first, tile), :].astype(jnp.float32)
        center, spread = center_and_spread(x)
        half_normed = (center * (0.5 * lax.rsqrt(spread + 1e-05))).astype(jnp.bfloat16)
        gate, values, query, keys = [
            half_silu(
                jnp.dot(
                    half_normed, w_in[:, part * width : (part + 1) * width],
                    preferred_element_type=jnp.float32,
                )
            ).astype(jnp.bfloat16)
            for part in range(4)
        ]
        key[pl.ds(first + length, tile), :] = keys
        value[pl.ds(first + length, tile), :] = values
        mixed = []
        for k in range(lines):
            base = pl.multiple_of(first + k * length, length)
            sources = pl.ds(base, 2 * length)
            start = starts_ref[pl.ds(base, length), :]
            ahead = packed_tgt[pl.ds(strip + k, 1), :] >= 0
            here = packed_tgt[pl.ds(strip + k + 1, 1), :] >= 0
            keep_ahead = (base - length + col >= start) & ahead
            keep_here = (col <= row) & (base + col >= start) & here
            keep = jnp.concatenate([keep_ahead, keep_here], axis=1)
            by_head = []
            for h in range(heads):
                cols = slice(h * hdim, (h + 1) * hdim)
                scores = lax.dot_general(
                    query[k * length : (k + 1) * length, cols], key[sources, cols], contract_last,
                    preferred_element_type=jnp.float32,
                )
                attn = half_silu(scores * (0.5 / math.sqrt(hdim)) + bias[h])
                attn = jnp.where(keep, attn, 0.0).astype(jnp.bfloat16)
                by_head.append(jnp.dot(attn, value[sources, cols], preferred_element_type=jnp.float32))
            mixed.append(jnp.concatenate(by_head, axis=1))
        center, spread = center_and_spread(jnp.concatenate(mixed, axis=0))
        normed = center * lax.rsqrt(spread + 1e-05)
        gated = (normed * gate.astype(jnp.float32)).astype(jnp.bfloat16)
        out = x + jnp.dot(gated, w_out[...], preferred_element_type=jnp.float32)
        out = out.astype(jnp.bfloat16).astype(jnp.float32)
        square = jnp.sum(out * out, axis=-1, keepdims=True)
        queries = (out * lax.rsqrt(square + 1e-06)).astype(jnp.bfloat16)

        target = jnp.concatenate(
            [packed_tgt[pl.ds(strip + k + 1, 1), :] for k in range(lines)], axis=1
        )
        total = jnp.zeros((1, tile), jnp.float32)
        target_dot = jnp.zeros((1, tile), jnp.float32)
        for j, block in enumerate(block_ids):
            dots = lax.dot_general(
                unit_refs[j][...], queries, contract_last, preferred_element_type=jnp.float32
            )
            exps = jnp.exp2(dots * rate - rate)
            exp_ref[j] = exps
            total += jnp.sum(exps, axis=0, keepdims=True)
            hit = item_id == target - block * items
            target_dot += jnp.sum(jnp.where(hit, dots, 0.0), axis=0, keepdims=True)
        loss = logit_scale + jnp.log(total) - logit_scale * target_dot
        for k in range(lines):
            packed_loss[pl.ds(strip + k, 1), :] = loss[:, k * length : (k + 1) * length]
        share = jnp.where(target >= 0, 1.0 / total, 0.0)
        for j, block in enumerate(block_ids):
            hit = item_id == target - block * items
            left = exp_ref[j] * share - jnp.where(hit, 1.0, 0.0)
            residual[j] = left.astype(jnp.bfloat16)
        for j in range(len(block_ids)):
            sums[j][...] += jnp.dot(residual[j], queries, preferred_element_type=jnp.float32)
        return 0

    lax.fori_loop(0, tiles, one_tile, 0)

    for u in range(per_step):
        line, turn = starts[u] // length, lax.rem(starts[u], length)
        back = lax.rem(length - turn, length)
        near = pltpu.roll(packed_loss[pl.ds(line, 1), :], back, 1)
        rest = pltpu.roll(packed_loss[pl.ds(line + 1, 1), :], back, 1)
        loss = jnp.where(place < length - turn, near, rest)
        loss_ref[pl.ds(spots[u], 1), :] = jnp.where(place < lens[u], loss, 0.0)


def step_scratch(places, length, width, blocks, items):
    rows = -(-min(len(places), 8) * length // tile) * tile
    lines = -(-(rows // length + 2) // 8) * 8
    return [
        pltpu.VMEM((blocks, items, tile), jnp.float32),
        pltpu.VMEM((blocks, items, tile), jnp.bfloat16),
        pltpu.VMEM((rows + tile, width), jnp.bfloat16),
        pltpu.VMEM((rows + tile, length), jnp.int32),
        pltpu.VMEM((length + rows + tile, width), jnp.bfloat16),
        pltpu.VMEM((length + rows + tile, width), jnp.bfloat16),
        pltpu.VMEM((lines, length), jnp.int32),
        pltpu.VMEM((lines, length), jnp.float32),
    ]


scalars = pl.BlockSpec(memory_space=pltpu.SMEM)
whole = pl.BlockSpec(memory_space=pltpu.VMEM)
far_off = pl.BlockSpec(memory_space=pltpu.HBM)


def first_call(ids, places, users, packed, units, w_in, w_out, rel_bias):
    heads, length = rel_bias.shape
    width, (blocks, items, _) = w_out.shape[0], units.shape
    table = (heads, length, 2 * length)
    return pl.pallas_call(
        functools.partial(first_kernel, places, blocks),
        in_specs=[scalars] + [far_off] * 3 + [whole] * (1 + len(places)),
        out_specs=[whole] * (2 + blocks),
        scratch_shapes=[
            pltpu.VMEM(w_in.shape, jnp.bfloat16),
            pltpu.VMEM(w_out.shape, jnp.bfloat16),
            pltpu.VMEM(rel_bias.shape, jnp.float32),
            pltpu.SemaphoreType.DMA((3,)),
        ]
        + step_scratch(places, length, width, blocks, items),
        out_shape=[pltpu.VMEM((users, length), jnp.float32)]
        + [pltpu.VMEM((items, width), jnp.float32)] * blocks
        + [pltpu.VMEM(table, jnp.float32)],
        compiler_params=pltpu.CompilerParams(vmem_limit_bytes=24 * 1024 * 1024),
        name="first_users",
    )(
        ids, *[in_hbm(array) for array in (w_in, w_out, rel_bias)], in_vmem(units),
        *[in_vmem(array) for array in packed],
    )


def second_call(ids, places, packed, units, w_in, w_out, loss, sums, bias):
    items, width = sums[0].shape
    length, blocks = bias.shape[1], len(sums)
    arrays = [w_in, w_out, bias, units, loss, *sums, *packed]
    return pl.pallas_call(
        functools.partial(second_kernel, places, blocks),
        in_specs=[scalars] + [whole] * len(arrays),
        out_specs=[whole] * (1 + blocks),
        scratch_shapes=[pltpu.VMEM((blocks - blocks // 2, items, width), jnp.float32)]
        + step_scratch(places, length, width, blocks, items),
        out_shape=[jax.ShapeDtypeStruct(loss.shape, jnp.float32)]
        + [
            pltpu.VMEM((items, width), jnp.float32 if k < blocks // 2 else jnp.bfloat16)
            for k in range(blocks)
        ],
        compiler_params=pltpu.CompilerParams(vmem_limit_bytes=24 * 1024 * 1024),
        name="second_users",
    )(ids, *[in_vmem(array) for array in arrays])


def shards(histories, lengths, targets, send_list, w_in, w_out, rel_bias, item_pool):
    user_count = histories.shape[0]
    groups, blocks = lax.axis_size("dp"), lax.axis_size("blk")
    slots = user_count // groups
    group, mine = lax.axis_index("dp").astype(jnp.int32), lax.axis_index("blk").astype(jnp.int32)

    work = sorted(
        ((shift, slot) for shift in range(groups) for slot in range(slots)),
        key=lambda pair: (pair[0] != 0, pair[0] not in (1, groups - 1), abs(pair[0] - groups / 2)),
    )
    *packed, units = pack(
        histories, lengths, targets, send_list, item_pool, work, groups, group.reshape(1), blocks
    )
    half = user_count // 2
    packed = [
        users if shift == 0 else from_behind(users, "dp", shift) for users, (shift, _) in zip(packed, work)
    ]
    units = lax.all_to_all(units, "blk", split_axis=0, concat_axis=0, tiled=True)

    pool_float = item_pool.astype(jnp.float32)
    item_norm = jnp.sqrt(jnp.sum(pool_float * pool_float, axis=-1, keepdims=True) + 1e-06)
    unit_rows = pool_float / item_norm

    came = [((group - shift) % groups) * slots + slot for shift, slot in work]
    ids = jnp.stack([mine, mine ^ 2, mine ^ 1, mine ^ 3, *came])
    order = tuple(range(user_count))
    loss, *sums, bias = first_call(
        ids, order[:half], user_count, packed[:half], units, w_in, w_out, rel_bias
    )
    row_loss, own, over, side, far = second_call(
        ids, order[half:], packed[half:], units, w_in, w_out, loss, sums, bias
    )
    over = over + swap(far, "blk", 1).astype(jnp.float32)
    own = own + swap(side, "blk", 1).astype(jnp.float32)
    item_sum = logit_scale * (own + swap(over.astype(jnp.bfloat16), "blk", 2).astype(jnp.float32))
    pool_grad = (
        item_sum - unit_rows * jnp.sum(unit_rows * item_sum, axis=-1, keepdims=True)
    ) / item_norm
    return (row_loss, pool_grad)


def solution(mesh):
    placed = (
        P(("dp", "blk"), None, None),
        P(("dp", "blk")),
        P(("dp", "blk"), None),
        P(("dp", "blk")),
        P(),
        P(),
        P(),
        P(("dp", "blk"), None),
    )
    return jax.shard_map(
        shards,
        mesh=mesh,
        in_specs=placed,
        out_specs=(P(("dp", "blk"), None), P(("dp", "blk"), None)),
        check_vma=False,
    )
```

```python
import functools
import math

import jax
import jax.numpy as jnp
from jax import lax
from jax.experimental import pallas as pl
from jax.experimental.pallas import tpu as pltpu
from jax.sharding import PartitionSpec as P

logit_scale = 20.0
contract_last = (((1,), (1,)), ((), ()))
tile = 256
chunk = 16
number_rows = 8


def swap(array, axis, bit):
    devices = lax.axis_size(axis)
    return lax.ppermute(array, axis, [(i, i ^ bit) for i in range(devices)])


def from_behind(array, axis, by):
    devices = lax.axis_size(axis)
    return lax.ppermute(array, axis, [(i, (i + by) % devices) for i in range(devices)])


def in_vmem(array):
    return pltpu.with_memory_space_constraint(array, pltpu.VMEM)


def in_hbm(array):
    return pltpu.with_memory_space_constraint(array, pltpu.HBM)


def half_silu(half):
    return half + half * jnp.tanh(half)


def center_and_spread(values):
    center = values - jnp.mean(values, axis=-1, keepdims=True)
    return center, jnp.mean(center * center, axis=-1, keepdims=True)


def pack_kernel(
    work, groups, group_ref, list_any, len_any, from_any, tgt_any, pool_any, *refs,
):
    users, length, width = from_any.shape
    to_refs, unit_any = refs[:users], refs[users]
    entries, lens, targets, pool, unit, sems, in_sems = refs[users + 1 :]
    pieces = width // length
    small = [
        pltpu.make_async_copy(source, target, sems.at[k])
        for k, (source, target) in enumerate(
            ((list_any, entries), (len_any, lens), (tgt_any, targets), (pool_any, pool))
        )
    ]
    for copy in small:
        copy.start()
    small[0].wait()
    slots = users // groups
    order = [entries[(group_ref[0] + shift) % groups * slots + slot] for shift, slot in work]
    copies_in = [
        pltpu.make_async_copy(
            from_any.at[order[k], :, pl.ds(c * length, length)],
            to_refs[k].at[pl.ds(c * length, length)],
            in_sems.at[k, c],
        )
        for k in range(users)
        for c in range(pieces)
    ]
    for copy in copies_in:
        copy.start()
    small[3].wait()
    rows = pool[...].astype(jnp.float32)
    unit[...] = (rows * lax.rsqrt(jnp.sum(rows * rows, axis=-1, keepdims=True) + 1e-06)).astype(jnp.bfloat16)
    units_out = [
        pltpu.make_async_copy(unit, unit_any.at[k], sems.at[4 + k]) for k in range(unit_any.shape[0])
    ]
    for copy in units_out:
        copy.start()
    small[1].wait()
    small[2].wait()
    row = lax.broadcasted_iota(jnp.int32, (number_rows, length), 0)
    for k in range(users):
        target = targets[pl.ds(order[k], 1), :]
        numbers = jnp.where(row == 0, lens[order[k]], jnp.where(row == 1, target // 256, target % 256))
        to_refs[k][width:, :] = numbers.astype(jnp.float32).astype(jnp.bfloat16)
    for copy in copies_in + units_out:
        copy.wait()


def pack(histories, lengths, targets, entries, item_pool, work, groups, group, blocks):
    users, length, width = histories.shape
    shape = (width + number_rows, length)
    hbm = pl.BlockSpec(memory_space=pltpu.HBM)
    return pl.pallas_call(
        functools.partial(pack_kernel, work, groups),
        in_specs=[pl.BlockSpec(memory_space=pltpu.SMEM)] + [hbm] * 5,
        out_specs=[pl.BlockSpec(memory_space=pltpu.VMEM)] * users + [hbm],
        scratch_shapes=[
            pltpu.SMEM(entries.shape, jnp.int32),
            pltpu.SMEM(lengths.shape, jnp.int32),
            pltpu.VMEM(targets.shape, jnp.int32),
            pltpu.VMEM(item_pool.shape, jnp.bfloat16),
            pltpu.VMEM(item_pool.shape, jnp.bfloat16),
            pltpu.SemaphoreType.DMA((4 + blocks,)),
            pltpu.SemaphoreType.DMA((users, width // length)),
        ],
        out_shape=[pltpu.VMEM(shape, jnp.bfloat16)] * users
        + [pltpu.HBM((blocks,) + item_pool.shape, jnp.bfloat16)],
        compiler_params=pltpu.CompilerParams(vmem_limit_bytes=16 * 1024 * 1024),
        name="pack",
    )(group, *[in_hbm(array) for array in (entries, lengths, histories, targets, item_pool)])


def users_kernel(places, blocks, id_ref, x_refs, w_in, w_out, unit_ref, sums, loss_ref, bias, scratch):
    count = len(places)
    units = [unit_ref.at[id_ref[k]] for k in range(blocks)]
    for at in range(0, count, 8):
        users_step(
            x_refs[at : at + 8], [id_ref[blocks + k] for k in places[at : at + 8]],
            [id_ref[k] for k in range(blocks)], w_in, w_out, units, loss_ref, sums, bias, *scratch,
        )


def first_kernel(
    places, blocks, id_ref, w_in_any, w_out_any, rel_any, unit_ref, *refs
):
    count = len(places)
    x_refs, refs = refs[:count], refs[count:]
    loss_ref, sums, bias, refs = refs[0], refs[1 : 1 + blocks], refs[1 + blocks], refs[2 + blocks :]
    w_in, w_out, rel, sems = refs[:4]
    heads, length = rel.shape
    moves = [(rel_any, rel), (w_in_any, w_in), (w_out_any, w_out)]
    copies = [pltpu.make_async_copy(*move, sems.at[k]) for k, move in enumerate(moves)]
    for copy in copies:
        copy.start()
    loss_ref[...] = jnp.zeros_like(loss_ref)
    for ref in sums:
        ref[...] = jnp.zeros_like(ref)
    copies[0].wait()
    for h in range(heads):
        wide = jnp.broadcast_to(0.5 * rel[h : h + 1, :], (length, length))
        turned = pltpu.roll(wide, 0, 1, stride=1, stride_axis=0).T
        bias[h] = jnp.concatenate([turned, turned], axis=1)
    for copy in copies[1:]:
        copy.wait()
    users_kernel(places, blocks, id_ref, x_refs, w_in, w_out, unit_ref, sums, loss_ref, bias, refs[4:])


def second_kernel(places, blocks, id_ref, w_in, w_out, bias, unit_ref, loss_in, *refs):
    count = len(places)
    sums_in, x_refs, refs = refs[:blocks], refs[blocks : blocks + count], refs[blocks + count :]
    loss_ref, out_refs, wide_sums = refs[0], refs[1 : 1 + blocks], refs[1 + blocks]
    sums = [out_refs[k] if k < blocks // 2 else wide_sums.at[k - blocks // 2] for k in range(blocks)]
    loss_ref[...] = loss_in[...]
    for k in range(blocks):
        sums[k][...] = sums_in[k][...]
    users_kernel(
        places, blocks, id_ref, x_refs, w_in, w_out, unit_ref, sums, loss_ref, bias, refs[2 + blocks :]
    )
    for k in range(blocks // 2, blocks):
        out_refs[k][...] = sums[k][...].astype(out_refs[k].dtype)


def users_step(
    x_refs, spots, block_ids, w_in, w_out, unit_refs, loss_ref, sums, bias,
    exp_ref, residual, events, starts_ref, key, value, packed_tgt, packed_loss,
):
    heads, length, _ = bias.shape
    width = w_out.shape[0]
    hdim = width // heads
    items = unit_refs[0].shape[0]
    per_step = len(x_refs)

    digits = [ref[width:, :].astype(jnp.float32) for ref in x_refs]
    lens = [jnp.max(digit[:1, :]).astype(jnp.int32) for digit in digits]
    starts, end = [], 0
    for u in range(per_step):
        starts.append(pl.multiple_of(end, chunk) if u else 0)
        end = end + (lens[u] + chunk - 1) // chunk * chunk
    end = pl.multiple_of(end, chunk)
    tiles = (end + tile - 1) // tile

    place = lax.broadcasted_iota(jnp.int32, (1, length), 1)
    packed_tgt[...] = jnp.full_like(packed_tgt, -1)
    key[:length, :] = jnp.zeros((length, width), key.dtype)
    value[:length, :] = jnp.zeros((length, width), value.dtype)
    for u in range(per_step):
        starts_ref[pl.ds(starts[u], length), :] = jnp.full((length, length), starts[u], jnp.int32)
    for u in range(per_step):
        for c in range(0, width, length):
            events[pl.ds(starts[u], length), c : c + length] = x_refs[u][c : c + length, :]
        target = digits[u][1:2, :] * 256.0 + digits[u][2:3, :]
        wanted = jnp.where(place < lens[u], target.astype(jnp.int32), -1)
        line, turn = starts[u] // length + 1, lax.rem(starts[u], length)
        turned = pltpu.roll(wanted, turn, 1)
        packed_tgt[pl.ds(line, 1), :] = jnp.where(place >= turn, turned, packed_tgt[pl.ds(line, 1), :])
        packed_tgt[pl.ds(line + 1, 1), :] = jnp.where(
            place < turn, turned, packed_tgt[pl.ds(line + 1, 1), :]
        )
    events[pl.ds(end, tile), :] = jnp.zeros((tile, width), events.dtype)

    row = lax.broadcasted_iota(jnp.int32, (length, length), 0)
    col = lax.broadcasted_iota(jnp.int32, (length, length), 1)
    rate = logit_scale * math.log2(math.e)

    lines = tile // length

    def one_tile(t, _):
        first, strip = pl.multiple_of(t * tile, tile), t * lines
        item_id = lax.broadcasted_iota(jnp.int32, (items, tile), 0)
        x = events[pl.ds(first, tile), :].astype(jnp.float32)
        center, spread = center_and_spread(x)
        half_normed = (center * (0.5 * lax.rsqrt(spread + 1e-05))).astype(jnp.bfloat16)
        gate, values, query, keys = [
            half_silu(
                jnp.dot(
                    half_normed, w_in[:, part * width : (part + 1) * width],
                    preferred_element_type=jnp.float32,
                )
            ).astype(jnp.bfloat16)
            for part in range(4)
        ]
        key[pl.ds(first + length, tile), :] = keys
        value[pl.ds(first + length, tile), :] = values
        mixed = []
        for k in range(lines):
            base = pl.multiple_of(first + k * length, length)
            sources = pl.ds(base, 2 * length)
            start = starts_ref[pl.ds(base, length), :]
            ahead = packed_tgt[pl.ds(strip + k, 1), :] >= 0
            here = packed_tgt[pl.ds(strip + k + 1, 1), :] >= 0
            keep_ahead = (base - length + col >= start) & ahead
            keep_here = (col <= row) & (base + col >= start) & here
            keep = jnp.concatenate([keep_ahead, keep_here], axis=1)
            by_head = []
            for h in range(heads):
                cols = slice(h * hdim, (h + 1) * hdim)
                scores = lax.dot_general(
                    query[k * length : (k + 1) * length, cols], key[sources, cols], contract_last,
                    preferred_element_type=jnp.float32,
                )
                attn = half_silu(scores * (0.5 / math.sqrt(hdim)) + bias[h])
                attn = jnp.where(keep, attn, 0.0).astype(jnp.bfloat16)
                by_head.append(jnp.dot(attn, value[sources, cols], preferred_element_type=jnp.float32))
            mixed.append(jnp.concatenate(by_head, axis=1))
        center, spread = center_and_spread(jnp.concatenate(mixed, axis=0))
        normed = center * lax.rsqrt(spread + 1e-05)
        gated = (normed * gate.astype(jnp.float32)).astype(jnp.bfloat16)
        out = x + jnp.dot(gated, w_out[...], preferred_element_type=jnp.float32)
        out = out.astype(jnp.bfloat16).astype(jnp.float32)
        square = jnp.sum(out * out, axis=-1, keepdims=True)
        queries = (out * lax.rsqrt(square + 1e-06)).astype(jnp.bfloat16)

        target = jnp.concatenate(
            [packed_tgt[pl.ds(strip + k + 1, 1), :] for k in range(lines)], axis=1
        )
        total = jnp.zeros((1, tile), jnp.float32)
        target_dot = jnp.zeros((1, tile), jnp.float32)
        for j, block in enumerate(block_ids):
            dots = lax.dot_general(
                unit_refs[j][...], queries, contract_last, preferred_element_type=jnp.float32
            )
            exps = jnp.exp2(dots * rate - rate)
            exp_ref[j] = exps
            total += jnp.sum(exps, axis=0, keepdims=True)
            hit = item_id == target - block * items
            target_dot += jnp.sum(jnp.where(hit, dots, 0.0), axis=0, keepdims=True)
        loss = logit_scale + jnp.log(total) - logit_scale * target_dot
        for k in range(lines):
            packed_loss[pl.ds(strip + k, 1), :] = loss[:, k * length : (k + 1) * length]
        share = jnp.where(target >= 0, 1.0 / total, 0.0)
        for j, block in enumerate(block_ids):
            hit = item_id == target - block * items
            left = exp_ref[j] * share - jnp.where(hit, 1.0, 0.0)
            residual[j] = left.astype(jnp.bfloat16)
        for j in range(len(block_ids)):
            sums[j][...] += jnp.dot(residual[j], queries, preferred_element_type=jnp.float32)
        return 0

    lax.fori_loop(0, tiles, one_tile, 0)

    for u in range(per_step):
        line, turn = starts[u] // length, lax.rem(starts[u], length)
        back = lax.rem(length - turn, length)
        near = pltpu.roll(packed_loss[pl.ds(line, 1), :], back, 1)
        rest = pltpu.roll(packed_loss[pl.ds(line + 1, 1), :], back, 1)
        loss = jnp.where(place < length - turn, near, rest)
        loss_ref[pl.ds(spots[u], 1), :] = jnp.where(place < lens[u], loss, 0.0)


def step_scratch(places, length, width, blocks, items):
    rows = -(-min(len(places), 8) * length // tile) * tile
    lines = -(-(rows // length + 2) // 8) * 8
    return [
        pltpu.VMEM((blocks, items, tile), jnp.float32),
        pltpu.VMEM((blocks, items, tile), jnp.bfloat16),
        pltpu.VMEM((rows + tile, width), jnp.bfloat16),
        pltpu.VMEM((rows + tile, length), jnp.int32),
        pltpu.VMEM((length + rows + tile, width), jnp.bfloat16),
        pltpu.VMEM((length + rows + tile, width), jnp.bfloat16),
        pltpu.VMEM((lines, length), jnp.int32),
        pltpu.VMEM((lines, length), jnp.float32),
    ]


scalars = pl.BlockSpec(memory_space=pltpu.SMEM)
whole = pl.BlockSpec(memory_space=pltpu.VMEM)
far_off = pl.BlockSpec(memory_space=pltpu.HBM)


def first_call(ids, places, users, packed, units, w_in, w_out, rel_bias):
    heads, length = rel_bias.shape
    width, (blocks, items, _) = w_out.shape[0], units.shape
    table = (heads, length, 2 * length)
    return pl.pallas_call(
        functools.partial(first_kernel, places, blocks),
        in_specs=[scalars] + [far_off] * 3 + [whole] * (1 + len(places)),
        out_specs=[whole] * (2 + blocks),
        scratch_shapes=[
            pltpu.VMEM(w_in.shape, jnp.bfloat16),
            pltpu.VMEM(w_out.shape, jnp.bfloat16),
            pltpu.VMEM(rel_bias.shape, jnp.float32),
            pltpu.SemaphoreType.DMA((3,)),
        ]
        + step_scratch(places, length, width, blocks, items),
        out_shape=[pltpu.VMEM((users, length), jnp.float32)]
        + [pltpu.VMEM((items, width), jnp.float32)] * blocks
        + [pltpu.VMEM(table, jnp.float32)],
        compiler_params=pltpu.CompilerParams(vmem_limit_bytes=24 * 1024 * 1024),
        name="first_users",
    )(
        ids, *[in_hbm(array) for array in (w_in, w_out, rel_bias)], in_vmem(units),
        *[in_vmem(array) for array in packed],
    )


def second_call(ids, places, packed, units, w_in, w_out, loss, sums, bias):
    items, width = sums[0].shape
    length, blocks = bias.shape[1], len(sums)
    arrays = [w_in, w_out, bias, units, loss, *sums, *packed]
    return pl.pallas_call(
        functools.partial(second_kernel, places, blocks),
        in_specs=[scalars] + [whole] * len(arrays),
        out_specs=[whole] * (1 + blocks),
        scratch_shapes=[pltpu.VMEM((blocks - blocks // 2, items, width), jnp.float32)]
        + step_scratch(places, length, width, blocks, items),
        out_shape=[jax.ShapeDtypeStruct(loss.shape, jnp.float32)]
        + [
            pltpu.VMEM((items, width), jnp.float32 if k < blocks // 2 else jnp.bfloat16)
            for k in range(blocks)
        ],
        compiler_params=pltpu.CompilerParams(vmem_limit_bytes=24 * 1024 * 1024),
        name="second_users",
    )(ids, *[in_vmem(array) for array in arrays])


def shards(histories, lengths, targets, send_list, w_in, w_out, rel_bias, item_pool):
    user_count = histories.shape[0]
    groups, blocks = lax.axis_size("dp"), lax.axis_size("blk")
    slots = user_count // groups
    group, mine = lax.axis_index("dp").astype(jnp.int32), lax.axis_index("blk").astype(jnp.int32)

    near = sorted({0, 1, groups - 1, 2 % groups}, key=lambda shift: (shift != 0, shift == 2))
    others = [shift for shift in range(groups) if shift not in near]
    order = near + sorted(others, key=lambda shift: abs(shift - groups / 2))
    work = [(shift, slot) for shift in order for slot in range(slots)]
    *packed, units = pack(
        histories, lengths, targets, send_list, item_pool, work, groups, group.reshape(1), blocks
    )
    half = user_count // 2
    packed = [
        users if shift == 0 else from_behind(users, "dp", shift) for users, (shift, _) in zip(packed, work)
    ]
    units = lax.all_to_all(units, "blk", split_axis=0, concat_axis=0, tiled=True)

    pool_float = item_pool.astype(jnp.float32)
    item_norm = jnp.sqrt(jnp.sum(pool_float * pool_float, axis=-1, keepdims=True) + 1e-06)
    unit_rows = pool_float / item_norm

    came = [((group - shift) % groups) * slots + slot for shift, slot in work]
    ids = jnp.stack([mine, mine ^ 2, mine ^ 1, mine ^ 3, *came])
    order = tuple(range(user_count))
    loss, *sums, bias = first_call(
        ids, order[:half], user_count, packed[:half], units, w_in, w_out, rel_bias
    )
    row_loss, own, over, side, far = second_call(
        ids, order[half:], packed[half:], units, w_in, w_out, loss, sums, bias
    )
    over = over + swap(far, "blk", 1).astype(jnp.float32)
    own = own + swap(side, "blk", 1).astype(jnp.float32)
    item_sum = logit_scale * (own + swap(over.astype(jnp.bfloat16), "blk", 2).astype(jnp.float32))
    pool_grad = (
        item_sum - unit_rows * jnp.sum(unit_rows * item_sum, axis=-1, keepdims=True)
    ) / item_norm
    return (row_loss, pool_grad)


def solution(mesh):
    placed = (
        P(("dp", "blk"), None, None),
        P(("dp", "blk")),
        P(("dp", "blk"), None),
        P(("dp", "blk")),
        P(),
        P(),
        P(),
        P(("dp", "blk"), None),
    )
    return jax.shard_map(
        shards,
        mesh=mesh,
        in_specs=placed,
        out_specs=(P(("dp", "blk"), None), P(("dp", "blk"), None)),
        check_vma=False,
    )
```

```python
import functools
import math

import jax
import jax.numpy as jnp
from jax import lax
from jax.experimental import pallas as pl
from jax.experimental.pallas import tpu as pltpu
from jax.sharding import PartitionSpec as P

logit_scale = 20.0
contract_last = (((1,), (1,)), ((), ()))
tile = 256
chunk = 16
number_rows = 8


def swap(array, axis, bit):
    devices = lax.axis_size(axis)
    return lax.ppermute(array, axis, [(i, i ^ bit) for i in range(devices)])


def from_behind(array, axis, by):
    devices = lax.axis_size(axis)
    return lax.ppermute(array, axis, [(i, (i + by) % devices) for i in range(devices)])


def in_vmem(array):
    return pltpu.with_memory_space_constraint(array, pltpu.VMEM)


def in_hbm(array):
    return pltpu.with_memory_space_constraint(array, pltpu.HBM)


def half_silu(half):
    return half + half * jnp.tanh(half)


def center_and_spread(values):
    center = values - jnp.mean(values, axis=-1, keepdims=True)
    return center, jnp.mean(center * center, axis=-1, keepdims=True)


def pack_kernel(
    work, groups, group_ref, list_any, len_any, from_any, tgt_any, pool_any, *refs,
):
    users, length, width = from_any.shape
    to_refs, unit_any = refs[:users], refs[users]
    entries, lens, targets, pool, unit, sems, in_sems = refs[users + 1 :]
    pieces = width // length
    small = [
        pltpu.make_async_copy(source, target, sems.at[k])
        for k, (source, target) in enumerate(
            ((list_any, entries), (len_any, lens), (tgt_any, targets), (pool_any, pool))
        )
    ]
    for copy in small:
        copy.start()
    small[0].wait()
    slots = users // groups
    order = [entries[(group_ref[0] + shift) % groups * slots + slot] for shift, slot in work]
    copies_in = [
        pltpu.make_async_copy(
            from_any.at[order[k], :, pl.ds(c * length, length)],
            to_refs[k].at[pl.ds(c * length, length)],
            in_sems.at[k, c],
        )
        for k in range(users)
        for c in range(pieces)
    ]
    for copy in copies_in:
        copy.start()
    small[3].wait()
    rows = pool[...].astype(jnp.float32)
    unit[...] = (rows * lax.rsqrt(jnp.sum(rows * rows, axis=-1, keepdims=True) + 1e-06)).astype(jnp.bfloat16)
    units_out = [
        pltpu.make_async_copy(unit, unit_any.at[k], sems.at[4 + k]) for k in range(unit_any.shape[0])
    ]
    for copy in units_out:
        copy.start()
    small[1].wait()
    small[2].wait()
    row = lax.broadcasted_iota(jnp.int32, (number_rows, length), 0)
    for k in range(users):
        target = targets[pl.ds(order[k], 1), :]
        numbers = jnp.where(row == 0, lens[order[k]], jnp.where(row == 1, target // 256, target % 256))
        to_refs[k][width:, :] = numbers.astype(jnp.float32).astype(jnp.bfloat16)
    for copy in copies_in + units_out:
        copy.wait()


def pack(histories, lengths, targets, entries, item_pool, work, groups, group, blocks):
    users, length, width = histories.shape
    shape = (width + number_rows, length)
    hbm = pl.BlockSpec(memory_space=pltpu.HBM)
    return pl.pallas_call(
        functools.partial(pack_kernel, work, groups),
        in_specs=[pl.BlockSpec(memory_space=pltpu.SMEM)] + [hbm] * 5,
        out_specs=[pl.BlockSpec(memory_space=pltpu.VMEM)] * users + [hbm],
        scratch_shapes=[
            pltpu.SMEM(entries.shape, jnp.int32),
            pltpu.SMEM(lengths.shape, jnp.int32),
            pltpu.VMEM(targets.shape, jnp.int32),
            pltpu.VMEM(item_pool.shape, jnp.bfloat16),
            pltpu.VMEM(item_pool.shape, jnp.bfloat16),
            pltpu.SemaphoreType.DMA((4 + blocks,)),
            pltpu.SemaphoreType.DMA((users, width // length)),
        ],
        out_shape=[pltpu.VMEM(shape, jnp.bfloat16)] * users
        + [pltpu.HBM((blocks,) + item_pool.shape, jnp.bfloat16)],
        compiler_params=pltpu.CompilerParams(vmem_limit_bytes=16 * 1024 * 1024),
        name="pack",
    )(group, *[in_hbm(array) for array in (entries, lengths, histories, targets, item_pool)])


def users_kernel(places, id_ref, x_refs, w_in, w_out, unit_ref, sums_in, sums, loss_ref, bias, scratch):
    blocks = unit_ref.shape[0]
    for at in range(0, len(places), 8):
        users_step(
            x_refs[at : at + 8], [id_ref[blocks + k] for k in places[at : at + 8]],
            w_in, w_out, unit_ref, sums if at else sums_in, sums, loss_ref, bias, *scratch,
        )


def first_kernel(places, id_ref, w_in_any, w_out_any, rel_any, unit_ref, *refs):
    count = len(places)
    x_refs, refs = refs[:count], refs[count:]
    loss_ref, sums, bias, refs = refs[0], refs[1], refs[2], refs[3:]
    w_in, w_out, rel, sems = refs[:4]
    heads, length = rel.shape
    moves = [(rel_any, rel), (w_in_any, w_in), (w_out_any, w_out)]
    copies = [pltpu.make_async_copy(*move, sems.at[k]) for k, move in enumerate(moves)]
    for copy in copies:
        copy.start()
    loss_ref[...] = jnp.zeros_like(loss_ref)
    copies[0].wait()
    for h in range(heads):
        wide = jnp.broadcast_to(0.5 * rel[h : h + 1, :], (length, length))
        turned = pltpu.roll(wide, 0, 1, stride=1, stride_axis=0).T
        bias[h] = jnp.concatenate([turned, turned], axis=1)
    for copy in copies[1:]:
        copy.wait()
    users_kernel(places, id_ref, x_refs, w_in, w_out, unit_ref, None, sums, loss_ref, bias, refs[4:])


def second_kernel(places, id_ref, w_in, w_out, bias, unit_ref, loss_in, sums_in, *refs):
    count = len(places)
    x_refs, refs = refs[:count], refs[count:]
    loss_ref, out_refs, sums, scratch = refs[0], refs[1:5], refs[5], refs[6:]
    loss_ref[...] = loss_in[...]
    users_kernel(places, id_ref, x_refs, w_in, w_out, unit_ref, sums_in, sums, loss_ref, bias, scratch)
    for k, ref in enumerate(out_refs):
        ref[...] = sums[id_ref[k]].astype(ref.dtype)


def users_step(
    x_refs, spots, w_in, w_out, unit_ref, sums_in, sums, loss_ref, bias,
    exp_ref, residual, events, starts_ref, key, value, packed_tgt, packed_loss,
):
    heads, length, _ = bias.shape
    width = w_out.shape[0]
    hdim = width // heads
    blocks, items, _ = unit_ref.shape
    per_step = len(x_refs)

    digits = [ref[width:, :].astype(jnp.float32) for ref in x_refs]
    lens = [jnp.max(digit[:1, :]).astype(jnp.int32) for digit in digits]
    starts, end = [], 0
    for u in range(per_step):
        starts.append(pl.multiple_of(end, chunk) if u else 0)
        end = end + (lens[u] + chunk - 1) // chunk * chunk
    end = pl.multiple_of(end, chunk)
    tiles = (end + tile - 1) // tile

    place = lax.broadcasted_iota(jnp.int32, (1, length), 1)
    packed_tgt[...] = jnp.full_like(packed_tgt, -1)
    for u in range(per_step):
        starts_ref[pl.ds(starts[u], length), :] = jnp.full((length, length), starts[u], jnp.int32)
    for u in range(per_step):
        for c in range(0, width, length):
            events[pl.ds(starts[u], length), c : c + length] = x_refs[u][c : c + length, :]
        target = digits[u][1:2, :] * 256.0 + digits[u][2:3, :]
        wanted = jnp.where(place < lens[u], target.astype(jnp.int32), -1)
        line, turn = starts[u] // length + 1, lax.rem(starts[u], length)
        turned = pltpu.roll(wanted, turn, 1)
        packed_tgt[pl.ds(line, 1), :] = jnp.where(place >= turn, turned, packed_tgt[pl.ds(line, 1), :])
        packed_tgt[pl.ds(line + 1, 1), :] = jnp.where(
            place < turn, turned, packed_tgt[pl.ds(line + 1, 1), :]
        )
    events[pl.ds(end, tile), :] = jnp.zeros((tile, width), events.dtype)

    row = lax.broadcasted_iota(jnp.int32, (length, length), 0)
    col = lax.broadcasted_iota(jnp.int32, (length, length), 1)
    rate = logit_scale * math.log2(math.e)

    lines = tile // length

    def one_tile(t):
        opening = isinstance(t, int)
        first, strip = t * tile, t * lines
        if not opening:
            first = pl.multiple_of(first, tile)
        item_id = lax.broadcasted_iota(jnp.int32, (items, tile), 0)
        x = events[pl.ds(first, tile), :].astype(jnp.float32)
        center, spread = center_and_spread(x)
        half_normed = (center * (0.5 * lax.rsqrt(spread + 1e-05))).astype(jnp.bfloat16)
        gate, values, query, keys = [
            half_silu(
                jnp.dot(
                    half_normed, w_in[:, part * width : (part + 1) * width],
                    preferred_element_type=jnp.float32,
                )
            ).astype(jnp.bfloat16)
            for part in range(4)
        ]
        key[pl.ds(first + length, tile), :] = keys
        value[pl.ds(first + length, tile), :] = values
        mixed = []
        for k in range(lines):
            base = first + k * length
            if not opening:
                base = pl.multiple_of(base, length)
            start = starts_ref[pl.ds(base, length), :]
            here = packed_tgt[pl.ds(strip + k + 1, 1), :] >= 0
            keep = (col <= row) & (base + col >= start) & here
            sources, seen = pl.ds(base + length, length), slice(length, 2 * length)
            if not (opening and k == 0):
                ahead = packed_tgt[pl.ds(strip + k, 1), :] >= 0
                keep = jnp.concatenate([(base - length + col >= start) & ahead, keep], axis=1)
                sources, seen = pl.ds(base, 2 * length), slice(0, 2 * length)
            by_head = []
            for h in range(heads):
                cols = slice(h * hdim, (h + 1) * hdim)
                scores = lax.dot_general(
                    query[k * length : (k + 1) * length, cols], key[sources, cols], contract_last,
                    preferred_element_type=jnp.float32,
                )
                attn = half_silu(scores * (0.5 / math.sqrt(hdim)) + bias[h, :, seen])
                attn = jnp.where(keep, attn, 0.0).astype(jnp.bfloat16)
                by_head.append(jnp.dot(attn, value[sources, cols], preferred_element_type=jnp.float32))
            mixed.append(jnp.concatenate(by_head, axis=1))
        center, spread = center_and_spread(jnp.concatenate(mixed, axis=0))
        normed = center * lax.rsqrt(spread + 1e-05)
        gated = (normed * gate.astype(jnp.float32)).astype(jnp.bfloat16)
        out = x + jnp.dot(gated, w_out[...], preferred_element_type=jnp.float32)
        out = out.astype(jnp.bfloat16).astype(jnp.float32)
        square = jnp.sum(out * out, axis=-1, keepdims=True)
        queries = (out * lax.rsqrt(square + 1e-06)).astype(jnp.bfloat16)

        target = jnp.concatenate(
            [packed_tgt[pl.ds(strip + k + 1, 1), :] for k in range(lines)], axis=1
        )
        total = jnp.zeros((1, tile), jnp.float32)
        target_dot = jnp.zeros((1, tile), jnp.float32)
        for j in range(blocks):
            dots = lax.dot_general(
                unit_ref[j], queries, contract_last, preferred_element_type=jnp.float32
            )
            exps = jnp.exp2(dots * rate - rate)
            exp_ref[j] = exps
            total += jnp.sum(exps, axis=0, keepdims=True)
            hit = item_id == target - j * items
            target_dot += jnp.sum(jnp.where(hit, dots, 0.0), axis=0, keepdims=True)
        loss = logit_scale + jnp.log(total) - logit_scale * target_dot
        for k in range(lines):
            packed_loss[pl.ds(strip + k, 1), :] = loss[:, k * length : (k + 1) * length]
        share = jnp.where(target >= 0, 1.0 / total, 0.0)
        for j in range(blocks):
            hit = item_id == target - j * items
            left = exp_ref[j] * share - jnp.where(hit, 1.0, 0.0)
            residual[j] = left.astype(jnp.bfloat16)
        before = sums_in if opening else sums
        for j in range(blocks):
            part = jnp.dot(residual[j], queries, preferred_element_type=jnp.float32)
            sums[j] = part if before is None else before[j] + part

    def later_tile(t, _):
        one_tile(t)
        return 0

    one_tile(0)
    lax.fori_loop(1, tiles, later_tile, 0)

    for u in range(per_step):
        line, turn = starts[u] // length, lax.rem(starts[u], length)
        back = lax.rem(length - turn, length)
        near = pltpu.roll(packed_loss[pl.ds(line, 1), :], back, 1)
        rest = pltpu.roll(packed_loss[pl.ds(line + 1, 1), :], back, 1)
        loss = jnp.where(place < length - turn, near, rest)
        loss_ref[pl.ds(spots[u], 1), :] = jnp.where(place < lens[u], loss, 0.0)


def step_scratch(places, length, width, blocks, items):
    rows = -(-min(len(places), 8) * length // tile) * tile
    lines = -(-(rows // length + 2) // 8) * 8
    return [
        pltpu.VMEM((blocks, items, tile), jnp.float32),
        pltpu.VMEM((blocks, items, tile), jnp.bfloat16),
        pltpu.VMEM((rows + tile, width), jnp.bfloat16),
        pltpu.VMEM((rows + tile, length), jnp.int32),
        pltpu.VMEM((length + rows + tile, width), jnp.bfloat16),
        pltpu.VMEM((length + rows + tile, width), jnp.bfloat16),
        pltpu.VMEM((lines, length), jnp.int32),
        pltpu.VMEM((lines, length), jnp.float32),
    ]


scalars = pl.BlockSpec(memory_space=pltpu.SMEM)
whole = pl.BlockSpec(memory_space=pltpu.VMEM)
far_off = pl.BlockSpec(memory_space=pltpu.HBM)


def first_call(ids, places, users, packed, units, w_in, w_out, rel_bias):
    heads, length = rel_bias.shape
    width, (blocks, items, _) = w_out.shape[0], units.shape
    return pl.pallas_call(
        functools.partial(first_kernel, places),
        in_specs=[scalars] + [far_off] * 3 + [whole] * (1 + len(places)),
        out_specs=[whole] * 3,
        scratch_shapes=[
            pltpu.VMEM(w_in.shape, jnp.bfloat16),
            pltpu.VMEM(w_out.shape, jnp.bfloat16),
            pltpu.VMEM(rel_bias.shape, jnp.float32),
            pltpu.SemaphoreType.DMA((3,)),
        ]
        + step_scratch(places, length, width, blocks, items),
        out_shape=[
            pltpu.VMEM((users, length), jnp.float32),
            pltpu.VMEM((blocks, items, width), jnp.float32),
            pltpu.VMEM((heads, length, 2 * length), jnp.float32),
        ],
        compiler_params=pltpu.CompilerParams(vmem_limit_bytes=24 * 1024 * 1024),
        name="first_users",
    )(
        ids, *[in_hbm(array) for array in (w_in, w_out, rel_bias)], in_vmem(units),
        *[in_vmem(array) for array in packed],
    )


def second_call(ids, places, packed, units, w_in, w_out, loss, sums, bias):
    blocks, items, width = sums.shape
    length = bias.shape[1]
    arrays = [w_in, w_out, bias, units, loss, sums, *packed]
    return pl.pallas_call(
        functools.partial(second_kernel, places),
        in_specs=[scalars] + [whole] * len(arrays),
        out_specs=[whole] * 5,
        scratch_shapes=[pltpu.VMEM(sums.shape, jnp.float32)]
        + step_scratch(places, length, width, blocks, items),
        out_shape=[jax.ShapeDtypeStruct(loss.shape, jnp.float32)]
        + [pltpu.VMEM((items, width), jnp.float32)] * 2
        + [pltpu.VMEM((items, width), jnp.bfloat16)] * 2,
        compiler_params=pltpu.CompilerParams(vmem_limit_bytes=24 * 1024 * 1024),
        name="second_users",
    )(ids, *[in_vmem(array) for array in arrays])


def shards(histories, lengths, targets, send_list, w_in, w_out, rel_bias, item_pool):
    user_count = histories.shape[0]
    groups, blocks = lax.axis_size("dp"), lax.axis_size("blk")
    slots = user_count // groups
    group, mine = lax.axis_index("dp").astype(jnp.int32), lax.axis_index("blk").astype(jnp.int32)

    near = sorted({0, 1, groups - 1, 2 % groups}, key=lambda shift: (shift != 0, shift == 2))
    others = [shift for shift in range(groups) if shift not in near]
    order = near + sorted(others, key=lambda shift: abs(shift - groups / 2))
    work = [(shift, slot) for shift in order for slot in range(slots)]
    *packed, units = pack(
        histories, lengths, targets, send_list, item_pool, work, groups, group.reshape(1), blocks
    )
    half = user_count // 2
    packed = [
        users if shift == 0 else from_behind(users, "dp", shift) for users, (shift, _) in zip(packed, work)
    ]
    units = lax.all_to_all(units, "blk", split_axis=0, concat_axis=0, tiled=True)

    pool_float = item_pool.astype(jnp.float32)
    item_norm = jnp.sqrt(jnp.sum(pool_float * pool_float, axis=-1, keepdims=True) + 1e-06)
    unit_rows = pool_float / item_norm

    came = [((group - shift) % groups) * slots + slot for shift, slot in work]
    ids = jnp.stack([mine, mine ^ 2, mine ^ 1, mine ^ 3, *came])
    order = tuple(range(user_count))
    loss, sums, bias = first_call(
        ids, order[:half], user_count, packed[:half], units, w_in, w_out, rel_bias
    )
    row_loss, own, over, side, far = second_call(
        ids, order[half:], packed[half:], units, w_in, w_out, loss, sums, bias
    )
    over = over + swap(far, "blk", 1).astype(jnp.float32)
    own = own + swap(side, "blk", 1).astype(jnp.float32)
    item_sum = logit_scale * (own + swap(over.astype(jnp.bfloat16), "blk", 2).astype(jnp.float32))
    pool_grad = (
        item_sum - unit_rows * jnp.sum(unit_rows * item_sum, axis=-1, keepdims=True)
    ) / item_norm
    return (row_loss, pool_grad)


def solution(mesh):
    placed = (
        P(("dp", "blk"), None, None),
        P(("dp", "blk")),
        P(("dp", "blk"), None),
        P(("dp", "blk")),
        P(),
        P(),
        P(),
        P(("dp", "blk"), None),
    )
    return jax.shard_map(
        shards,
        mesh=mesh,
        in_specs=placed,
        out_specs=(P(("dp", "blk"), None), P(("dp", "blk"), None)),
        check_vma=False,
    )
```

```python
import functools
import math

import jax
import jax.numpy as jnp
from jax import lax
from jax.experimental import pallas as pl
from jax.experimental.pallas import tpu as pltpu
from jax.sharding import PartitionSpec as P

logit_scale = 20.0
contract_last = (((1,), (1,)), ((), ()))
tile = 256
chunk = 16
number_rows = 8


def swap(array, axis, bit):
    devices = lax.axis_size(axis)
    return lax.ppermute(array, axis, [(i, i ^ bit) for i in range(devices)])


def from_behind(array, axis, by):
    devices = lax.axis_size(axis)
    return lax.ppermute(array, axis, [(i, (i + by) % devices) for i in range(devices)])


def in_vmem(array):
    return pltpu.with_memory_space_constraint(array, pltpu.VMEM)


def in_hbm(array):
    return pltpu.with_memory_space_constraint(array, pltpu.HBM)


def half_silu(half):
    return half + half * jnp.tanh(half)


def center_and_spread(values):
    center = values - jnp.mean(values, axis=-1, keepdims=True)
    return center, jnp.mean(center * center, axis=-1, keepdims=True)


def pack_kernel(
    work, groups, group_ref, list_any, len_any, from_any, tgt_any, pool_any, *refs,
):
    users, length, width = from_any.shape
    to_refs, unit_any = refs[:users], refs[users]
    entries, lens, targets, pool, unit, sems, in_sems = refs[users + 1 :]
    pieces = width // length
    small = [
        pltpu.make_async_copy(source, target, sems.at[k])
        for k, (source, target) in enumerate(
            ((list_any, entries), (len_any, lens), (tgt_any, targets), (pool_any, pool))
        )
    ]
    for copy in small:
        copy.start()
    small[0].wait()
    slots = users // groups
    order = [entries[(group_ref[0] + shift) % groups * slots + slot] for shift, slot in work]
    copies_in = [
        pltpu.make_async_copy(
            from_any.at[order[k], :, pl.ds(c * length, length)],
            to_refs[k].at[pl.ds(c * length, length)],
            in_sems.at[k, c],
        )
        for k in range(users)
        for c in range(pieces)
    ]
    for copy in copies_in:
        copy.start()
    small[3].wait()
    rows = pool[...].astype(jnp.float32)
    unit[...] = (rows * lax.rsqrt(jnp.sum(rows * rows, axis=-1, keepdims=True) + 1e-06)).astype(jnp.bfloat16)
    units_out = [
        pltpu.make_async_copy(unit, unit_any.at[k], sems.at[4 + k]) for k in range(unit_any.shape[0])
    ]
    for copy in units_out:
        copy.start()
    small[1].wait()
    small[2].wait()
    row = lax.broadcasted_iota(jnp.int32, (number_rows, length), 0)
    for k in range(users):
        target = targets[pl.ds(order[k], 1), :]
        numbers = jnp.where(row == 0, lens[order[k]], jnp.where(row == 1, target // 256, target % 256))
        to_refs[k][width:, :] = numbers.astype(jnp.float32).astype(jnp.bfloat16)
    for copy in copies_in + units_out:
        copy.wait()


def pack(histories, lengths, targets, entries, item_pool, work, groups, group, blocks):
    users, length, width = histories.shape
    shape = (width + number_rows, length)
    hbm = pl.BlockSpec(memory_space=pltpu.HBM)
    return pl.pallas_call(
        functools.partial(pack_kernel, work, groups),
        in_specs=[pl.BlockSpec(memory_space=pltpu.SMEM)] + [hbm] * 5,
        out_specs=[pl.BlockSpec(memory_space=pltpu.VMEM)] * users + [hbm],
        scratch_shapes=[
            pltpu.SMEM(entries.shape, jnp.int32),
            pltpu.SMEM(lengths.shape, jnp.int32),
            pltpu.VMEM(targets.shape, jnp.int32),
            pltpu.VMEM(item_pool.shape, jnp.bfloat16),
            pltpu.VMEM(item_pool.shape, jnp.bfloat16),
            pltpu.SemaphoreType.DMA((4 + blocks,)),
            pltpu.SemaphoreType.DMA((users, width // length)),
        ],
        out_shape=[pltpu.VMEM(shape, jnp.bfloat16)] * users
        + [pltpu.HBM((blocks,) + item_pool.shape, jnp.bfloat16)],
        compiler_params=pltpu.CompilerParams(vmem_limit_bytes=16 * 1024 * 1024),
        name="pack",
    )(group, *[in_hbm(array) for array in (entries, lengths, histories, targets, item_pool)])


def users_kernel(places, id_ref, x_refs, w_in, w_out, unit_ref, sums, loss_ref, bias, scratch):
    blocks = unit_ref.shape[0]
    for at in range(0, len(places), 8):
        users_step(
            x_refs[at : at + 8], [id_ref[blocks + k] for k in places[at : at + 8]],
            w_in, w_out, unit_ref, sums, loss_ref, bias, *scratch,
        )


def first_kernel(places, id_ref, w_in_any, w_out_any, rel_any, unit_ref, *refs):
    count = len(places)
    x_refs, refs = refs[:count], refs[count:]
    loss_ref, sums, bias, refs = refs[0], refs[1], refs[2], refs[3:]
    w_in, w_out, rel, sems = refs[:4]
    heads, length = rel.shape
    moves = [(rel_any, rel), (w_in_any, w_in), (w_out_any, w_out)]
    copies = [pltpu.make_async_copy(*move, sems.at[k]) for k, move in enumerate(moves)]
    for copy in copies:
        copy.start()
    loss_ref[...] = jnp.zeros_like(loss_ref)
    sums[...] = jnp.zeros_like(sums)
    copies[0].wait()
    for h in range(heads):
        wide = jnp.broadcast_to(0.5 * rel[h : h + 1, :], (length, length))
        turned = pltpu.roll(wide, 0, 1, stride=1, stride_axis=0).T
        bias[h] = jnp.concatenate([turned, turned], axis=1)
    for copy in copies[1:]:
        copy.wait()
    users_kernel(places, id_ref, x_refs, w_in, w_out, unit_ref, sums, loss_ref, bias, refs[4:])


def second_kernel(places, id_ref, w_in, w_out, bias, unit_ref, loss_in, sums_in, *refs):
    count = len(places)
    x_refs, refs = refs[:count], refs[count:]
    loss_ref, out_refs, sums, scratch = refs[0], refs[1:5], refs[5], refs[6:]
    loss_ref[...] = loss_in[...]
    sums[...] = sums_in[...]
    users_kernel(places, id_ref, x_refs, w_in, w_out, unit_ref, sums, loss_ref, bias, scratch)
    for k, ref in enumerate(out_refs):
        ref[...] = sums[id_ref[k]].astype(ref.dtype)


def users_step(
    x_refs, spots, w_in, w_out, unit_ref, sums, loss_ref, bias,
    exp_ref, residual, events, starts_ref, key, value, packed_tgt, packed_loss,
):
    heads, length, _ = bias.shape
    width = w_out.shape[0]
    hdim = width // heads
    blocks, items, _ = unit_ref.shape
    per_step = len(x_refs)

    digits = [ref[width:, :].astype(jnp.float32) for ref in x_refs]
    lens = [jnp.max(digit[:1, :]).astype(jnp.int32) for digit in digits]
    starts, end = [], 0
    for u in range(per_step):
        starts.append(pl.multiple_of(end, chunk) if u else 0)
        end = end + (lens[u] + chunk - 1) // chunk * chunk
    end = pl.multiple_of(end, chunk)
    tiles = (end + tile - 1) // tile

    place = lax.broadcasted_iota(jnp.int32, (1, length), 1)
    packed_tgt[...] = jnp.full_like(packed_tgt, -1)
    key[:length, :] = jnp.zeros((length, width), key.dtype)
    value[:length, :] = jnp.zeros((length, width), value.dtype)
    for u in range(per_step):
        starts_ref[pl.ds(starts[u], length), :] = jnp.full((length, length), starts[u], jnp.int32)
    for u in range(per_step):
        for c in range(0, width, length):
            events[pl.ds(starts[u], length), c : c + length] = x_refs[u][c : c + length, :]
        target = digits[u][1:2, :] * 256.0 + digits[u][2:3, :]
        wanted = jnp.where(place < lens[u], target.astype(jnp.int32), -1)
        line, turn = starts[u] // length + 1, lax.rem(starts[u], length)
        turned = pltpu.roll(wanted, turn, 1)
        packed_tgt[pl.ds(line, 1), :] = jnp.where(place >= turn, turned, packed_tgt[pl.ds(line, 1), :])
        packed_tgt[pl.ds(line + 1, 1), :] = jnp.where(
            place < turn, turned, packed_tgt[pl.ds(line + 1, 1), :]
        )
    events[pl.ds(end, tile), :] = jnp.zeros((tile, width), events.dtype)

    row = lax.broadcasted_iota(jnp.int32, (length, length), 0)
    col = lax.broadcasted_iota(jnp.int32, (length, length), 1)
    rate = logit_scale * math.log2(math.e)

    lines = tile // length

    def one_tile(t, _):
        first, strip = pl.multiple_of(t * tile, tile), t * lines
        item_id = lax.broadcasted_iota(jnp.int32, (items, tile), 0)
        x = events[pl.ds(first, tile), :].astype(jnp.float32)
        center, spread = center_and_spread(x)
        half_normed = (center * (0.5 * lax.rsqrt(spread + 1e-05))).astype(jnp.bfloat16)
        gate, values, query, keys = [
            half_silu(
                jnp.dot(
                    half_normed, w_in[:, part * width : (part + 1) * width],
                    preferred_element_type=jnp.float32,
                )
            ).astype(jnp.bfloat16)
            for part in range(4)
        ]
        key[pl.ds(first + length, tile), :] = keys
        value[pl.ds(first + length, tile), :] = values
        mixed = []
        for k in range(lines):
            base = pl.multiple_of(first + k * length, length)
            sources = pl.ds(base, 2 * length)
            start = starts_ref[pl.ds(base, length), :]
            ahead = packed_tgt[pl.ds(strip + k, 1), :] >= 0
            here = packed_tgt[pl.ds(strip + k + 1, 1), :] >= 0
            keep_ahead = (base - length + col >= start) & ahead
            keep_here = (col <= row) & (base + col >= start) & here
            keep = jnp.concatenate([keep_ahead, keep_here], axis=1)
            by_head = []
            for h in range(heads):
                cols = slice(h * hdim, (h + 1) * hdim)
                scores = lax.dot_general(
                    query[k * length : (k + 1) * length, cols], key[sources, cols], contract_last,
                    preferred_element_type=jnp.float32,
                )
                attn = half_silu(scores * (0.5 / math.sqrt(hdim)) + bias[h])
                attn = jnp.where(keep, attn, 0.0).astype(jnp.bfloat16)
                by_head.append(jnp.dot(attn, value[sources, cols], preferred_element_type=jnp.float32))
            mixed.append(jnp.concatenate(by_head, axis=1))
        center, spread = center_and_spread(jnp.concatenate(mixed, axis=0))
        normed = center * lax.rsqrt(spread + 1e-05)
        gated = (normed * gate.astype(jnp.float32)).astype(jnp.bfloat16)
        out = x + jnp.dot(gated, w_out[...], preferred_element_type=jnp.float32)
        out = out.astype(jnp.bfloat16).astype(jnp.float32)
        square = jnp.sum(out * out, axis=-1, keepdims=True)
        queries = (out * lax.rsqrt(square + 1e-06)).astype(jnp.bfloat16)

        target = jnp.concatenate(
            [packed_tgt[pl.ds(strip + k + 1, 1), :] for k in range(lines)], axis=1
        )
        total = jnp.zeros((1, tile), jnp.float32)
        target_dot = jnp.zeros((1, tile), jnp.float32)
        for j in range(blocks):
            dots = lax.dot_general(
                unit_ref[j], queries, contract_last, preferred_element_type=jnp.float32
            )
            exps = jnp.exp2(dots * rate - rate)
            exp_ref[j] = exps
            total += jnp.sum(exps, axis=0, keepdims=True)
            hit = item_id == target - j * items
            target_dot += jnp.sum(jnp.where(hit, dots, 0.0), axis=0, keepdims=True)
        loss = logit_scale + jnp.log(total) - logit_scale * target_dot
        for k in range(lines):
            packed_loss[pl.ds(strip + k, 1), :] = loss[:, k * length : (k + 1) * length]
        share = jnp.where(target >= 0, 1.0 / total, 0.0)
        for j in range(blocks):
            hit = item_id == target - j * items
            left = exp_ref[j] * share - jnp.where(hit, 1.0, 0.0)
            residual[j] = left.astype(jnp.bfloat16)
        for j in range(blocks):
            sums[j] += jnp.dot(residual[j], queries, preferred_element_type=jnp.float32)
        return 0

    lax.fori_loop(0, tiles, one_tile, 0)

    for u in range(per_step):
        line, turn = starts[u] // length, lax.rem(starts[u], length)
        back = lax.rem(length - turn, length)
        near = pltpu.roll(packed_loss[pl.ds(line, 1), :], back, 1)
        rest = pltpu.roll(packed_loss[pl.ds(line + 1, 1), :], back, 1)
        loss = jnp.where(place < length - turn, near, rest)
        loss_ref[pl.ds(spots[u], 1), :] = jnp.where(place < lens[u], loss, 0.0)


def step_scratch(places, length, width, blocks, items):
    rows = -(-min(len(places), 8) * length // tile) * tile
    lines = -(-(rows // length + 2) // 8) * 8
    return [
        pltpu.VMEM((blocks, items, tile), jnp.float32),
        pltpu.VMEM((blocks, items, tile), jnp.bfloat16),
        pltpu.VMEM((rows + tile, width), jnp.bfloat16),
        pltpu.VMEM((rows + tile, length), jnp.int32),
        pltpu.VMEM((length + rows + tile, width), jnp.bfloat16),
        pltpu.VMEM((length + rows + tile, width), jnp.bfloat16),
        pltpu.VMEM((lines, length), jnp.int32),
        pltpu.VMEM((lines, length), jnp.float32),
    ]


scalars = pl.BlockSpec(memory_space=pltpu.SMEM)
whole = pl.BlockSpec(memory_space=pltpu.VMEM)
far_off = pl.BlockSpec(memory_space=pltpu.HBM)


def first_call(ids, places, users, packed, units, w_in, w_out, rel_bias):
    heads, length = rel_bias.shape
    width, (blocks, items, _) = w_out.shape[0], units.shape
    return pl.pallas_call(
        functools.partial(first_kernel, places),
        in_specs=[scalars] + [far_off] * 3 + [whole] * (1 + len(places)),
        out_specs=[whole] * 3,
        scratch_shapes=[
            pltpu.VMEM(w_in.shape, jnp.bfloat16),
            pltpu.VMEM(w_out.shape, jnp.bfloat16),
            pltpu.VMEM(rel_bias.shape, jnp.float32),
            pltpu.SemaphoreType.DMA((3,)),
        ]
        + step_scratch(places, length, width, blocks, items),
        out_shape=[
            pltpu.VMEM((users, length), jnp.float32),
            pltpu.VMEM((blocks, items, width), jnp.float32),
            pltpu.VMEM((heads, length, 2 * length), jnp.float32),
        ],
        compiler_params=pltpu.CompilerParams(vmem_limit_bytes=24 * 1024 * 1024),
        name="first_users",
    )(
        ids, *[in_hbm(array) for array in (w_in, w_out, rel_bias)], in_vmem(units),
        *[in_vmem(array) for array in packed],
    )


def second_call(ids, places, packed, units, w_in, w_out, loss, sums, bias):
    blocks, items, width = sums.shape
    length = bias.shape[1]
    arrays = [w_in, w_out, bias, units, loss, sums, *packed]
    return pl.pallas_call(
        functools.partial(second_kernel, places),
        in_specs=[scalars] + [whole] * len(arrays),
        out_specs=[whole] * 5,
        scratch_shapes=[pltpu.VMEM(sums.shape, jnp.float32)]
        + step_scratch(places, length, width, blocks, items),
        out_shape=[jax.ShapeDtypeStruct(loss.shape, jnp.float32)]
        + [pltpu.VMEM((items, width), jnp.float32)] * 2
        + [pltpu.VMEM((items, width), jnp.bfloat16)] * 2,
        compiler_params=pltpu.CompilerParams(vmem_limit_bytes=24 * 1024 * 1024),
        name="second_users",
    )(ids, *[in_vmem(array) for array in arrays])


def shards(histories, lengths, targets, send_list, w_in, w_out, rel_bias, item_pool):
    user_count = histories.shape[0]
    groups, blocks = lax.axis_size("dp"), lax.axis_size("blk")
    slots = user_count // groups
    group, mine = lax.axis_index("dp").astype(jnp.int32), lax.axis_index("blk").astype(jnp.int32)

    near = sorted({0, 1, groups - 1, 2 % groups}, key=lambda shift: (shift != 0, shift == 2))
    others = [shift for shift in range(groups) if shift not in near]
    order = near + sorted(others, key=lambda shift: abs(shift - groups / 2))
    work = [(shift, slot) for shift in order for slot in range(slots)]
    *packed, units = pack(
        histories, lengths, targets, send_list, item_pool, work, groups, group.reshape(1), blocks
    )
    half = user_count // 2
    packed = [
        users if shift == 0 else from_behind(users, "dp", shift) for users, (shift, _) in zip(packed, work)
    ]
    units = lax.all_to_all(units, "blk", split_axis=0, concat_axis=0, tiled=True)

    pool_float = item_pool.astype(jnp.float32)
    item_norm = jnp.sqrt(jnp.sum(pool_float * pool_float, axis=-1, keepdims=True) + 1e-06)
    unit_rows = pool_float / item_norm

    came = [((group - shift) % groups) * slots + slot for shift, slot in work]
    ids = jnp.stack([mine, mine ^ 2, mine ^ 1, mine ^ 3, *came])
    order = tuple(range(user_count))
    loss, sums, bias = first_call(
        ids, order[:half], user_count, packed[:half], units, w_in, w_out, rel_bias
    )
    row_loss, own, over, side, far = second_call(
        ids, order[half:], packed[half:], units, w_in, w_out, loss, sums, bias
    )
    over = over + swap(far, "blk", 1).astype(jnp.float32)
    own = own + swap(side, "blk", 1).astype(jnp.float32)
    item_sum = logit_scale * (own + swap(over.astype(jnp.bfloat16), "blk", 2).astype(jnp.float32))
    pool_grad = (
        item_sum - unit_rows * jnp.sum(unit_rows * item_sum, axis=-1, keepdims=True)
    ) / item_norm
    return (row_loss, pool_grad)


def solution(mesh):
    placed = (
        P(("dp", "blk"), None, None),
        P(("dp", "blk")),
        P(("dp", "blk"), None),
        P(("dp", "blk")),
        P(),
        P(),
        P(),
        P(("dp", "blk"), None),
    )
    return jax.shard_map(
        shards,
        mesh=mesh,
        in_specs=placed,
        out_specs=(P(("dp", "blk"), None), P(("dp", "blk"), None)),
        check_vma=False,
    )
```

```python
import functools
import math

import jax
import jax.numpy as jnp
from jax import lax
from jax.experimental import pallas as pl
from jax.experimental.pallas import tpu as pltpu
from jax.sharding import PartitionSpec as P

logit_scale = 20.0
contract_last = (((1,), (1,)), ((), ()))
tile = 256
chunk = 16
number_rows = 8


def swap(array, axis, bit):
    devices = lax.axis_size(axis)
    return lax.ppermute(array, axis, [(i, i ^ bit) for i in range(devices)])


def from_behind(array, axis, by):
    devices = lax.axis_size(axis)
    return lax.ppermute(array, axis, [(i, (i + by) % devices) for i in range(devices)])


def in_vmem(array):
    return pltpu.with_memory_space_constraint(array, pltpu.VMEM)


def in_hbm(array):
    return pltpu.with_memory_space_constraint(array, pltpu.HBM)


def half_silu(half):
    return half + half * jnp.tanh(half)


def center_and_spread(values):
    center = values - jnp.mean(values, axis=-1, keepdims=True)
    return center, jnp.mean(center * center, axis=-1, keepdims=True)


def pack_kernel(
    work, groups, list_any, len_any, from_any, tgt_any, pool_any, *refs,
):
    users, length, width = from_any.shape
    to_refs, unit_any = refs[:users], refs[users]
    entries, lens, targets, pool, unit, sems, in_sems = refs[users + 1 :]
    pieces = width // length
    small = [
        pltpu.make_async_copy(source, target, sems.at[k])
        for k, (source, target) in enumerate(
            ((list_any, entries), (len_any, lens), (tgt_any, targets), (pool_any, pool))
        )
    ]
    for copy in small:
        copy.start()
    small[0].wait()
    slots = users // groups
    group = lax.axis_index("dp")
    order = [entries[lax.rem(group + shift, groups) * slots + slot] for shift, slot in work]
    copies_in = [
        pltpu.make_async_copy(
            from_any.at[order[k], :, pl.ds(c * length, length)],
            to_refs[k].at[pl.ds(c * length, length)],
            in_sems.at[k, c],
        )
        for k in range(users)
        for c in range(pieces)
    ]
    for copy in copies_in:
        copy.start()
    small[3].wait()
    rows = pool[...].astype(jnp.float32)
    unit[...] = (rows * lax.rsqrt(jnp.sum(rows * rows, axis=-1, keepdims=True) + 1e-06)).astype(jnp.bfloat16)
    units_out = [
        pltpu.make_async_copy(unit, unit_any.at[k], sems.at[4 + k]) for k in range(unit_any.shape[0])
    ]
    for copy in units_out:
        copy.start()
    small[1].wait()
    small[2].wait()
    row = lax.broadcasted_iota(jnp.int32, (number_rows, length), 0)
    for k in range(users):
        target = targets[pl.ds(order[k], 1), :]
        numbers = jnp.where(row == 0, lens[order[k]], jnp.where(row == 1, target // 256, target % 256))
        to_refs[k][width:, :] = numbers.astype(jnp.float32).astype(jnp.bfloat16)
    for copy in copies_in + units_out:
        copy.wait()


def pack(histories, lengths, targets, entries, item_pool, work, groups, blocks):
    users, length, width = histories.shape
    shape = (width + number_rows, length)
    hbm = pl.BlockSpec(memory_space=pltpu.HBM)
    return pl.pallas_call(
        functools.partial(pack_kernel, work, groups),
        in_specs=[hbm] * 5,
        out_specs=[pl.BlockSpec(memory_space=pltpu.VMEM)] * users + [hbm],
        scratch_shapes=[
            pltpu.SMEM(entries.shape, jnp.int32),
            pltpu.SMEM(lengths.shape, jnp.int32),
            pltpu.VMEM(targets.shape, jnp.int32),
            pltpu.VMEM(item_pool.shape, jnp.bfloat16),
            pltpu.VMEM(item_pool.shape, jnp.bfloat16),
            pltpu.SemaphoreType.DMA((4 + blocks,)),
            pltpu.SemaphoreType.DMA((users, width // length)),
        ],
        out_shape=[pltpu.VMEM(shape, jnp.bfloat16)] * users
        + [pltpu.HBM((blocks,) + item_pool.shape, jnp.bfloat16)],
        compiler_params=pltpu.CompilerParams(vmem_limit_bytes=16 * 1024 * 1024),
        name="pack",
    )(*[in_hbm(array) for array in (entries, lengths, histories, targets, item_pool)])


def users_kernel(work, groups, x_refs, w_in, w_out, unit_ref, sums, loss_ref, bias, scratch):
    slots = loss_ref.shape[0] // groups
    group = lax.axis_index("dp")
    spots = [lax.rem(group + groups - shift, groups) * slots + slot for shift, slot in work]
    for at in range(0, len(work), 8):
        users_step(
            x_refs[at : at + 8], spots[at : at + 8],
            w_in, w_out, unit_ref, sums, loss_ref, bias, *scratch,
        )


def first_kernel(work, groups, w_in_any, w_out_any, rel_any, unit_ref, *refs):
    count = len(work)
    x_refs, refs = refs[:count], refs[count:]
    loss_ref, sums, bias, refs = refs[0], refs[1], refs[2], refs[3:]
    w_in, w_out, rel, sems = refs[:4]
    heads, length = rel.shape
    moves = [(rel_any, rel), (w_in_any, w_in), (w_out_any, w_out)]
    copies = [pltpu.make_async_copy(*move, sems.at[k]) for k, move in enumerate(moves)]
    for copy in copies:
        copy.start()
    loss_ref[...] = jnp.zeros_like(loss_ref)
    sums[...] = jnp.zeros_like(sums)
    copies[0].wait()
    for h in range(heads):
        wide = jnp.broadcast_to(0.5 * rel[h : h + 1, :], (length, length))
        turned = pltpu.roll(wide, 0, 1, stride=1, stride_axis=0).T
        bias[h] = jnp.concatenate([turned, turned], axis=1)
    for copy in copies[1:]:
        copy.wait()
    users_kernel(work, groups, x_refs, w_in, w_out, unit_ref, sums, loss_ref, bias, refs[4:])


def second_kernel(work, groups, w_in, w_out, bias, unit_ref, loss_in, sums_in, *refs):
    count = len(work)
    x_refs, refs = refs[:count], refs[count:]
    loss_ref, out_refs, sums, scratch = refs[0], refs[1:5], refs[5], refs[6:]
    loss_ref[...] = loss_in[...]
    sums[...] = sums_in[...]
    users_kernel(work, groups, x_refs, w_in, w_out, unit_ref, sums, loss_ref, bias, scratch)
    mine = lax.axis_index("blk")
    for bits, ref in zip((0, 2, 1, 3), out_refs):
        ref[...] = sums[mine ^ bits].astype(ref.dtype)


def users_step(
    x_refs, spots, w_in, w_out, unit_ref, sums, loss_ref, bias,
    exp_ref, residual, events, starts_ref, key, value, packed_tgt, packed_loss,
):
    heads, length, _ = bias.shape
    width = w_out.shape[0]
    hdim = width // heads
    blocks, items, _ = unit_ref.shape
    per_step = len(x_refs)

    digits = [ref[width:, :].astype(jnp.float32) for ref in x_refs]
    lens = [jnp.max(digit[:1, :]).astype(jnp.int32) for digit in digits]
    starts, end = [], 0
    for u in range(per_step):
        starts.append(pl.multiple_of(end, chunk) if u else 0)
        end = end + (lens[u] + chunk - 1) // chunk * chunk
    end = pl.multiple_of(end, chunk)
    tiles = (end + tile - 1) // tile

    place = lax.broadcasted_iota(jnp.int32, (1, length), 1)
    packed_tgt[...] = jnp.full_like(packed_tgt, -1)
    key[:length, :] = jnp.zeros((length, width), key.dtype)
    value[:length, :] = jnp.zeros((length, width), value.dtype)
    for u in range(per_step):
        starts_ref[pl.ds(starts[u], length), :] = jnp.full((length, length), starts[u], jnp.int32)
    for u in range(per_step):
        for c in range(0, width, length):
            events[pl.ds(starts[u], length), c : c + length] = x_refs[u][c : c + length, :]
        target = digits[u][1:2, :] * 256.0 + digits[u][2:3, :]
        wanted = jnp.where(place < lens[u], target.astype(jnp.int32), -1)
        line, turn = starts[u] // length + 1, lax.rem(starts[u], length)
        turned = pltpu.roll(wanted, turn, 1)
        packed_tgt[pl.ds(line, 1), :] = jnp.where(place >= turn, turned, packed_tgt[pl.ds(line, 1), :])
        packed_tgt[pl.ds(line + 1, 1), :] = jnp.where(
            place < turn, turned, packed_tgt[pl.ds(line + 1, 1), :]
        )
    events[pl.ds(end, tile), :] = jnp.zeros((tile, width), events.dtype)

    row = lax.broadcasted_iota(jnp.int32, (length, length), 0)
    col = lax.broadcasted_iota(jnp.int32, (length, length), 1)
    rate = logit_scale * math.log2(math.e)

    lines = tile // length

    def one_tile(t, _):
        first, strip = pl.multiple_of(t * tile, tile), t * lines
        item_id = lax.broadcasted_iota(jnp.int32, (items, tile), 0)
        x = events[pl.ds(first, tile), :].astype(jnp.float32)
        center, spread = center_and_spread(x)
        half_normed = (center * (0.5 * lax.rsqrt(spread + 1e-05))).astype(jnp.bfloat16)
        gate, values, query, keys = [
            half_silu(
                jnp.dot(
                    half_normed, w_in[:, part * width : (part + 1) * width],
                    preferred_element_type=jnp.float32,
                )
            ).astype(jnp.bfloat16)
            for part in range(4)
        ]
        key[pl.ds(first + length, tile), :] = keys
        value[pl.ds(first + length, tile), :] = values
        mixed = []
        for k in range(lines):
            base = pl.multiple_of(first + k * length, length)
            sources = pl.ds(base, 2 * length)
            start = starts_ref[pl.ds(base, length), :]
            ahead = packed_tgt[pl.ds(strip + k, 1), :] >= 0
            here = packed_tgt[pl.ds(strip + k + 1, 1), :] >= 0
            keep_ahead = (base - length + col >= start) & ahead
            keep_here = (col <= row) & (base + col >= start) & here
            keep = jnp.concatenate([keep_ahead, keep_here], axis=1)
            by_head = []
            for h in range(heads):
                cols = slice(h * hdim, (h + 1) * hdim)
                scores = lax.dot_general(
                    query[k * length : (k + 1) * length, cols], key[sources, cols], contract_last,
                    preferred_element_type=jnp.float32,
                )
                attn = half_silu(scores * (0.5 / math.sqrt(hdim)) + bias[h])
                attn = jnp.where(keep, attn, 0.0).astype(jnp.bfloat16)
                by_head.append(jnp.dot(attn, value[sources, cols], preferred_element_type=jnp.float32))
            mixed.append(jnp.concatenate(by_head, axis=1))
        center, spread = center_and_spread(jnp.concatenate(mixed, axis=0))
        normed = center * lax.rsqrt(spread + 1e-05)
        gated = (normed * gate.astype(jnp.float32)).astype(jnp.bfloat16)
        out = x + jnp.dot(gated, w_out[...], preferred_element_type=jnp.float32)
        out = out.astype(jnp.bfloat16).astype(jnp.float32)
        square = jnp.sum(out * out, axis=-1, keepdims=True)
        queries = (out * lax.rsqrt(square + 1e-06)).astype(jnp.bfloat16)

        target = jnp.concatenate(
            [packed_tgt[pl.ds(strip + k + 1, 1), :] for k in range(lines)], axis=1
        )
        total = jnp.zeros((1, tile), jnp.float32)
        target_dot = jnp.zeros((1, tile), jnp.float32)
        for j in range(blocks):
            dots = lax.dot_general(
                unit_ref[j], queries, contract_last, preferred_element_type=jnp.float32
            )
            exps = jnp.exp2(dots * rate - rate)
            exp_ref[j] = exps
            total += jnp.sum(exps, axis=0, keepdims=True)
            hit = item_id == target - j * items
            target_dot += jnp.sum(jnp.where(hit, dots, 0.0), axis=0, keepdims=True)
        loss = logit_scale + jnp.log(total) - logit_scale * target_dot
        for k in range(lines):
            packed_loss[pl.ds(strip + k, 1), :] = loss[:, k * length : (k + 1) * length]
        share = jnp.where(target >= 0, 1.0 / total, 0.0)
        for j in range(blocks):
            hit = item_id == target - j * items
            left = exp_ref[j] * share - jnp.where(hit, 1.0, 0.0)
            residual[j] = left.astype(jnp.bfloat16)
        for j in range(blocks):
            sums[j] += jnp.dot(residual[j], queries, preferred_element_type=jnp.float32)
        return 0

    lax.fori_loop(0, tiles, one_tile, 0)

    for u in range(per_step):
        line, turn = starts[u] // length, lax.rem(starts[u], length)
        back = lax.rem(length - turn, length)
        near = pltpu.roll(packed_loss[pl.ds(line, 1), :], back, 1)
        rest = pltpu.roll(packed_loss[pl.ds(line + 1, 1), :], back, 1)
        loss = jnp.where(place < length - turn, near, rest)
        loss_ref[pl.ds(spots[u], 1), :] = jnp.where(place < lens[u], loss, 0.0)


def step_scratch(count, length, width, blocks, items):
    rows = -(-min(count, 8) * length // tile) * tile
    lines = -(-(rows // length + 2) // 8) * 8
    return [
        pltpu.VMEM((blocks, items, tile), jnp.float32),
        pltpu.VMEM((blocks, items, tile), jnp.bfloat16),
        pltpu.VMEM((rows + tile, width), jnp.bfloat16),
        pltpu.VMEM((rows + tile, length), jnp.int32),
        pltpu.VMEM((length + rows + tile, width), jnp.bfloat16),
        pltpu.VMEM((length + rows + tile, width), jnp.bfloat16),
        pltpu.VMEM((lines, length), jnp.int32),
        pltpu.VMEM((lines, length), jnp.float32),
    ]


whole = pl.BlockSpec(memory_space=pltpu.VMEM)
far_off = pl.BlockSpec(memory_space=pltpu.HBM)


def first_call(work, groups, users, packed, units, w_in, w_out, rel_bias):
    heads, length = rel_bias.shape
    width, (blocks, items, _) = w_out.shape[0], units.shape
    return pl.pallas_call(
        functools.partial(first_kernel, work, groups),
        in_specs=[far_off] * 3 + [whole] * (1 + len(work)),
        out_specs=[whole] * 3,
        scratch_shapes=[
            pltpu.VMEM(w_in.shape, jnp.bfloat16),
            pltpu.VMEM(w_out.shape, jnp.bfloat16),
            pltpu.VMEM(rel_bias.shape, jnp.float32),
            pltpu.SemaphoreType.DMA((3,)),
        ]
        + step_scratch(len(work), length, width, blocks, items),
        out_shape=[
            pltpu.VMEM((users, length), jnp.float32),
            pltpu.VMEM((blocks, items, width), jnp.float32),
            pltpu.VMEM((heads, length, 2 * length), jnp.float32),
        ],
        compiler_params=pltpu.CompilerParams(vmem_limit_bytes=24 * 1024 * 1024),
        name="first_users",
    )(
        *[in_hbm(array) for array in (w_in, w_out, rel_bias)], in_vmem(units),
        *[in_vmem(array) for array in packed],
    )


def second_call(work, groups, packed, units, w_in, w_out, loss, sums, bias):
    blocks, items, width = sums.shape
    length = bias.shape[1]
    arrays = [w_in, w_out, bias, units, loss, sums, *packed]
    return pl.pallas_call(
        functools.partial(second_kernel, work, groups),
        in_specs=[whole] * len(arrays),
        out_specs=[whole] * 5,
        scratch_shapes=[pltpu.VMEM(sums.shape, jnp.float32)]
        + step_scratch(len(work), length, width, blocks, items),
        out_shape=[pltpu.VMEM(loss.shape, jnp.float32)]
        + [pltpu.VMEM((items, width), jnp.float32)] * 2
        + [pltpu.VMEM((items, width), jnp.bfloat16)] * 2,
        compiler_params=pltpu.CompilerParams(vmem_limit_bytes=24 * 1024 * 1024),
        name="second_users",
    )(*[in_vmem(array) for array in arrays])


def shards(histories, lengths, targets, send_list, w_in, w_out, rel_bias, item_pool):
    user_count = histories.shape[0]
    groups, blocks = lax.axis_size("dp"), lax.axis_size("blk")
    slots = user_count // groups

    near = sorted({0, 1, groups - 1, 2 % groups}, key=lambda shift: (shift != 0, shift == 2))
    others = [shift for shift in range(groups) if shift not in near]
    order = near + sorted(others, key=lambda shift: abs(shift - groups / 2))
    work = [(shift, slot) for shift in order for slot in range(slots)]
    *packed, units = pack(
        histories, lengths, targets, send_list, item_pool, work, groups, blocks
    )
    half = user_count // 2
    packed = [
        users if shift == 0 else from_behind(users, "dp", shift) for users, (shift, _) in zip(packed, work)
    ]
    units = lax.all_to_all(units, "blk", split_axis=0, concat_axis=0, tiled=True)

    pool_float = item_pool.astype(jnp.float32)
    item_norm = jnp.sqrt(jnp.sum(pool_float * pool_float, axis=-1, keepdims=True) + 1e-06)
    unit_rows = pool_float / item_norm

    loss, sums, bias = first_call(
        work[:half], groups, user_count, packed[:half], units, w_in, w_out, rel_bias
    )
    row_loss, own, over, side, far = second_call(
        work[half:], groups, packed[half:], units, w_in, w_out, loss, sums, bias
    )
    over = over + swap(far, "blk", 1).astype(jnp.float32)
    own = own + swap(side, "blk", 1).astype(jnp.float32)
    item_sum = logit_scale * (own + swap(over.astype(jnp.bfloat16), "blk", 2).astype(jnp.float32))
    pool_grad = (
        item_sum - unit_rows * jnp.sum(unit_rows * item_sum, axis=-1, keepdims=True)
    ) / item_norm
    return (row_loss, pool_grad)


def solution(mesh):
    placed = (
        P(("dp", "blk"), None, None),
        P(("dp", "blk")),
        P(("dp", "blk"), None),
        P(("dp", "blk")),
        P(),
        P(),
        P(),
        P(("dp", "blk"), None),
    )
    return jax.shard_map(
        shards,
        mesh=mesh,
        in_specs=placed,
        out_specs=(P(("dp", "blk"), None), P(("dp", "blk"), None)),
        check_vma=False,
    )
```

```python
import functools
import math

import jax
import jax.numpy as jnp
from jax import lax
from jax.experimental import pallas as pl
from jax.experimental.pallas import tpu as pltpu
from jax.sharding import PartitionSpec as P

logit_scale = 20.0
contract_last = (((1,), (1,)), ((), ()))
tile = 256
chunk = 16
number_rows = 8


def swap(array, axis, bit):
    devices = lax.axis_size(axis)
    return lax.ppermute(array, axis, [(i, i ^ bit) for i in range(devices)])


def from_behind(array, axis, by):
    devices = lax.axis_size(axis)
    return lax.ppermute(array, axis, [(i, (i + by) % devices) for i in range(devices)])


def in_vmem(array):
    return pltpu.with_memory_space_constraint(array, pltpu.VMEM)


def in_hbm(array):
    return pltpu.with_memory_space_constraint(array, pltpu.HBM)


def half_silu(half):
    return half + half * jnp.tanh(half)


def center_and_spread(values):
    center = values - jnp.mean(values, axis=-1, keepdims=True)
    return center, jnp.mean(center * center, axis=-1, keepdims=True)


def pack_kernel(
    work, groups, list_any, len_any, from_any, tgt_any, pool_any, *refs,
):
    users, length, width = from_any.shape
    to_refs, unit_any = refs[:users], refs[users]
    entries, lens, targets, pool, unit, events, sems, in_sems = refs[users + 1 :]
    small = [
        pltpu.make_async_copy(source, target, sems.at[k])
        for k, (source, target) in enumerate(
            ((list_any, entries), (len_any, lens), (tgt_any, targets), (pool_any, pool))
        )
    ]
    for copy in small:
        copy.start()
    copies_in = [
        pltpu.make_async_copy(from_any.at[u], events.at[u], in_sems.at[u]) for u in range(users)
    ]
    for copy in copies_in:
        copy.start()
    small[3].wait()
    rows = pool[...].astype(jnp.float32)
    unit[...] = (rows * lax.rsqrt(jnp.sum(rows * rows, axis=-1, keepdims=True) + 1e-06)).astype(jnp.bfloat16)
    units_out = [
        pltpu.make_async_copy(unit, unit_any.at[k], sems.at[4 + k]) for k in range(unit_any.shape[0])
    ]
    for copy in units_out:
        copy.start()
    for copy in small[:3]:
        copy.wait()
    slots = users // groups
    group = lax.axis_index("dp")
    order = [entries[lax.rem(group + shift, groups) * slots + slot] for shift, slot in work]
    row = lax.broadcasted_iota(jnp.int32, (number_rows, length), 0)
    for k in range(users):
        target = targets[pl.ds(order[k], 1), :]
        numbers = jnp.where(row == 0, lens[order[k]], jnp.where(row == 1, target // 256, target % 256))
        to_refs[k][width:, :] = numbers.astype(jnp.float32).astype(jnp.bfloat16)
    for copy in copies_in:
        copy.wait()
    for k in range(users):
        for c in range(0, width, length):
            to_refs[k][c : c + length, :] = events[order[k], :, c : c + length]
    for copy in units_out:
        copy.wait()


def pack(histories, lengths, targets, entries, item_pool, work, groups, blocks):
    users, length, width = histories.shape
    shape = (width + number_rows, length)
    hbm = pl.BlockSpec(memory_space=pltpu.HBM)
    return pl.pallas_call(
        functools.partial(pack_kernel, work, groups),
        in_specs=[hbm] * 5,
        out_specs=[pl.BlockSpec(memory_space=pltpu.VMEM)] * users + [hbm],
        scratch_shapes=[
            pltpu.SMEM(entries.shape, jnp.int32),
            pltpu.SMEM(lengths.shape, jnp.int32),
            pltpu.VMEM(targets.shape, jnp.int32),
            pltpu.VMEM(item_pool.shape, jnp.bfloat16),
            pltpu.VMEM(item_pool.shape, jnp.bfloat16),
            pltpu.VMEM(histories.shape, jnp.bfloat16),
            pltpu.SemaphoreType.DMA((4 + blocks,)),
            pltpu.SemaphoreType.DMA((users,)),
        ],
        out_shape=[pltpu.VMEM(shape, jnp.bfloat16)] * users
        + [pltpu.HBM((blocks,) + item_pool.shape, jnp.bfloat16)],
        compiler_params=pltpu.CompilerParams(vmem_limit_bytes=16 * 1024 * 1024),
        name="pack",
    )(*[in_hbm(array) for array in (entries, lengths, histories, targets, item_pool)])


def users_kernel(work, groups, x_refs, w_in, w_out, unit_ref, sums, loss_ref, bias, scratch):
    slots = loss_ref.shape[0] // groups
    group = lax.axis_index("dp")
    spots = [lax.rem(group + groups - shift, groups) * slots + slot for shift, slot in work]
    for at in range(0, len(work), 8):
        users_step(
            x_refs[at : at + 8], spots[at : at + 8],
            w_in, w_out, unit_ref, sums, loss_ref, bias, *scratch,
        )


def first_kernel(work, groups, w_in_any, w_out_any, rel_any, unit_ref, *refs):
    count = len(work)
    x_refs, refs = refs[:count], refs[count:]
    loss_ref, sums, bias, refs = refs[0], refs[1], refs[2], refs[3:]
    w_in, w_out, rel, sems = refs[:4]
    heads, length = rel.shape
    moves = [(rel_any, rel), (w_in_any, w_in), (w_out_any, w_out)]
    copies = [pltpu.make_async_copy(*move, sems.at[k]) for k, move in enumerate(moves)]
    for copy in copies:
        copy.start()
    loss_ref[...] = jnp.zeros_like(loss_ref)
    sums[...] = jnp.zeros_like(sums)
    copies[0].wait()
    for h in range(heads):
        wide = jnp.broadcast_to(0.5 * rel[h : h + 1, :], (length, length))
        turned = pltpu.roll(wide, 0, 1, stride=1, stride_axis=0).T
        bias[h] = jnp.concatenate([turned, turned], axis=1)
    for copy in copies[1:]:
        copy.wait()
    users_kernel(work, groups, x_refs, w_in, w_out, unit_ref, sums, loss_ref, bias, refs[4:])


def second_kernel(work, groups, w_in, w_out, bias, unit_ref, loss_in, sums_in, *refs):
    count = len(work)
    x_refs, refs = refs[:count], refs[count:]
    loss_ref, out_refs, sums, scratch = refs[0], refs[1:5], refs[5], refs[6:]
    loss_ref[...] = loss_in[...]
    sums[...] = sums_in[...]
    users_kernel(work, groups, x_refs, w_in, w_out, unit_ref, sums, loss_ref, bias, scratch)
    mine = lax.axis_index("blk")
    for bits, ref in zip((0, 2, 1, 3), out_refs):
        ref[...] = sums[mine ^ bits].astype(ref.dtype)


def users_step(
    x_refs, spots, w_in, w_out, unit_ref, sums, loss_ref, bias,
    exp_ref, residual, events, starts_ref, key, value, packed_tgt, packed_loss,
):
    heads, length, _ = bias.shape
    width = w_out.shape[0]
    hdim = width // heads
    blocks, items, _ = unit_ref.shape
    per_step = len(x_refs)

    digits = [ref[width:, :].astype(jnp.float32) for ref in x_refs]
    lens = [jnp.max(digit[:1, :]).astype(jnp.int32) for digit in digits]
    starts, end = [], 0
    for u in range(per_step):
        starts.append(pl.multiple_of(end, chunk) if u else 0)
        end = end + (lens[u] + chunk - 1) // chunk * chunk
    end = pl.multiple_of(end, chunk)
    tiles = (end + tile - 1) // tile

    place = lax.broadcasted_iota(jnp.int32, (1, length), 1)
    packed_tgt[...] = jnp.full_like(packed_tgt, -1)
    key[:length, :] = jnp.zeros((length, width), key.dtype)
    value[:length, :] = jnp.zeros((length, width), value.dtype)
    for u in range(per_step):
        starts_ref[pl.ds(starts[u], length), :] = jnp.full((length, length), starts[u], jnp.int32)
    for u in range(per_step):
        for c in range(0, width, length):
            events[pl.ds(starts[u], length), c : c + length] = x_refs[u][c : c + length, :]
        target = digits[u][1:2, :] * 256.0 + digits[u][2:3, :]
        wanted = jnp.where(place < lens[u], target.astype(jnp.int32), -1)
        line, turn = starts[u] // length + 1, lax.rem(starts[u], length)
        turned = pltpu.roll(wanted, turn, 1)
        packed_tgt[pl.ds(line, 1), :] = jnp.where(place >= turn, turned, packed_tgt[pl.ds(line, 1), :])
        packed_tgt[pl.ds(line + 1, 1), :] = jnp.where(
            place < turn, turned, packed_tgt[pl.ds(line + 1, 1), :]
        )
    events[pl.ds(end, tile), :] = jnp.zeros((tile, width), events.dtype)

    row = lax.broadcasted_iota(jnp.int32, (length, length), 0)
    col = lax.broadcasted_iota(jnp.int32, (length, length), 1)
    rate = logit_scale * math.log2(math.e)

    lines = tile // length

    def one_tile(t, _):
        first, strip = pl.multiple_of(t * tile, tile), t * lines
        item_id = lax.broadcasted_iota(jnp.int32, (items, tile), 0)
        x = events[pl.ds(first, tile), :].astype(jnp.float32)
        center, spread = center_and_spread(x)
        half_normed = (center * (0.5 * lax.rsqrt(spread + 1e-05))).astype(jnp.bfloat16)
        gate, values, query, keys = [
            half_silu(
                jnp.dot(
                    half_normed, w_in[:, part * width : (part + 1) * width],
                    preferred_element_type=jnp.float32,
                )
            ).astype(jnp.bfloat16)
            for part in range(4)
        ]
        key[pl.ds(first + length, tile), :] = keys
        value[pl.ds(first + length, tile), :] = values
        mixed = []
        for k in range(lines):
            base = pl.multiple_of(first + k * length, length)
            sources = pl.ds(base, 2 * length)
            start = starts_ref[pl.ds(base, length), :]
            ahead = packed_tgt[pl.ds(strip + k, 1), :] >= 0
            here = packed_tgt[pl.ds(strip + k + 1, 1), :] >= 0
            keep_ahead = (base - length + col >= start) & ahead
            keep_here = (col <= row) & (base + col >= start) & here
            keep = jnp.concatenate([keep_ahead, keep_here], axis=1)
            by_head = []
            for h in range(heads):
                cols = slice(h * hdim, (h + 1) * hdim)
                scores = lax.dot_general(
                    query[k * length : (k + 1) * length, cols], key[sources, cols], contract_last,
                    preferred_element_type=jnp.float32,
                )
                attn = half_silu(scores * (0.5 / math.sqrt(hdim)) + bias[h])
                attn = jnp.where(keep, attn, 0.0).astype(jnp.bfloat16)
                by_head.append(jnp.dot(attn, value[sources, cols], preferred_element_type=jnp.float32))
            mixed.append(jnp.concatenate(by_head, axis=1))
        center, spread = center_and_spread(jnp.concatenate(mixed, axis=0))
        normed = center * lax.rsqrt(spread + 1e-05)
        gated = (normed * gate.astype(jnp.float32)).astype(jnp.bfloat16)
        out = x + jnp.dot(gated, w_out[...], preferred_element_type=jnp.float32)
        out = out.astype(jnp.bfloat16).astype(jnp.float32)
        square = jnp.sum(out * out, axis=-1, keepdims=True)
        queries = (out * lax.rsqrt(square + 1e-06)).astype(jnp.bfloat16)

        target = jnp.concatenate(
            [packed_tgt[pl.ds(strip + k + 1, 1), :] for k in range(lines)], axis=1
        )
        total = jnp.zeros((1, tile), jnp.float32)
        target_dot = jnp.zeros((1, tile), jnp.float32)
        for j in range(blocks):
            dots = lax.dot_general(
                unit_ref[j], queries, contract_last, preferred_element_type=jnp.float32
            )
            exps = jnp.exp2(dots * rate - rate)
            exp_ref[j] = exps
            total += jnp.sum(exps, axis=0, keepdims=True)
            hit = item_id == target - j * items
            target_dot += jnp.sum(jnp.where(hit, dots, 0.0), axis=0, keepdims=True)
        loss = logit_scale + jnp.log(total) - logit_scale * target_dot
        for k in range(lines):
            packed_loss[pl.ds(strip + k, 1), :] = loss[:, k * length : (k + 1) * length]
        share = jnp.where(target >= 0, 1.0 / total, 0.0)
        for j in range(blocks):
            hit = item_id == target - j * items
            left = exp_ref[j] * share - jnp.where(hit, 1.0, 0.0)
            residual[j] = left.astype(jnp.bfloat16)
        for j in range(blocks):
            sums[j] += jnp.dot(residual[j], queries, preferred_element_type=jnp.float32)
        return 0

    lax.fori_loop(0, tiles, one_tile, 0)

    for u in range(per_step):
        line, turn = starts[u] // length, lax.rem(starts[u], length)
        back = lax.rem(length - turn, length)
        near = pltpu.roll(packed_loss[pl.ds(line, 1), :], back, 1)
        rest = pltpu.roll(packed_loss[pl.ds(line + 1, 1), :], back, 1)
        loss = jnp.where(place < length - turn, near, rest)
        loss_ref[pl.ds(spots[u], 1), :] = jnp.where(place < lens[u], loss, 0.0)


def step_scratch(count, length, width, blocks, items):
    rows = -(-min(count, 8) * length // tile) * tile
    lines = -(-(rows // length + 2) // 8) * 8
    return [
        pltpu.VMEM((blocks, items, tile), jnp.float32),
        pltpu.VMEM((blocks, items, tile), jnp.bfloat16),
        pltpu.VMEM((rows + tile, width), jnp.bfloat16),
        pltpu.VMEM((rows + tile, length), jnp.int32),
        pltpu.VMEM((length + rows + tile, width), jnp.bfloat16),
        pltpu.VMEM((length + rows + tile, width), jnp.bfloat16),
        pltpu.VMEM((lines, length), jnp.int32),
        pltpu.VMEM((lines, length), jnp.float32),
    ]


whole = pl.BlockSpec(memory_space=pltpu.VMEM)
far_off = pl.BlockSpec(memory_space=pltpu.HBM)


def first_call(work, groups, users, packed, units, w_in, w_out, rel_bias):
    heads, length = rel_bias.shape
    width, (blocks, items, _) = w_out.shape[0], units.shape
    return pl.pallas_call(
        functools.partial(first_kernel, work, groups),
        in_specs=[far_off] * 3 + [whole] * (1 + len(work)),
        out_specs=[whole] * 3,
        scratch_shapes=[
            pltpu.VMEM(w_in.shape, jnp.bfloat16),
            pltpu.VMEM(w_out.shape, jnp.bfloat16),
            pltpu.VMEM(rel_bias.shape, jnp.float32),
            pltpu.SemaphoreType.DMA((3,)),
        ]
        + step_scratch(len(work), length, width, blocks, items),
        out_shape=[
            pltpu.VMEM((users, length), jnp.float32),
            pltpu.VMEM((blocks, items, width), jnp.float32),
            pltpu.VMEM((heads, length, 2 * length), jnp.float32),
        ],
        compiler_params=pltpu.CompilerParams(vmem_limit_bytes=24 * 1024 * 1024),
        name="first_users",
    )(
        *[in_hbm(array) for array in (w_in, w_out, rel_bias)], in_vmem(units),
        *[in_vmem(array) for array in packed],
    )


def second_call(work, groups, packed, units, w_in, w_out, loss, sums, bias):
    blocks, items, width = sums.shape
    length = bias.shape[1]
    arrays = [w_in, w_out, bias, units, loss, sums, *packed]
    return pl.pallas_call(
        functools.partial(second_kernel, work, groups),
        in_specs=[whole] * len(arrays),
        out_specs=[whole] * 5,
        scratch_shapes=[pltpu.VMEM(sums.shape, jnp.float32)]
        + step_scratch(len(work), length, width, blocks, items),
        out_shape=[pltpu.VMEM(loss.shape, jnp.float32)]
        + [pltpu.VMEM((items, width), jnp.float32)] * 2
        + [pltpu.VMEM((items, width), jnp.bfloat16)] * 2,
        compiler_params=pltpu.CompilerParams(vmem_limit_bytes=24 * 1024 * 1024),
        name="second_users",
    )(*[in_vmem(array) for array in arrays])


def shards(histories, lengths, targets, send_list, w_in, w_out, rel_bias, item_pool):
    user_count = histories.shape[0]
    groups, blocks = lax.axis_size("dp"), lax.axis_size("blk")
    slots = user_count // groups

    near = sorted({0, 1, groups - 1, 2 % groups}, key=lambda shift: (shift != 0, shift == 2))
    others = [shift for shift in range(groups) if shift not in near]
    order = near + sorted(others, key=lambda shift: abs(shift - groups / 2))
    work = [(shift, slot) for shift in order for slot in range(slots)]
    *packed, units = pack(
        histories, lengths, targets, send_list, item_pool, work, groups, blocks
    )
    half = user_count // 2
    packed = [
        users if shift == 0 else from_behind(users, "dp", shift) for users, (shift, _) in zip(packed, work)
    ]
    units = lax.all_to_all(units, "blk", split_axis=0, concat_axis=0, tiled=True)

    pool_float = item_pool.astype(jnp.float32)
    item_norm = jnp.sqrt(jnp.sum(pool_float * pool_float, axis=-1, keepdims=True) + 1e-06)
    unit_rows = pool_float / item_norm

    loss, sums, bias = first_call(
        work[:half], groups, user_count, packed[:half], units, w_in, w_out, rel_bias
    )
    row_loss, own, over, side, far = second_call(
        work[half:], groups, packed[half:], units, w_in, w_out, loss, sums, bias
    )
    over = over + swap(far, "blk", 1).astype(jnp.float32)
    own = own + swap(side, "blk", 1).astype(jnp.float32)
    item_sum = logit_scale * (own + swap(over.astype(jnp.bfloat16), "blk", 2).astype(jnp.float32))
    pool_grad = (
        item_sum - unit_rows * jnp.sum(unit_rows * item_sum, axis=-1, keepdims=True)
    ) / item_norm
    return (row_loss, pool_grad)


def solution(mesh):
    placed = (
        P(("dp", "blk"), None, None),
        P(("dp", "blk")),
        P(("dp", "blk"), None),
        P(("dp", "blk")),
        P(),
        P(),
        P(),
        P(("dp", "blk"), None),
    )
    return jax.shard_map(
        shards,
        mesh=mesh,
        in_specs=placed,
        out_specs=(P(("dp", "blk"), None), P(("dp", "blk"), None)),
        check_vma=False,
    )
```

```python
import functools
import math

import jax
import jax.numpy as jnp
from jax import lax
from jax.experimental import pallas as pl
from jax.experimental.pallas import tpu as pltpu
from jax.sharding import PartitionSpec as P

logit_scale = 20.0
contract_last = (((1,), (1,)), ((), ()))
first_tile, second_tile = 384, 256
chunk = 16
number_rows = 8


def swap(array, axis, bit):
    devices = lax.axis_size(axis)
    return lax.ppermute(array, axis, [(i, i ^ bit) for i in range(devices)])


def from_behind(array, axis, by):
    devices = lax.axis_size(axis)
    return lax.ppermute(array, axis, [(i, (i + by) % devices) for i in range(devices)])


def in_vmem(array):
    return pltpu.with_memory_space_constraint(array, pltpu.VMEM)


def in_hbm(array):
    return pltpu.with_memory_space_constraint(array, pltpu.HBM)


def half_silu(half):
    return half + half * jnp.tanh(half)


def center_and_spread(values):
    center = values - jnp.mean(values, axis=-1, keepdims=True)
    return center, jnp.mean(center * center, axis=-1, keepdims=True)


def pack_kernel(
    work, groups, list_any, len_any, from_any, tgt_any, pool_any, *refs,
):
    users, length, width = from_any.shape
    to_refs, unit_any = refs[:users], refs[users]
    entries, lens, targets, pool, unit, sems, in_sems = refs[users + 1 :]
    pieces = width // length
    small = [
        pltpu.make_async_copy(source, target, sems.at[k])
        for k, (source, target) in enumerate(
            ((list_any, entries), (len_any, lens), (tgt_any, targets), (pool_any, pool))
        )
    ]
    for copy in reversed(small):
        copy.start()
    small[0].wait()
    slots = users // groups
    group = lax.axis_index("dp")
    order = [entries[lax.rem(group + shift, groups) * slots + slot] for shift, slot in work]
    copies_in = [
        pltpu.make_async_copy(
            from_any.at[order[k], :, pl.ds(c * length, length)],
            to_refs[k].at[pl.ds(c * length, length)],
            in_sems.at[k, c],
        )
        for k in range(users)
        for c in range(pieces)
    ]
    for copy in copies_in:
        copy.start()
    small[3].wait()
    rows = pool[...].astype(jnp.float32)
    unit[...] = (rows * lax.rsqrt(jnp.sum(rows * rows, axis=-1, keepdims=True) + 1e-06)).astype(jnp.bfloat16)
    units_out = [
        pltpu.make_async_copy(unit, unit_any.at[k], sems.at[4 + k]) for k in range(unit_any.shape[0])
    ]
    for copy in units_out:
        copy.start()
    small[1].wait()
    small[2].wait()
    row = lax.broadcasted_iota(jnp.int32, (number_rows, length), 0)
    for k in range(users):
        target = targets[pl.ds(order[k], 1), :]
        numbers = jnp.where(row == 0, lens[order[k]], jnp.where(row == 1, target // 256, target % 256))
        to_refs[k][width:, :] = numbers.astype(jnp.float32).astype(jnp.bfloat16)
    for copy in copies_in + units_out:
        copy.wait()


def pack(histories, lengths, targets, entries, item_pool, work, groups, blocks):
    users, length, width = histories.shape
    shape = (width + number_rows, length)
    hbm = pl.BlockSpec(memory_space=pltpu.HBM)
    return pl.pallas_call(
        functools.partial(pack_kernel, work, groups),
        in_specs=[hbm] * 5,
        out_specs=[pl.BlockSpec(memory_space=pltpu.VMEM)] * users + [hbm],
        scratch_shapes=[
            pltpu.SMEM(entries.shape, jnp.int32),
            pltpu.SMEM(lengths.shape, jnp.int32),
            pltpu.VMEM(targets.shape, jnp.int32),
            pltpu.VMEM(item_pool.shape, jnp.bfloat16),
            pltpu.VMEM(item_pool.shape, jnp.bfloat16),
            pltpu.SemaphoreType.DMA((4 + blocks,)),
            pltpu.SemaphoreType.DMA((users, width // length)),
        ],
        out_shape=[pltpu.VMEM(shape, jnp.bfloat16)] * users
        + [pltpu.HBM((blocks,) + item_pool.shape, jnp.bfloat16)],
        compiler_params=pltpu.CompilerParams(vmem_limit_bytes=16 * 1024 * 1024),
        name="pack",
    )(*[in_hbm(array) for array in (entries, lengths, histories, targets, item_pool)])


def users_kernel(tile, work, groups, x_refs, w_in, w_out, unit_ref, sums, loss_ref, bias, scratch):
    slots = loss_ref.shape[0] // groups
    group = lax.axis_index("dp")
    spots = [lax.rem(group + groups - shift, groups) * slots + slot for shift, slot in work]
    for at in range(0, len(work), 8):
        users_step(
            tile, x_refs[at : at + 8], spots[at : at + 8],
            w_in, w_out, unit_ref, sums, loss_ref, bias, *scratch,
        )


def first_kernel(work, groups, w_in_any, w_out_any, rel_any, unit_ref, *refs):
    count = len(work)
    x_refs, refs = refs[:count], refs[count:]
    loss_ref, sums, bias, refs = refs[0], refs[1], refs[2], refs[3:]
    w_in, w_out, rel, sems = refs[:4]
    heads, length = rel.shape
    moves = [(rel_any, rel), (w_in_any, w_in), (w_out_any, w_out)]
    copies = [pltpu.make_async_copy(*move, sems.at[k]) for k, move in enumerate(moves)]
    for copy in copies:
        copy.start()
    loss_ref[...] = jnp.zeros_like(loss_ref)
    sums[...] = jnp.zeros_like(sums)
    copies[0].wait()
    for h in range(heads):
        wide = jnp.broadcast_to(0.5 * rel[h : h + 1, :], (length, length))
        turned = pltpu.roll(wide, 0, 1, stride=1, stride_axis=0).T
        bias[h] = jnp.concatenate([turned, turned], axis=1)
    for copy in copies[1:]:
        copy.wait()
    users_kernel(first_tile, work, groups, x_refs, w_in, w_out, unit_ref, sums, loss_ref, bias, refs[4:])


def second_kernel(work, groups, w_in, w_out, bias, unit_ref, loss_in, sums_in, *refs):
    count = len(work)
    x_refs, refs = refs[:count], refs[count:]
    loss_ref, out_refs, sums, scratch = refs[0], refs[1:5], refs[5], refs[6:]
    loss_ref[...] = loss_in[...]
    sums[...] = sums_in[...]
    users_kernel(second_tile, work, groups, x_refs, w_in, w_out, unit_ref, sums, loss_ref, bias, scratch)
    mine = lax.axis_index("blk")
    for bits, ref in zip((0, 2, 1, 3), out_refs):
        ref[...] = sums[mine ^ bits].astype(ref.dtype)


def users_step(
    tile, x_refs, spots, w_in, w_out, unit_ref, sums, loss_ref, bias,
    exp_ref, residual, events, starts_ref, key, value, packed_tgt, packed_loss,
):
    heads, length, _ = bias.shape
    width = w_out.shape[0]
    hdim = width // heads
    blocks, items, _ = unit_ref.shape
    per_step = len(x_refs)

    digits = [ref[width:, :].astype(jnp.float32) for ref in x_refs]
    lens = [jnp.max(digit[:1, :]).astype(jnp.int32) for digit in digits]
    starts, end = [], 0
    for u in range(per_step):
        starts.append(pl.multiple_of(end, chunk) if u else 0)
        end = end + (lens[u] + chunk - 1) // chunk * chunk
    end = pl.multiple_of(end, chunk)
    tiles = (end + tile - 1) // tile

    place = lax.broadcasted_iota(jnp.int32, (1, length), 1)
    packed_tgt[...] = jnp.full_like(packed_tgt, -1)
    key[:length, :] = jnp.zeros((length, width), key.dtype)
    value[:length, :] = jnp.zeros((length, width), value.dtype)
    for u in range(per_step):
        starts_ref[pl.ds(starts[u], length), :] = jnp.full((length, length), starts[u], jnp.int32)
    for u in range(per_step):
        for c in range(0, width, length):
            events[pl.ds(starts[u], length), c : c + length] = x_refs[u][c : c + length, :]
        target = digits[u][1:2, :] * 256.0 + digits[u][2:3, :]
        wanted = jnp.where(place < lens[u], target.astype(jnp.int32), -1)
        line, turn = starts[u] // length + 1, lax.rem(starts[u], length)
        turned = pltpu.roll(wanted, turn, 1)
        packed_tgt[pl.ds(line, 1), :] = jnp.where(place >= turn, turned, packed_tgt[pl.ds(line, 1), :])
        packed_tgt[pl.ds(line + 1, 1), :] = jnp.where(
            place < turn, turned, packed_tgt[pl.ds(line + 1, 1), :]
        )
    events[pl.ds(end, tile), :] = jnp.zeros((tile, width), events.dtype)

    row = lax.broadcasted_iota(jnp.int32, (length, length), 0)
    col = lax.broadcasted_iota(jnp.int32, (length, length), 1)
    rate = logit_scale * math.log2(math.e)

    lines = tile // length

    def one_tile(t, _):
        first, strip = pl.multiple_of(t * tile, tile), t * lines
        item_id = lax.broadcasted_iota(jnp.int32, (items, tile), 0)
        x = events[pl.ds(first, tile), :].astype(jnp.float32)
        center, spread = center_and_spread(x)
        half_normed = (center * (0.5 * lax.rsqrt(spread + 1e-05))).astype(jnp.bfloat16)
        gate, values, query, keys = [
            half_silu(
                jnp.dot(
                    half_normed, w_in[:, part * width : (part + 1) * width],
                    preferred_element_type=jnp.float32,
                )
            ).astype(jnp.bfloat16)
            for part in range(4)
        ]
        key[pl.ds(first + length, tile), :] = keys
        value[pl.ds(first + length, tile), :] = values
        mixed = []
        for k in range(lines):
            base = pl.multiple_of(first + k * length, length)
            sources = pl.ds(base, 2 * length)
            start = starts_ref[pl.ds(base, length), :]
            ahead = packed_tgt[pl.ds(strip + k, 1), :] >= 0
            here = packed_tgt[pl.ds(strip + k + 1, 1), :] >= 0
            keep_ahead = (base - length + col >= start) & ahead
            keep_here = (col <= row) & (base + col >= start) & here
            keep = jnp.concatenate([keep_ahead, keep_here], axis=1)
            by_head = []
            for h in range(heads):
                cols = slice(h * hdim, (h + 1) * hdim)
                scores = lax.dot_general(
                    query[k * length : (k + 1) * length, cols], key[sources, cols], contract_last,
                    preferred_element_type=jnp.float32,
                )
                attn = half_silu(scores * (0.5 / math.sqrt(hdim)) + bias[h])
                attn = jnp.where(keep, attn, 0.0).astype(jnp.bfloat16)
                by_head.append(jnp.dot(attn, value[sources, cols], preferred_element_type=jnp.float32))
            mixed.append(jnp.concatenate(by_head, axis=1))
        center, spread = center_and_spread(jnp.concatenate(mixed, axis=0))
        normed = center * lax.rsqrt(spread + 1e-05)
        gated = (normed * gate.astype(jnp.float32)).astype(jnp.bfloat16)
        out = x + jnp.dot(gated, w_out[...], preferred_element_type=jnp.float32)
        out = out.astype(jnp.bfloat16).astype(jnp.float32)
        square = jnp.sum(out * out, axis=-1, keepdims=True)
        queries = (out * lax.rsqrt(square + 1e-06)).astype(jnp.bfloat16)

        target = jnp.concatenate(
            [packed_tgt[pl.ds(strip + k + 1, 1), :] for k in range(lines)], axis=1
        )
        total = jnp.zeros((1, tile), jnp.float32)
        target_dot = jnp.zeros((1, tile), jnp.float32)
        for j in range(blocks):
            dots = lax.dot_general(
                unit_ref[j], queries, contract_last, preferred_element_type=jnp.float32
            )
            exps = jnp.exp2(dots * rate - rate)
            exp_ref[j] = exps
            total += jnp.sum(exps, axis=0, keepdims=True)
            hit = item_id == target - j * items
            target_dot += jnp.sum(jnp.where(hit, dots, 0.0), axis=0, keepdims=True)
        loss = logit_scale + jnp.log(total) - logit_scale * target_dot
        for k in range(lines):
            packed_loss[pl.ds(strip + k, 1), :] = loss[:, k * length : (k + 1) * length]
        share = jnp.where(target >= 0, 1.0 / total, 0.0)
        for j in range(blocks):
            hit = item_id == target - j * items
            left = exp_ref[j] * share - jnp.where(hit, 1.0, 0.0)
            residual[j] = left.astype(jnp.bfloat16)
        for j in range(blocks):
            sums[j] += jnp.dot(residual[j], queries, preferred_element_type=jnp.float32)
        return 0

    lax.fori_loop(0, tiles, one_tile, 0)

    for u in range(per_step):
        line, turn = starts[u] // length, lax.rem(starts[u], length)
        back = lax.rem(length - turn, length)
        near = pltpu.roll(packed_loss[pl.ds(line, 1), :], back, 1)
        rest = pltpu.roll(packed_loss[pl.ds(line + 1, 1), :], back, 1)
        loss = jnp.where(place < length - turn, near, rest)
        loss_ref[pl.ds(spots[u], 1), :] = jnp.where(place < lens[u], loss, 0.0)


def step_scratch(tile, count, length, width, blocks, items):
    rows = -(-min(count, 8) * length // tile) * tile
    lines = -(-(rows // length + 2) // 8) * 8
    return [
        pltpu.VMEM((blocks, items, tile), jnp.float32),
        pltpu.VMEM((blocks, items, tile), jnp.bfloat16),
        pltpu.VMEM((rows + tile, width), jnp.bfloat16),
        pltpu.VMEM((rows + tile, length), jnp.int32),
        pltpu.VMEM((length + rows + tile, width), jnp.bfloat16),
        pltpu.VMEM((length + rows + tile, width), jnp.bfloat16),
        pltpu.VMEM((lines, length), jnp.int32),
        pltpu.VMEM((lines, length), jnp.float32),
    ]


whole = pl.BlockSpec(memory_space=pltpu.VMEM)
far_off = pl.BlockSpec(memory_space=pltpu.HBM)


def first_call(work, groups, users, packed, units, w_in, w_out, rel_bias):
    heads, length = rel_bias.shape
    width, (blocks, items, _) = w_out.shape[0], units.shape
    return pl.pallas_call(
        functools.partial(first_kernel, work, groups),
        in_specs=[far_off] * 3 + [whole] * (1 + len(work)),
        out_specs=[whole] * 3,
        scratch_shapes=[
            pltpu.VMEM(w_in.shape, jnp.bfloat16),
            pltpu.VMEM(w_out.shape, jnp.bfloat16),
            pltpu.VMEM(rel_bias.shape, jnp.float32),
            pltpu.SemaphoreType.DMA((3,)),
        ]
        + step_scratch(first_tile, len(work), length, width, blocks, items),
        out_shape=[
            pltpu.VMEM((users, length), jnp.float32),
            pltpu.VMEM((blocks, items, width), jnp.float32),
            pltpu.VMEM((heads, length, 2 * length), jnp.float32),
        ],
        compiler_params=pltpu.CompilerParams(vmem_limit_bytes=24 * 1024 * 1024),
        name="first_users",
    )(
        *[in_hbm(array) for array in (w_in, w_out, rel_bias)], in_vmem(units),
        *[in_vmem(array) for array in packed],
    )


def second_call(work, groups, packed, units, w_in, w_out, loss, sums, bias):
    blocks, items, width = sums.shape
    length = bias.shape[1]
    arrays = [w_in, w_out, bias, units, loss, sums, *packed]
    return pl.pallas_call(
        functools.partial(second_kernel, work, groups),
        in_specs=[whole] * len(arrays),
        out_specs=[whole] * 5,
        scratch_shapes=[pltpu.VMEM(sums.shape, jnp.float32)]
        + step_scratch(second_tile, len(work), length, width, blocks, items),
        out_shape=[pltpu.VMEM(loss.shape, jnp.float32)]
        + [pltpu.VMEM((items, width), jnp.float32)] * 2
        + [pltpu.VMEM((items, width), jnp.bfloat16)] * 2,
        compiler_params=pltpu.CompilerParams(vmem_limit_bytes=24 * 1024 * 1024),
        name="second_users",
    )(*[in_vmem(array) for array in arrays])


def shards(histories, lengths, targets, send_list, w_in, w_out, rel_bias, item_pool):
    user_count = histories.shape[0]
    groups, blocks = lax.axis_size("dp"), lax.axis_size("blk")
    slots = user_count // groups

    near = sorted({0, 1, groups - 1, 2 % groups}, key=lambda shift: (shift != 0, shift == 2))
    others = [shift for shift in range(groups) if shift not in near]
    order = near + sorted(others, key=lambda shift: abs(shift - groups / 2))
    work = [(shift, slot) for shift in order for slot in range(slots)]
    *packed, units = pack(
        histories, lengths, targets, send_list, item_pool, work, groups, blocks
    )
    half = user_count // 2
    packed = [
        users if shift == 0 else from_behind(users, "dp", shift) for users, (shift, _) in zip(packed, work)
    ]
    units = lax.all_to_all(units, "blk", split_axis=0, concat_axis=0, tiled=True)

    pool_float = item_pool.astype(jnp.float32)
    item_norm = jnp.sqrt(jnp.sum(pool_float * pool_float, axis=-1, keepdims=True) + 1e-06)
    unit_rows = pool_float / item_norm

    loss, sums, bias = first_call(
        work[:half], groups, user_count, packed[:half], units, w_in, w_out, rel_bias
    )
    row_loss, own, over, side, far = second_call(
        work[half:], groups, packed[half:], units, w_in, w_out, loss, sums, bias
    )
    over = over + swap(far, "blk", 1).astype(jnp.float32)
    own = own + swap(side, "blk", 1).astype(jnp.float32)
    item_sum = logit_scale * (own + swap(over.astype(jnp.bfloat16), "blk", 2).astype(jnp.float32))
    pool_grad = (
        item_sum - unit_rows * jnp.sum(unit_rows * item_sum, axis=-1, keepdims=True)
    ) / item_norm
    return (row_loss, pool_grad)


def solution(mesh):
    placed = (
        P(("dp", "blk"), None, None),
        P(("dp", "blk")),
        P(("dp", "blk"), None),
        P(("dp", "blk")),
        P(),
        P(),
        P(),
        P(("dp", "blk"), None),
    )
    return jax.shard_map(
        shards,
        mesh=mesh,
        in_specs=placed,
        out_specs=(P(("dp", "blk"), None), P(("dp", "blk"), None)),
        check_vma=False,
    )
```

```python
import functools
import math

import jax
import jax.numpy as jnp
from jax import lax
from jax.experimental import pallas as pl
from jax.experimental.pallas import tpu as pltpu
from jax.sharding import PartitionSpec as P

logit_scale = 20.0
contract_last = (((1,), (1,)), ((), ()))
first_tile, second_tile = 384, 256
chunk = 16
number_rows = 8


def swap(array, axis, bit):
    devices = lax.axis_size(axis)
    return lax.ppermute(array, axis, [(i, i ^ bit) for i in range(devices)])


def from_behind(array, axis, by):
    devices = lax.axis_size(axis)
    return lax.ppermute(array, axis, [(i, (i + by) % devices) for i in range(devices)])


def in_vmem(array):
    return pltpu.with_memory_space_constraint(array, pltpu.VMEM)


def in_hbm(array):
    return pltpu.with_memory_space_constraint(array, pltpu.HBM)


def half_silu(half):
    return half + half * jnp.tanh(half)


def center_and_spread(values):
    center = values - jnp.mean(values, axis=-1, keepdims=True)
    return center, jnp.mean(center * center, axis=-1, keepdims=True)


def pack_kernel(
    work, groups, list_any, len_any, from_any, tgt_any, pool_any, *refs,
):
    users, length, width = from_any.shape
    to_refs, unit_any = refs[:users], refs[users]
    entries, lens, targets, pool, unit, sems, in_sems = refs[users + 1 :]
    pieces = width // length
    small = [
        pltpu.make_async_copy(source, target, sems.at[k])
        for k, (source, target) in enumerate(
            ((list_any, entries), (len_any, lens), (tgt_any, targets), (pool_any, pool))
        )
    ]
    for copy in small:
        copy.start()
    small[0].wait()
    slots = users // groups
    group = lax.axis_index("dp")
    order = [entries[lax.rem(group + shift, groups) * slots + slot] for shift, slot in work]
    copies_in = [
        pltpu.make_async_copy(
            from_any.at[order[k], :, pl.ds(c * length, length)],
            to_refs[k].at[pl.ds(c * length, length)],
            in_sems.at[k, c],
        )
        for k in range(users)
        for c in range(pieces)
    ]
    for copy in copies_in:
        copy.start()
    small[3].wait()
    rows = pool[...].astype(jnp.float32)
    unit[...] = (rows * lax.rsqrt(jnp.sum(rows * rows, axis=-1, keepdims=True) + 1e-06)).astype(jnp.bfloat16)
    units_out = [
        pltpu.make_async_copy(unit, unit_any.at[k], sems.at[4 + k]) for k in range(unit_any.shape[0])
    ]
    for copy in units_out:
        copy.start()
    small[1].wait()
    small[2].wait()
    row = lax.broadcasted_iota(jnp.int32, (number_rows, length), 0)
    for k in range(users):
        target = targets[pl.ds(order[k], 1), :]
        numbers = jnp.where(row == 0, lens[order[k]], jnp.where(row == 1, target // 256, target % 256))
        to_refs[k][width:, :] = numbers.astype(jnp.float32).astype(jnp.bfloat16)
    for copy in copies_in + units_out:
        copy.wait()


def pack(histories, lengths, targets, entries, item_pool, work, groups, blocks):
    users, length, width = histories.shape
    shape = (width + number_rows, length)
    hbm = pl.BlockSpec(memory_space=pltpu.HBM)
    return pl.pallas_call(
        functools.partial(pack_kernel, work, groups),
        in_specs=[hbm] * 5,
        out_specs=[pl.BlockSpec(memory_space=pltpu.VMEM)] * users + [hbm],
        scratch_shapes=[
            pltpu.SMEM(entries.shape, jnp.int32),
            pltpu.SMEM(lengths.shape, jnp.int32),
            pltpu.VMEM(targets.shape, jnp.int32),
            pltpu.VMEM(item_pool.shape, jnp.bfloat16),
            pltpu.VMEM(item_pool.shape, jnp.bfloat16),
            pltpu.SemaphoreType.DMA((4 + blocks,)),
            pltpu.SemaphoreType.DMA((users, width // length)),
        ],
        out_shape=[pltpu.VMEM(shape, jnp.bfloat16)] * users
        + [pltpu.HBM((blocks,) + item_pool.shape, jnp.bfloat16)],
        compiler_params=pltpu.CompilerParams(vmem_limit_bytes=16 * 1024 * 1024),
        name="pack",
    )(*[in_hbm(array) for array in (entries, lengths, histories, targets, item_pool)])


def users_kernel(tile, work, groups, x_refs, w_in, w_out, unit_ref, sums, loss_ref, bias, scratch):
    slots = loss_ref.shape[0] // groups
    group = lax.axis_index("dp")
    spots = [lax.rem(group + groups - shift, groups) * slots + slot for shift, slot in work]
    for at in range(0, len(work), 8):
        users_step(
            tile, x_refs[at : at + 8], spots[at : at + 8],
            w_in, w_out, unit_ref, sums, loss_ref, bias, *scratch,
        )


def first_kernel(work, groups, w_in_any, w_out_any, rel_any, unit_ref, *refs):
    count = len(work)
    x_refs, refs = refs[:count], refs[count:]
    loss_ref, sums, bias, refs = refs[0], refs[1], refs[2], refs[3:]
    w_in, w_out, rel, sems = refs[:4]
    heads, length = rel.shape
    moves = [(rel_any, rel), (w_in_any, w_in), (w_out_any, w_out)]
    copies = [pltpu.make_async_copy(*move, sems.at[k]) for k, move in enumerate(moves)]
    for copy in copies:
        copy.start()
    loss_ref[...] = jnp.zeros_like(loss_ref)
    sums[...] = jnp.zeros_like(sums)
    copies[0].wait()
    for h in range(heads):
        wide = jnp.broadcast_to(0.5 * rel[h : h + 1, :], (length, length))
        turned = pltpu.roll(wide, 0, 1, stride=1, stride_axis=0).T
        bias[h] = jnp.concatenate([turned, turned], axis=1)
    for copy in copies[1:]:
        copy.wait()
    users_kernel(first_tile, work, groups, x_refs, w_in, w_out, unit_ref, sums, loss_ref, bias, refs[4:])


def second_kernel(work, groups, w_in, w_out, bias, unit_ref, loss_in, sums_in, *refs):
    count = len(work)
    x_refs, refs = refs[:count], refs[count:]
    loss_ref, out_refs, sums, scratch = refs[0], refs[1:5], refs[5], refs[6:]
    loss_ref[...] = loss_in[...]
    sums[...] = sums_in[...]
    users_kernel(second_tile, work, groups, x_refs, w_in, w_out, unit_ref, sums, loss_ref, bias, scratch)
    mine = lax.axis_index("blk")
    for bits, ref in zip((0, 2, 1, 3), out_refs):
        ref[...] = sums[mine ^ bits].astype(ref.dtype)


def users_step(
    tile, x_refs, spots, w_in, w_out, unit_ref, sums, loss_ref, bias,
    exp_ref, residual, events, starts_ref, key, value, packed_tgt, packed_loss,
):
    heads, length, _ = bias.shape
    width = w_out.shape[0]
    hdim = width // heads
    blocks, items, _ = unit_ref.shape
    per_step = len(x_refs)

    digits = [ref[width:, :].astype(jnp.float32) for ref in x_refs]
    lens = [jnp.max(digit[:1, :]).astype(jnp.int32) for digit in digits]
    starts, end = [], 0
    for u in range(per_step):
        starts.append(pl.multiple_of(end, chunk) if u else 0)
        end = end + (lens[u] + chunk - 1) // chunk * chunk
    end = pl.multiple_of(end, chunk)
    tiles = (end + tile - 1) // tile

    place = lax.broadcasted_iota(jnp.int32, (1, length), 1)
    packed_tgt[...] = jnp.full_like(packed_tgt, -1)
    key[:length, :] = jnp.zeros((length, width), key.dtype)
    value[:length, :] = jnp.zeros((length, width), value.dtype)
    for u in range(per_step):
        starts_ref[pl.ds(starts[u], length), :] = jnp.full((length, length), starts[u], jnp.int32)
    for u in range(per_step):
        for c in range(0, width, length):
            events[pl.ds(starts[u], length), c : c + length] = x_refs[u][c : c + length, :]
        target = digits[u][1:2, :] * 256.0 + digits[u][2:3, :]
        wanted = jnp.where(place < lens[u], target.astype(jnp.int32), -1)
        line, turn = starts[u] // length + 1, lax.rem(starts[u], length)
        turned = pltpu.roll(wanted, turn, 1)
        packed_tgt[pl.ds(line, 1), :] = jnp.where(place >= turn, turned, packed_tgt[pl.ds(line, 1), :])
        packed_tgt[pl.ds(line + 1, 1), :] = jnp.where(
            place < turn, turned, packed_tgt[pl.ds(line + 1, 1), :]
        )
    events[pl.ds(end, tile), :] = jnp.zeros((tile, width), events.dtype)

    row = lax.broadcasted_iota(jnp.int32, (length, length), 0)
    col = lax.broadcasted_iota(jnp.int32, (length, length), 1)
    rate = logit_scale * math.log2(math.e)

    lines = tile // length

    def one_tile(t, _):
        first, strip = pl.multiple_of(t * tile, tile), t * lines
        item_id = lax.broadcasted_iota(jnp.int32, (items, tile), 0)
        x = events[pl.ds(first, tile), :].astype(jnp.float32)
        center, spread = center_and_spread(x)
        half_normed = (center * (0.5 * lax.rsqrt(spread + 1e-05))).astype(jnp.bfloat16)
        gate, values, query, keys = [
            half_silu(
                jnp.dot(
                    half_normed, w_in[:, part * width : (part + 1) * width],
                    preferred_element_type=jnp.float32,
                )
            ).astype(jnp.bfloat16)
            for part in range(4)
        ]
        key[pl.ds(first + length, tile), :] = keys
        value[pl.ds(first + length, tile), :] = values
        mixed = []
        for k in range(lines):
            base = pl.multiple_of(first + k * length, length)
            sources = pl.ds(base, 2 * length)
            start = starts_ref[pl.ds(base, length), :]
            ahead = packed_tgt[pl.ds(strip + k, 1), :] >= 0
            here = packed_tgt[pl.ds(strip + k + 1, 1), :] >= 0
            keep_ahead = (base - length + col >= start) & ahead
            keep_here = (col <= row) & (base + col >= start) & here
            keep = jnp.concatenate([keep_ahead, keep_here], axis=1)
            by_head = []
            for h in range(heads):
                cols = slice(h * hdim, (h + 1) * hdim)
                scores = lax.dot_general(
                    query[k * length : (k + 1) * length, cols], key[sources, cols], contract_last,
                    preferred_element_type=jnp.float32,
                )
                attn = half_silu(scores * (0.5 / math.sqrt(hdim)) + bias[h])
                attn = jnp.where(keep, attn, 0.0).astype(jnp.bfloat16)
                by_head.append(jnp.dot(attn, value[sources, cols], preferred_element_type=jnp.float32))
            mixed.append(jnp.concatenate(by_head, axis=1))
        center, spread = center_and_spread(jnp.concatenate(mixed, axis=0))
        normed = center * lax.rsqrt(spread + 1e-05)
        gated = (normed * gate.astype(jnp.float32)).astype(jnp.bfloat16)
        out = x + jnp.dot(gated, w_out[...], preferred_element_type=jnp.float32)
        out = out.astype(jnp.bfloat16).astype(jnp.float32)
        square = jnp.sum(out * out, axis=-1, keepdims=True)
        queries = (out * lax.rsqrt(square + 1e-06)).astype(jnp.bfloat16)

        target = jnp.concatenate(
            [packed_tgt[pl.ds(strip + k + 1, 1), :] for k in range(lines)], axis=1
        )
        total = jnp.zeros((1, tile), jnp.float32)
        target_dot = jnp.zeros((1, tile), jnp.float32)
        for j in range(blocks):
            dots = lax.dot_general(
                unit_ref[j], queries, contract_last, preferred_element_type=jnp.float32
            )
            exps = jnp.exp2(dots * rate - rate)
            exp_ref[j] = exps
            total += jnp.sum(exps, axis=0, keepdims=True)
            hit = item_id == target - j * items
            target_dot += jnp.sum(jnp.where(hit, dots, 0.0), axis=0, keepdims=True)
        loss = logit_scale + jnp.log(total) - logit_scale * target_dot
        for k in range(lines):
            packed_loss[pl.ds(strip + k, 1), :] = loss[:, k * length : (k + 1) * length]
        share = jnp.where(target >= 0, 1.0 / total, 0.0)
        for j in range(blocks):
            hit = item_id == target - j * items
            left = exp_ref[j] * share - jnp.where(hit, 1.0, 0.0)
            residual[j] = left.astype(jnp.bfloat16)
        for j in range(blocks):
            sums[j] += jnp.dot(residual[j], queries, preferred_element_type=jnp.float32)
        return 0

    lax.fori_loop(0, tiles, one_tile, 0)

    for u in range(per_step):
        line, turn = starts[u] // length, lax.rem(starts[u], length)
        back = lax.rem(length - turn, length)
        near = pltpu.roll(packed_loss[pl.ds(line, 1), :], back, 1)
        rest = pltpu.roll(packed_loss[pl.ds(line + 1, 1), :], back, 1)
        loss = jnp.where(place < length - turn, near, rest)
        loss_ref[pl.ds(spots[u], 1), :] = jnp.where(place < lens[u], loss, 0.0)


def step_scratch(tile, count, length, width, blocks, items):
    rows = -(-min(count, 8) * length // tile) * tile
    lines = -(-(rows // length + 2) // 8) * 8
    return [
        pltpu.VMEM((blocks, items, tile), jnp.float32),
        pltpu.VMEM((blocks, items, tile), jnp.bfloat16),
        pltpu.VMEM((rows + tile, width), jnp.bfloat16),
        pltpu.VMEM((rows + tile, length), jnp.int32),
        pltpu.VMEM((length + rows + tile, width), jnp.bfloat16),
        pltpu.VMEM((length + rows + tile, width), jnp.bfloat16),
        pltpu.VMEM((lines, length), jnp.int32),
        pltpu.VMEM((lines, length), jnp.float32),
    ]


whole = pl.BlockSpec(memory_space=pltpu.VMEM)
far_off = pl.BlockSpec(memory_space=pltpu.HBM)


def first_call(work, groups, users, packed, units, w_in, w_out, rel_bias):
    heads, length = rel_bias.shape
    width, (blocks, items, _) = w_out.shape[0], units.shape
    return pl.pallas_call(
        functools.partial(first_kernel, work, groups),
        in_specs=[far_off] * 3 + [whole] * (1 + len(work)),
        out_specs=[whole] * 3,
        scratch_shapes=[
            pltpu.VMEM(w_in.shape, jnp.bfloat16),
            pltpu.VMEM(w_out.shape, jnp.bfloat16),
            pltpu.VMEM(rel_bias.shape, jnp.float32),
            pltpu.SemaphoreType.DMA((3,)),
        ]
        + step_scratch(first_tile, len(work), length, width, blocks, items),
        out_shape=[
            pltpu.VMEM((users, length), jnp.float32),
            pltpu.VMEM((blocks, items, width), jnp.float32),
            pltpu.VMEM((heads, length, 2 * length), jnp.float32),
        ],
        compiler_params=pltpu.CompilerParams(vmem_limit_bytes=24 * 1024 * 1024),
        name="first_users",
    )(
        *[in_hbm(array) for array in (w_in, w_out, rel_bias)], in_vmem(units),
        *[in_vmem(array) for array in packed],
    )


def second_call(work, groups, packed, units, w_in, w_out, loss, sums, bias):
    blocks, items, width = sums.shape
    length = bias.shape[1]
    arrays = [w_in, w_out, bias, units, loss, sums, *packed]
    return pl.pallas_call(
        functools.partial(second_kernel, work, groups),
        in_specs=[whole] * len(arrays),
        out_specs=[whole] * 5,
        scratch_shapes=[pltpu.VMEM(sums.shape, jnp.float32)]
        + step_scratch(second_tile, len(work), length, width, blocks, items),
        out_shape=[pltpu.VMEM(loss.shape, jnp.float32)]
        + [pltpu.VMEM((items, width), jnp.float32)] * 2
        + [pltpu.VMEM((items, width), jnp.bfloat16)] * 2,
        compiler_params=pltpu.CompilerParams(vmem_limit_bytes=24 * 1024 * 1024),
        name="second_users",
    )(*[in_vmem(array) for array in arrays])


def shards(histories, lengths, targets, send_list, w_in, w_out, rel_bias, item_pool):
    user_count = histories.shape[0]
    groups, blocks = lax.axis_size("dp"), lax.axis_size("blk")
    slots = user_count // groups

    near = sorted({0, 1, groups - 1, 2 % groups}, key=lambda shift: (shift != 0, shift == 2))
    others = [shift for shift in range(groups) if shift not in near]
    order = near + sorted(others, key=lambda shift: abs(shift - groups / 2))
    work = [(shift, slot) for shift in order for slot in range(slots)]
    *packed, units = pack(
        histories, lengths, targets, send_list, item_pool, work, groups, blocks
    )
    half = user_count // 2
    packed = [
        users if shift == 0 else from_behind(users, "dp", shift) for users, (shift, _) in zip(packed, work)
    ]
    units = lax.all_to_all(units, "blk", split_axis=0, concat_axis=0, tiled=True)

    pool_float = item_pool.astype(jnp.float32)
    inverse_norm = lax.rsqrt(jnp.sum(pool_float * pool_float, axis=-1, keepdims=True) + 1e-06)
    unit_rows = pool_float * inverse_norm

    loss, sums, bias = first_call(
        work[:half], groups, user_count, packed[:half], units, w_in, w_out, rel_bias
    )
    row_loss, own, over, side, far = second_call(
        work[half:], groups, packed[half:], units, w_in, w_out, loss, sums, bias
    )
    over = over + swap(far, "blk", 1).astype(jnp.float32)
    own = own + swap(side, "blk", 1).astype(jnp.float32)
    item_sum = logit_scale * (own + swap(over.astype(jnp.bfloat16), "blk", 2).astype(jnp.float32))
    pool_grad = (
        item_sum - unit_rows * jnp.sum(unit_rows * item_sum, axis=-1, keepdims=True)
    ) * inverse_norm
    return (row_loss, pool_grad)


def solution(mesh):
    placed = (
        P(("dp", "blk"), None, None),
        P(("dp", "blk")),
        P(("dp", "blk"), None),
        P(("dp", "blk")),
        P(),
        P(),
        P(),
        P(("dp", "blk"), None),
    )
    return jax.shard_map(
        shards,
        mesh=mesh,
        in_specs=placed,
        out_specs=(P(("dp", "blk"), None), P(("dp", "blk"), None)),
        check_vma=False,
    )
```

```python
import functools
import math

import jax
import jax.numpy as jnp
from jax import lax
from jax.experimental import pallas as pl
from jax.experimental.pallas import tpu as pltpu
from jax.sharding import PartitionSpec as P

logit_scale = 20.0
contract_last = (((1,), (1,)), ((), ()))
first_tile, second_tile = 384, 256
chunk = 16
number_rows = 8


def swap(array, axis, bit):
    devices = lax.axis_size(axis)
    return lax.ppermute(array, axis, [(i, i ^ bit) for i in range(devices)])


def from_behind(array, axis, by):
    devices = lax.axis_size(axis)
    return lax.ppermute(array, axis, [(i, (i + by) % devices) for i in range(devices)])


def in_vmem(array):
    return pltpu.with_memory_space_constraint(array, pltpu.VMEM)


def in_hbm(array):
    return pltpu.with_memory_space_constraint(array, pltpu.HBM)


def half_silu(half):
    return half + half * jnp.tanh(half)


def center_and_spread(values):
    center = values - jnp.mean(values, axis=-1, keepdims=True)
    return center, jnp.mean(center * center, axis=-1, keepdims=True)


def pack_kernel(
    work, groups, list_any, len_any, from_any, tgt_any, pool_any, *refs,
):
    users, length, width = from_any.shape
    to_refs, unit_any = refs[:users], refs[users]
    entries, lens, targets, pool, unit, sems, in_sems = refs[users + 1 :]
    pieces = width // length
    small = [
        pltpu.make_async_copy(source, target, sems.at[k])
        for k, (source, target) in enumerate(
            ((list_any, entries), (len_any, lens), (tgt_any, targets), (pool_any, pool))
        )
    ]
    for copy in small:
        copy.start()
    small[0].wait()
    slots = users // groups
    group = lax.axis_index("dp")
    order = [entries[lax.rem(group + shift, groups) * slots + slot] for shift, slot in work]
    copies_in = [
        pltpu.make_async_copy(
            from_any.at[order[k], :, pl.ds(c * length, length)],
            to_refs[k].at[pl.ds(c * length, length)],
            in_sems.at[k, c],
        )
        for k in range(users)
        for c in range(pieces)
    ]
    for copy in copies_in:
        copy.start()
    small[3].wait()
    rows = pool[...].astype(jnp.float32)
    unit[...] = (rows * lax.rsqrt(jnp.sum(rows * rows, axis=-1, keepdims=True) + 1e-06)).astype(jnp.bfloat16)
    units_out = [
        pltpu.make_async_copy(unit, unit_any.at[k], sems.at[4 + k]) for k in range(unit_any.shape[0])
    ]
    for copy in units_out:
        copy.start()
    small[1].wait()
    small[2].wait()
    row = lax.broadcasted_iota(jnp.int32, (number_rows, length), 0)
    for k in range(users):
        target = targets[pl.ds(order[k], 1), :]
        numbers = jnp.where(row == 0, lens[order[k]], jnp.where(row == 1, target // 256, target % 256))
        to_refs[k][width:, :] = numbers.astype(jnp.float32).astype(jnp.bfloat16)
    for copy in copies_in + units_out:
        copy.wait()


def pack(histories, lengths, targets, entries, item_pool, work, groups, blocks):
    users, length, width = histories.shape
    shape = (width + number_rows, length)
    hbm = pl.BlockSpec(memory_space=pltpu.HBM)
    return pl.pallas_call(
        functools.partial(pack_kernel, work, groups),
        in_specs=[hbm] * 5,
        out_specs=[pl.BlockSpec(memory_space=pltpu.VMEM)] * users + [hbm],
        scratch_shapes=[
            pltpu.SMEM(entries.shape, jnp.int32),
            pltpu.SMEM(lengths.shape, jnp.int32),
            pltpu.VMEM(targets.shape, jnp.int32),
            pltpu.VMEM(item_pool.shape, jnp.bfloat16),
            pltpu.VMEM(item_pool.shape, jnp.bfloat16),
            pltpu.SemaphoreType.DMA((4 + blocks,)),
            pltpu.SemaphoreType.DMA((users, width // length)),
        ],
        out_shape=[pltpu.VMEM(shape, jnp.bfloat16)] * users
        + [pltpu.HBM((blocks,) + item_pool.shape, jnp.bfloat16)],
        compiler_params=pltpu.CompilerParams(vmem_limit_bytes=16 * 1024 * 1024),
        name="pack",
    )(*[in_hbm(array) for array in (entries, lengths, histories, targets, item_pool)])


def users_kernel(tile, work, groups, x_refs, w_in, w_out, unit_ref, sums, loss_ref, bias, scratch):
    slots = loss_ref.shape[0] // groups
    group = lax.axis_index("dp")
    spots = [lax.rem(group + groups - shift, groups) * slots + slot for shift, slot in work]
    for at in range(0, len(work), 8):
        users_step(
            tile, x_refs[at : at + 8], spots[at : at + 8],
            w_in, w_out, unit_ref, sums, loss_ref, bias, *scratch,
        )


def first_kernel(work, groups, w_in_any, w_out_any, rel_any, unit_ref, *refs):
    count = len(work)
    x_refs, refs = refs[:count], refs[count:]
    loss_ref, sums, bias, refs = refs[0], refs[1], refs[2], refs[3:]
    w_in, w_out, rel, sems = refs[:4]
    heads, length = rel.shape
    moves = [(rel_any, rel), (w_in_any, w_in), (w_out_any, w_out)]
    copies = [pltpu.make_async_copy(*move, sems.at[k]) for k, move in enumerate(moves)]
    for copy in copies:
        copy.start()
    loss_ref[...] = jnp.zeros_like(loss_ref)
    sums[...] = jnp.zeros_like(sums)
    copies[0].wait()
    for h in range(heads):
        wide = jnp.broadcast_to(0.5 * rel[h : h + 1, :], (length, length))
        turned = pltpu.roll(wide, 0, 1, stride=1, stride_axis=0).T
        bias[h] = jnp.concatenate([turned, turned], axis=1)
    for copy in copies[1:]:
        copy.wait()
    users_kernel(first_tile, work, groups, x_refs, w_in, w_out, unit_ref, sums, loss_ref, bias, refs[4:])


def second_kernel(work, groups, w_in, w_out, bias, unit_ref, loss_in, sums_in, *refs):
    count = len(work)
    x_refs, refs = refs[:count], refs[count:]
    loss_ref, out_refs, sums, scratch = refs[0], refs[1:5], refs[5], refs[6:]
    loss_ref[...] = loss_in[...]
    sums[...] = sums_in[...]
    users_kernel(second_tile, work, groups, x_refs, w_in, w_out, unit_ref, sums, loss_ref, bias, scratch)
    mine = lax.axis_index("blk")
    for bits, ref in zip((0, 2, 1, 3), out_refs):
        ref[...] = sums[mine ^ bits].astype(ref.dtype)


def users_step(
    tile, x_refs, spots, w_in, w_out, unit_ref, sums, loss_ref, bias,
    exp_ref, residual, events, starts_ref, key, value, packed_tgt, packed_loss,
):
    heads, length, _ = bias.shape
    width = w_out.shape[0]
    hdim = width // heads
    blocks, items, _ = unit_ref.shape
    per_step = len(x_refs)

    digits = [ref[width:, :].astype(jnp.float32) for ref in x_refs]
    lens = [jnp.max(digit[:1, :]).astype(jnp.int32) for digit in digits]
    starts, end = [], 0
    for u in range(per_step):
        starts.append(pl.multiple_of(end, chunk) if u else 0)
        end = end + (lens[u] + chunk - 1) // chunk * chunk
    end = pl.multiple_of(end, chunk)
    tiles = (end + tile - 1) // tile

    place = lax.broadcasted_iota(jnp.int32, (1, length), 1)
    packed_tgt[...] = jnp.full_like(packed_tgt, -1)
    key[:length, :] = jnp.zeros((length, width), key.dtype)
    value[:length, :] = jnp.zeros((length, width), value.dtype)
    for u in range(per_step):
        starts_ref[pl.ds(starts[u], length), :] = jnp.full((length, length), starts[u], jnp.int32)
    for u in range(per_step):
        for c in range(0, width, length):
            events[pl.ds(starts[u], length), c : c + length] = x_refs[u][c : c + length, :]
        target = digits[u][1:2, :] * 256.0 + digits[u][2:3, :]
        wanted = jnp.where(place < lens[u], target.astype(jnp.int32), -1)
        line, turn = starts[u] // length + 1, lax.rem(starts[u], length)
        turned = pltpu.roll(wanted, turn, 1)
        packed_tgt[pl.ds(line, 1), :] = jnp.where(place >= turn, turned, packed_tgt[pl.ds(line, 1), :])
        packed_tgt[pl.ds(line + 1, 1), :] = jnp.where(
            place < turn, turned, packed_tgt[pl.ds(line + 1, 1), :]
        )
    events[pl.ds(end, tile), :] = jnp.zeros((tile, width), events.dtype)

    row = lax.broadcasted_iota(jnp.int32, (length, length), 0)
    col = lax.broadcasted_iota(jnp.int32, (length, length), 1)
    rate = logit_scale * math.log2(math.e)

    lines = tile // length

    def one_tile(t, _):
        first, strip = pl.multiple_of(t * tile, tile), t * lines
        item_id = lax.broadcasted_iota(jnp.int32, (items, tile), 0)
        x = events[pl.ds(first, tile), :].astype(jnp.float32)
        center, spread = center_and_spread(x)
        half_normed = (center * (0.5 * lax.rsqrt(spread + 1e-05))).astype(jnp.bfloat16)
        gate, values, query, keys = [
            half_silu(
                jnp.dot(
                    half_normed, w_in[:, part * width : (part + 1) * width],
                    preferred_element_type=jnp.float32,
                )
            ).astype(jnp.bfloat16)
            for part in range(4)
        ]
        key[pl.ds(first + length, tile), :] = keys
        value[pl.ds(first + length, tile), :] = values
        mixed = []
        for k in range(lines):
            base = pl.multiple_of(first + k * length, length)
            sources = pl.ds(base, 2 * length)
            start = starts_ref[pl.ds(base, length), :]
            ahead = packed_tgt[pl.ds(strip + k, 1), :] >= 0
            here = packed_tgt[pl.ds(strip + k + 1, 1), :] >= 0
            keep_ahead = (base - length + col >= start) & ahead
            keep_here = (col <= row) & (base + col >= start) & here
            keep = jnp.concatenate([keep_ahead, keep_here], axis=1)
            by_head = []
            for h in range(heads):
                cols = slice(h * hdim, (h + 1) * hdim)
                scores = lax.dot_general(
                    query[k * length : (k + 1) * length, cols], key[sources, cols], contract_last,
                    preferred_element_type=jnp.float32,
                )
                attn = half_silu(scores * (0.5 / math.sqrt(hdim)) + bias[h])
                attn = jnp.where(keep, attn, 0.0).astype(jnp.bfloat16)
                by_head.append(jnp.dot(attn, value[sources, cols], preferred_element_type=jnp.float32))
            mixed.append(jnp.concatenate(by_head, axis=1))
        center, spread = center_and_spread(jnp.concatenate(mixed, axis=0))
        normed = center * lax.rsqrt(spread + 1e-05)
        gated = (normed * gate.astype(jnp.float32)).astype(jnp.bfloat16)
        out = x + jnp.dot(gated, w_out[...], preferred_element_type=jnp.float32)
        out = out.astype(jnp.bfloat16).astype(jnp.float32)
        square = jnp.sum(out * out, axis=-1, keepdims=True)
        queries = (out * lax.rsqrt(square + 1e-06)).astype(jnp.bfloat16)

        target = jnp.concatenate(
            [packed_tgt[pl.ds(strip + k + 1, 1), :] for k in range(lines)], axis=1
        )
        total = jnp.zeros((1, tile), jnp.float32)
        target_dot = jnp.zeros((1, tile), jnp.float32)
        for j in range(blocks):
            dots = lax.dot_general(
                unit_ref[j], queries, contract_last, preferred_element_type=jnp.float32
            )
            exps = jnp.exp2(dots * rate - rate)
            exp_ref[j] = exps
            total += jnp.sum(exps, axis=0, keepdims=True)
            hit = item_id == target - j * items
            target_dot += jnp.sum(jnp.where(hit, dots, 0.0), axis=0, keepdims=True)
        loss = logit_scale + jnp.log(total) - logit_scale * target_dot
        for k in range(lines):
            packed_loss[pl.ds(strip + k, 1), :] = loss[:, k * length : (k + 1) * length]
        share = jnp.where(target >= 0, 1.0 / total, 0.0)
        for j in range(blocks):
            hit = item_id == target - j * items
            left = exp_ref[j] * share - jnp.where(hit, 1.0, 0.0)
            residual[j] = left.astype(jnp.bfloat16)
        for j in range(blocks):
            sums[j] += jnp.dot(residual[j], queries, preferred_element_type=jnp.float32)
        return 0

    lax.fori_loop(0, tiles, one_tile, 0)

    for u in range(per_step):
        line, turn = starts[u] // length, lax.rem(starts[u], length)
        back = lax.rem(length - turn, length)
        near = pltpu.roll(packed_loss[pl.ds(line, 1), :], back, 1)
        rest = pltpu.roll(packed_loss[pl.ds(line + 1, 1), :], back, 1)
        loss = jnp.where(place < length - turn, near, rest)
        loss_ref[pl.ds(spots[u], 1), :] = jnp.where(place < lens[u], loss, 0.0)


def step_scratch(tile, count, length, width, blocks, items):
    rows = -(-min(count, 8) * length // tile) * tile
    lines = -(-(rows // length + 2) // 8) * 8
    return [
        pltpu.VMEM((blocks, items, tile), jnp.float32),
        pltpu.VMEM((blocks, items, tile), jnp.bfloat16),
        pltpu.VMEM((rows + tile, width), jnp.bfloat16),
        pltpu.VMEM((rows + tile, length), jnp.int32),
        pltpu.VMEM((length + rows + tile, width), jnp.bfloat16),
        pltpu.VMEM((length + rows + tile, width), jnp.bfloat16),
        pltpu.VMEM((lines, length), jnp.int32),
        pltpu.VMEM((lines, length), jnp.float32),
    ]


whole = pl.BlockSpec(memory_space=pltpu.VMEM)
far_off = pl.BlockSpec(memory_space=pltpu.HBM)


def first_call(work, groups, users, packed, units, w_in, w_out, rel_bias):
    heads, length = rel_bias.shape
    width, (blocks, items, _) = w_out.shape[0], units.shape
    return pl.pallas_call(
        functools.partial(first_kernel, work, groups),
        in_specs=[far_off] * 3 + [whole] * (1 + len(work)),
        out_specs=[whole] * 3,
        scratch_shapes=[
            pltpu.VMEM(w_in.shape, jnp.bfloat16),
            pltpu.VMEM(w_out.shape, jnp.bfloat16),
            pltpu.VMEM(rel_bias.shape, jnp.float32),
            pltpu.SemaphoreType.DMA((3,)),
        ]
        + step_scratch(first_tile, len(work), length, width, blocks, items),
        out_shape=[
            pltpu.VMEM((users, length), jnp.float32),
            pltpu.VMEM((blocks, items, width), jnp.float32),
            pltpu.VMEM((heads, length, 2 * length), jnp.float32),
        ],
        compiler_params=pltpu.CompilerParams(vmem_limit_bytes=24 * 1024 * 1024),
        name="first_users",
    )(
        *[in_hbm(array) for array in (w_in, w_out, rel_bias)], in_vmem(units),
        *[in_vmem(array) for array in packed],
    )


def second_call(work, groups, packed, units, w_in, w_out, loss, sums, bias):
    blocks, items, width = sums.shape
    length = bias.shape[1]
    arrays = [w_in, w_out, bias, units, loss, sums, *packed]
    return pl.pallas_call(
        functools.partial(second_kernel, work, groups),
        in_specs=[whole] * len(arrays),
        out_specs=[whole] * 5,
        scratch_shapes=[pltpu.VMEM(sums.shape, jnp.float32)]
        + step_scratch(second_tile, len(work), length, width, blocks, items),
        out_shape=[pltpu.VMEM(loss.shape, jnp.float32)]
        + [pltpu.VMEM((items, width), jnp.float32)] * 2
        + [pltpu.VMEM((items, width), jnp.bfloat16)] * 2,
        compiler_params=pltpu.CompilerParams(vmem_limit_bytes=24 * 1024 * 1024),
        name="second_users",
    )(*[in_vmem(array) for array in arrays])


def finish_kernel(own, side, over, pool, out_any, out, sems):
    quarter = own.shape[0] // 4
    copies = []
    for k in range(4):
        rows = slice(k * quarter, (k + 1) * quarter)
        items = pool[rows].astype(jnp.float32)
        inverse = lax.rsqrt(jnp.sum(items * items, axis=-1, keepdims=True) + 1e-06)
        unit = items * inverse
        total = logit_scale * (own[rows] + side[rows].astype(jnp.float32) + over[rows].astype(jnp.float32))
        out[rows] = (total - unit * jnp.sum(unit * total, axis=-1, keepdims=True)) * inverse
        part = pl.ds(k * quarter, quarter)
        copies.append(pltpu.make_async_copy(out.at[part], out_any.at[part], sems.at[k]))
        copies[k].start()
    for copy in copies:
        copy.wait()


def finish(own, side, over, pool):
    return pl.pallas_call(
        finish_kernel,
        in_specs=[whole] * 4,
        out_specs=far_off,
        scratch_shapes=[pltpu.VMEM(own.shape, jnp.float32), pltpu.SemaphoreType.DMA((4,))],
        out_shape=jax.ShapeDtypeStruct(own.shape, jnp.float32),
        name="finish",
    )(*[in_vmem(array) for array in (own, side, over, pool)])


def shards(histories, lengths, targets, send_list, w_in, w_out, rel_bias, item_pool):
    user_count = histories.shape[0]
    groups, blocks = lax.axis_size("dp"), lax.axis_size("blk")
    slots = user_count // groups

    near = sorted({0, 1, groups - 1, 2 % groups}, key=lambda shift: (shift != 0, shift == 2))
    others = [shift for shift in range(groups) if shift not in near]
    order = near + sorted(others, key=lambda shift: abs(shift - groups / 2))
    work = [(shift, slot) for shift in order for slot in range(slots)]
    *packed, units = pack(
        histories, lengths, targets, send_list, item_pool, work, groups, blocks
    )
    half = user_count // 2
    packed = [
        users if shift == 0 else from_behind(users, "dp", shift) for users, (shift, _) in zip(packed, work)
    ]
    units = lax.all_to_all(units, "blk", split_axis=0, concat_axis=0, tiled=True)

    loss, sums, bias = first_call(
        work[:half], groups, user_count, packed[:half], units, w_in, w_out, rel_bias
    )
    row_loss, own, over, side, far = second_call(
        work[half:], groups, packed[half:], units, w_in, w_out, loss, sums, bias
    )
    over = over + swap(far, "blk", 1).astype(jnp.float32)
    side = swap(side, "blk", 1)
    pool_grad = finish(own, side, swap(over.astype(jnp.bfloat16), "blk", 2), item_pool)
    return (row_loss, pool_grad)


def solution(mesh):
    placed = (
        P(("dp", "blk"), None, None),
        P(("dp", "blk")),
        P(("dp", "blk"), None),
        P(("dp", "blk")),
        P(),
        P(),
        P(),
        P(("dp", "blk"), None),
    )
    return jax.shard_map(
        shards,
        mesh=mesh,
        in_specs=placed,
        out_specs=(P(("dp", "blk"), None), P(("dp", "blk"), None)),
        check_vma=False,
    )
```
